32 devices in a mesh: ctx: 16 (over z, x, core), dp: 2 (over y).
Axes of the slice: x: 2, y: 2, z: 4, core: 2. Of those that a mesh axis runs over, the one named last changes fastest.
Arguments:
- hidden_in: bfloat16 [8192, 8192], P(('dp', 'ctx')), parts along dimension 0, may hold values from -32 to 32
- segment_ids: int32 [8192], P('dp'), parts along dimension 0, may hold values from 1023 to 4095, as said below
- w_query: bfloat16 [8192, 512], P('ctx'), may hold values from -0.0625 to 0.0625
- w_key: bfloat16 [8192, 128], P('ctx'), may hold values from -0.0625 to 0.0625
- w_value: bfloat16 [8192, 128], P('ctx'), may hold values from -0.0625 to 0.0625
- w_out: bfloat16 [512, 8192], P(None, 'ctx'), may hold values from -0.25 to 0.25
Outputs:
- attended: bfloat16 [8192, 8192], P(('dp', 'ctx')), parts along dimension 0
The draws below stay inside these ranges and needn't reach their ends.
There are 2 independent parts, one for each index of `dp`. The reference program is written for one: setup_inputs(seed, part) draws one part's arguments, and reference() takes and returns one part's arrays. A program takes and returns all parts, laid end to end along the dimension named above; an argument that names none is the same for every part. Nothing has to cross between parts.
Inputs may be any that keep to these rules, and one draw needn't show every extreme that they name: `segment_ids`: A token's id is the position in sequence order of the last token of its document, so ids never fall along the sequence and tokens share an id exactly when they share a document; every document holds 1 to 1024 tokens, and the first one exactly 1024. Stored in the same block order as hidden_in.
All inputs are finite; a program needn't handle non-finite values.
Results may differ from the reference program's by a relative error of at most 0.034.
Values may be sent and summed in bfloat16 or wider, within the bound.
No kernel may reach another device: no remote copies, remote signals or barrier semaphores. Data moves between devices by JAX's collectives and lax.ppermute only.
A program may use at most 128 MiB of HBM per device.

```python
import math
import jax
import jax.numpy as jnp
from jax import lax

D = 8192
HD = 128
HQ = 4
REACH = 8
BLOCK = 128
TOKENS = 4096
N_CTX = 16


def draw_hidden_in(key, part):
    key = jax.random.fold_in(key, 5)
    first_key = jax.random.fold_in(key, 0)
    drawn = jnp.clip(jax.random.normal(first_key, (TOKENS, D), jnp.float32), -6.0, 6.0)
    return drawn.astype(jnp.bfloat16)


def draw_segment_ids(key, part):
    key = jax.random.fold_in(key, 9)
    first_key = jax.random.fold_in(key, 0)
    longest = REACH * BLOCK
    lengths = jax.random.randint(first_key, (TOKENS,), 1, longest + 1, dtype=jnp.int32)
    lengths = jnp.where(jnp.arange(TOKENS, dtype=jnp.int32) == 0, longest, lengths)
    bounds = jnp.cumsum(lengths).astype(jnp.int32)
    doc_index = jnp.searchsorted(bounds, jnp.arange(TOKENS, dtype=jnp.int32), side='right').astype(jnp.int32)
    last_pos = jnp.minimum(bounds[doc_index] - 1, TOKENS - 1).astype(jnp.int32)
    stored = jnp.arange(2 * N_CTX, dtype=jnp.int32)
    sequence_of = jnp.where(stored % 2 == 0, stored // 2, 2 * N_CTX - 1 - stored // 2)
    return last_pos.reshape(2 * N_CTX, BLOCK)[sequence_of].reshape(TOKENS).astype(jnp.int32)


def shard_levels(rng, extent, shards, least, high):
    loudness = 1.0
    for dim, blocks in shards:
        heights = jax.random.uniform(jax.random.fold_in(jax.random.fold_in(rng, 6), dim), (blocks,), jnp.float32, least / len(shards), high / len(shards))
        loudness = loudness * jnp.repeat(jnp.exp(heights), extent[dim] // blocks).reshape((-1,) + (1,) * (len(extent) - 1 - dim))
    return loudness


def gaussian(own_key, dims, scale, bound, pieces=(), kind=jnp.bfloat16):
    level = shard_levels(own_key, dims, pieces, -0.22, 0.18) if pieces else 1.0
    values = jax.random.normal(own_key, dims, jnp.float32) * scale * level
    return jnp.minimum(jnp.maximum(values, -bound), bound).astype(kind)


def setup_inputs(seed: int = 0, part: int = 0) -> dict:
    arg_keys = jax.random.split(jax.random.key(seed), 7)
    own_keys = jax.random.split(jax.random.fold_in(arg_keys[6], part), 7)
    return {
        "hidden_in": draw_hidden_in(jax.random.fold_in(jax.random.fold_in(arg_keys[6], part), 71), part),
        "segment_ids": draw_segment_ids(jax.random.fold_in(jax.random.fold_in(arg_keys[6], part), 71), part),
        "w_query": gaussian(arg_keys[2], (D, HQ * HD), D ** -0.5, 0.0625, ((0, 16),)),
        "w_key": gaussian(arg_keys[3], (D, HD), D ** -0.5, 0.0625, ((0, 16),)),
        "w_value": gaussian(arg_keys[4], (D, HD), D ** -0.5, 0.0625, ((0, 16),)),
        "w_out": gaussian(arg_keys[5], (HQ * HD, D), (HQ * HD) ** -0.5, 0.25, ((1, 16),)),
    }


ROPE_BASE = 500000.0

def rotate(rows_in, positions):
    half_dim = rows_in.shape[-1] // 2
    frequency = ROPE_BASE ** (-(jnp.arange(half_dim, dtype=jnp.float32) * 2.0) / rows_in.shape[-1])
    angles = positions.astype(jnp.float32)[:, None] * frequency[None, :]
    cosine = jnp.cos(angles)[:, None, :]
    sine_part = jnp.sin(angles)[:, None, :]
    front_part = rows_in[..., :half_dim]
    back_part = rows_in[..., half_dim:]
    return jnp.concatenate([front_part * cosine - back_part * sine_part, back_part * cosine + front_part * sine_part], axis=-1)

def block_order():
    seq_blocks = jnp.arange(2 * N_CTX, dtype=jnp.int32)
    storage_of = jnp.where(seq_blocks < N_CTX, 2 * seq_blocks, 2 * (2 * N_CTX - 1 - seq_blocks) + 1)
    stored = jnp.arange(2 * N_CTX, dtype=jnp.int32)
    sequence_of = jnp.where(stored % 2 == 0, stored // 2, 2 * N_CTX - 1 - stored // 2)
    return (storage_of, sequence_of)

def reference(hidden_in, segment_ids, w_query, w_key, w_value, w_out):
    storage_of, sequence_of = block_order()
    tokens_seq = hidden_in.reshape(2 * N_CTX, BLOCK, D)[storage_of].reshape(TOKENS, D)
    seg_seq = segment_ids.reshape(2 * N_CTX, BLOCK)[storage_of].reshape(TOKENS)
    positions = jnp.arange(TOKENS, dtype=jnp.int32)
    query_sum = jnp.dot(tokens_seq, w_query, preferred_element_type=jnp.float32)
    queries = rotate(query_sum.reshape(TOKENS, HQ, HD), positions).astype(jnp.bfloat16)
    key_sum = jnp.dot(tokens_seq, w_key, preferred_element_type=jnp.float32)
    key_rows = rotate(key_sum.reshape(TOKENS, 1, HD), positions).reshape(TOKENS, HD).astype(jnp.bfloat16)
    value_rows = jnp.dot(tokens_seq, w_value, preferred_element_type=jnp.float32).astype(jnp.bfloat16)
    margin = REACH * BLOCK
    key_padded = jnp.concatenate([jnp.zeros((margin, HD), jnp.bfloat16), key_rows], axis=0)
    value_padded = jnp.concatenate([jnp.zeros((margin, HD), jnp.bfloat16), value_rows], axis=0)
    seg_padded = jnp.concatenate([jnp.full((margin,), -1, jnp.int32), seg_seq], axis=0)
    span_len = (REACH + 1) * BLOCK

    def one_block(block_id):
        begin = (block_id * BLOCK).astype(jnp.int32)
        query_part = lax.dynamic_slice_in_dim(queries, begin, BLOCK, 0).astype(jnp.float32)
        key_part = lax.dynamic_slice_in_dim(key_padded, begin, span_len, 0).astype(jnp.float32)
        value_part = lax.dynamic_slice_in_dim(value_padded, begin, span_len, 0).astype(jnp.float32)
        key_seg = lax.dynamic_slice_in_dim(seg_padded, begin, span_len, 0)
        query_seg = lax.dynamic_slice_in_dim(seg_seq, begin, BLOCK, 0)
        query_pos = begin + jnp.arange(BLOCK, dtype=jnp.int32)
        key_pos = begin - margin + jnp.arange(span_len, dtype=jnp.int32)
        scores = jnp.einsum('qhd,kd->hqk', query_part, key_part) / math.sqrt(HD)
        allowed = (query_seg[:, None] == key_seg[None, :]) & (key_pos[None, :] <= query_pos[:, None])
        scores = jnp.where(allowed[None], scores, -1e+30)
        row_peak = lax.optimization_barrier(jnp.max(scores, axis=-1, keepdims=True))
        exp_terms = jnp.exp(scores - row_peak)
        weights = (exp_terms / lax.optimization_barrier(jnp.sum(exp_terms, axis=-1, keepdims=True))).astype(jnp.bfloat16)
        mixed_part = jnp.einsum('hqk,kd->qhd', weights.astype(jnp.float32), value_part)
        return mixed_part.reshape(BLOCK, HQ * HD).astype(jnp.bfloat16)
    mixed_rows = lax.map(one_block, jnp.arange(2 * N_CTX, dtype=jnp.int32)).reshape(TOKENS, HQ * HD)
    attended_seq = jnp.dot(mixed_rows, w_out, preferred_element_type=jnp.float32).astype(jnp.bfloat16)
    return attended_seq.reshape(2 * N_CTX, BLOCK, D)[sequence_of].reshape(TOKENS, D)
```

```python
import functools
import math

import jax
import jax.numpy as jnp
from jax import lax
from jax.experimental import pallas as pl
from jax.experimental.pallas import tpu as pltpu
from jax.sharding import PartitionSpec as P

REACH = 8
ROPE_BASE = 500000.0
RING_LIMIT = 16
VMEM_LIMIT = 16 * 1024 * 1024


def chip_at(place, chips):
    place = place % chips
    return jnp.where(place < chips // 2, 2 * place, 2 * (chips - 1 - place) + 1)


def static_chip_at(place, chips):
    place %= chips
    return 2 * place if place < chips // 2 else 2 * (chips - 1 - place) + 1


def ring_pairs(chips):
    pairs = []
    for place in range(chips):
        here = static_chip_at(place, chips)
        pairs.append((2 * here, 2 * static_chip_at(place + 1, chips)))
        pairs.append((2 * here + 1, 2 * static_chip_at(place - 1, chips) + 1))
    return pairs


def core_swap(value, count):
    return lax.ppermute(value, "ctx", [(i, i ^ 1) for i in range(count)])


def plane_swap(value):
    return lax.ppermute(value, "dp", [(0, 1), (1, 0)])


def pair_device(pair, count):
    return 2 * pair if pair < count // 2 else 2 * (count - 1 - pair) + 1


def after(value, *others):
    return lax.optimization_barrier((value, *others))[0]


def shard_owners(me, count):
    chips = count // 2
    half = chips // 2
    core, chip = me % 2, me // 2
    place = jnp.where(chip % 2 == 0, chip // 2, chips - 1 - chip // 2)
    way = jnp.where(core == 0, -1, 1)
    owners = [me]
    for step in range(1, half + 1):
        source = chip_at(place + way * step + chips, chips)
        owners.append(2 * source + core)
        if step < half:
            owners.append(2 * source + 1 - core)
    return owners


def params(**settings):
    return pltpu.CompilerParams(vmem_limit_bytes=VMEM_LIMIT, **settings)


def in_vmem(*arrays):
    return [pltpu.with_memory_space_constraint(array, pltpu.VMEM) for array in arrays]


def in_hbm(*arrays):
    return [pltpu.with_memory_space_constraint(array, pltpu.HBM) for array in arrays]


IN_VMEM = pl.BlockSpec(memory_space=pltpu.VMEM)
IN_HBM = pl.BlockSpec(memory_space=pl.ANY)
IN_SMEM = pl.BlockSpec(memory_space=pltpu.SMEM)


def rotate_kernel(head_dim, kept_ref, came_ref, cos_ref, sin_ref, joined_ref, query_ref):
    cosine, sine = cos_ref[...], sin_ref[...]

    def rotated(column):
        span = pl.ds(column, head_dim)
        part = kept_ref[:, span] + came_ref[:, span]
        return (part * cosine + pltpu.roll(part, head_dim // 2, 1) * sine).astype(jnp.bfloat16)

    joined_ref[:, :head_dim] = rotated(0)
    values = pl.ds(head_dim, head_dim)
    joined_ref[:, values] = (kept_ref[:, values] + came_ref[:, values]).astype(jnp.bfloat16)
    for column in range(0, query_ref.shape[1], head_dim):
        query_ref[:, pl.ds(column, head_dim)] = rotated(2 * head_dim + column)


def rotate_sums(kept, came, positions, head_dim):
    rows, columns = kept.shape
    frequency = ROPE_BASE ** (
        -(jnp.arange(head_dim // 2, dtype=jnp.float32) * 2.0) / head_dim
    )
    angles = positions.astype(jnp.float32)[:, None] * frequency[None, :]
    cosine, sine = jnp.cos(angles), jnp.sin(angles)
    cosine = jnp.concatenate([cosine, cosine], axis=1)
    sine = jnp.concatenate([-sine, sine], axis=1)
    return pl.pallas_call(
        functools.partial(rotate_kernel, head_dim),
        out_shape=(
            pltpu.VMEM((rows, 2 * head_dim), jnp.bfloat16),
            pltpu.VMEM((rows, columns - 2 * head_dim), jnp.bfloat16),
        ),
        in_specs=[IN_VMEM] * 4,
        out_specs=(IN_VMEM, IN_VMEM),
        compiler_params=params(),
        name="rotate_sums",
    )(*in_vmem(kept, came, cosine, sine))


def attend_kernel(
    head_dim, reach, query_ref, key_seg_ref, query_seg_ref, *refs
):
    windows, mixed_ref = refs[:-1], refs[-1]
    rows = query_ref.shape[0]
    query_seg = query_seg_ref[...]
    base = lax.broadcasted_iota(jnp.int32, (rows, rows), 0)
    offset = lax.broadcasted_iota(jnp.int32, (rows, rows), 1)
    allowed = []
    for piece in range(reach + 1):
        same = query_seg == key_seg_ref[:, pl.ds(piece * rows, rows)]
        if piece == reach:
            same = same & (offset <= base)
        allowed.append(same)
    for column in range(0, query_ref.shape[1], head_dim):
        span = pl.ds(column, head_dim)
        query = query_ref[:, span]
        scores = []
        for piece in range(reach + 1):
            score = lax.dot_general(
                query,
                windows[piece][:, :head_dim],
                (((1,), (1,)), ((), ())),
                preferred_element_type=jnp.float32,
            ) / math.sqrt(head_dim)
            scores.append(jnp.where(allowed[piece], score, -1e30))
        peak = scores[0]
        for score in scores[1:]:
            peak = jnp.maximum(peak, score)
        peak = jnp.max(peak, axis=1, keepdims=True)
        terms = [jnp.exp(score - peak) for score in scores]
        total = terms[0]
        for term in terms[1:]:
            total = total + term
        inverse = 1.0 / jnp.sum(total, axis=1, keepdims=True)
        mixed = jnp.zeros((rows, head_dim), jnp.float32)
        for piece in range(reach + 1):
            mixed += jnp.dot(
                (terms[piece] * inverse).astype(jnp.bfloat16),
                windows[piece][:, head_dim:],
                preferred_element_type=jnp.float32,
            )
        mixed_ref[:, span] = mixed.astype(jnp.bfloat16)


def attend(queries, windows, key_seg, query_seg, head_dim):
    reach = len(windows) - 1
    rows = queries.shape[0]
    kernel = functools.partial(attend_kernel, head_dim, reach)
    return pl.pallas_call(
        kernel,
        out_shape=pltpu.VMEM(queries.shape, jnp.bfloat16),
        in_specs=[IN_VMEM] * (3 + len(windows)),
        out_specs=IN_VMEM,
        compiler_params=params(),
        name="attend",
    )(*in_vmem(queries, key_seg.reshape(1, -1), query_seg.reshape(rows, 1), *windows))


def join_projections_kernel(plane_ref, *refs):
    own, beside, (near_out, common_out, far_out, sems) = refs[:3], refs[3:6], refs[6:]
    q_half, kv_half = near_out.shape[2], common_out.shape[2] // 2
    near = pl.ds(pl.multiple_of(plane_ref[0] * q_half, q_half), q_half)
    far = pl.ds(pl.multiple_of((1 - plane_ref[0]) * q_half, q_half), q_half)
    moves = [(own[0].at[:, far], far_out.at[0])]
    for slot, (query_ref, key_ref, value_ref) in enumerate((own, beside)):
        moves += [
            (query_ref.at[:, near], near_out.at[slot]),
            (key_ref, common_out.at[slot, :, :kv_half]),
            (value_ref, common_out.at[slot, :, kv_half:]),
        ]
    copies = [
        pltpu.make_async_copy(source, target, sems.at[place])
        for place, (source, target) in enumerate(moves)
    ]
    for copy in copies:
        copy.start()
    for copy in copies:
        copy.wait()


def join_projections(plane, own, beside):
    query, key, value = own
    depth, q_half = query.shape[0], query.shape[1] // 2
    shapes = ((2, depth, q_half), (2, depth, 2 * key.shape[1]), (1, depth, q_half))
    return pl.pallas_call(
        join_projections_kernel,
        in_specs=[IN_SMEM] + [IN_HBM] * 3 + [IN_VMEM] * 3,
        out_specs=[IN_VMEM] * 3,
        scratch_shapes=[pltpu.SemaphoreType.DMA((7,))],
        out_shape=[pltpu.VMEM(shape, jnp.bfloat16) for shape in shapes],
        compiler_params=params(),
        name="join_projections",
    )(plane, *in_hbm(*own), *in_vmem(*beside))


def project_kernel(slots, groups, first, last, index_ref, *refs):
    sources, refs = refs[:2], refs[2:]
    refs, (tokens, sems) = refs[:-2], refs[-2:]
    rows, depth = tokens.shape[1:]
    copies = []
    for place in range(len(slots)):
        column = pl.multiple_of(index_ref[1 + place] * depth, depth)
        for side in range(2):
            entry = 2 * place + side
            copy = pltpu.make_async_copy(
                sources[side].at[:, pl.ds(column, depth)], tokens.at[entry], sems.at[entry]
            )
            copy.start()
            copies.append(copy)
    held_weights = groups * (1 + slots[-1][0])
    weights, refs = refs[:held_weights], refs[held_weights:]
    total_ref, refs = (None, refs) if first else (refs[0], refs[1:])
    block = rows // 2
    width = weights[0].shape[-1]
    out_ref = refs[2] if last else refs[0]
    for copy in copies:
        copy.wait()
    for side in range(2):
        for group in range(groups):
            columns = pl.ds(group * width, width)
            total = None if first else total_ref[side, :, columns]
            for place, (step, slot) in enumerate(slots):
                product = jnp.dot(
                    tokens[2 * place + side],
                    weights[groups * step + group][slot],
                    preferred_element_type=jnp.float32,
                )
                total = product if total is None else total + product
            out_ref[side, :, columns] = total
    if last:
        kept_ref, sent_ref, held = refs
        mine = pl.multiple_of(index_ref[0] * block, block)
        others = pl.multiple_of((1 - index_ref[0]) * block, block)
        kept_ref[:block] = held[0, pl.ds(mine, block), :]
        kept_ref[block:] = held[1, pl.ds(mine, block), :]
        sent_ref[:block] = held[1, pl.ds(others, block), :]
        sent_ref[block:] = held[0, pl.ds(others, block), :]


def project(index, tokens, steps, total, last):
    groups = len(steps[0][1])
    slots = [(i, slot) for i, (used, _) in enumerate(steps) for slot in range(used)]
    rows = tokens[0].shape[0]
    depth = steps[0][1][0].shape[1]
    columns = sum(part.shape[2] for part in steps[0][1])
    operands = in_hbm(tokens[0]) + in_vmem(tokens[1], *(part for _, parts in steps for part in parts))
    if total is not None:
        operands += in_vmem(total)
    specs = [IN_SMEM, IN_HBM] + [IN_VMEM] * (len(operands) - 1)
    shapes = ((rows, columns), (rows, columns)) if last else ((2, rows, columns),)
    out = pl.pallas_call(
        functools.partial(project_kernel, slots, groups, total is None, last),
        in_specs=specs,
        out_specs=[IN_VMEM] * len(shapes),
        scratch_shapes=([pltpu.VMEM((2, rows, columns), jnp.float32)] if last else [])
        + [
            pltpu.VMEM((2 * len(slots), rows, depth), jnp.bfloat16),
            pltpu.SemaphoreType.DMA((2 * len(slots),)),
        ],
        out_shape=[pltpu.VMEM(shape, jnp.float32) for shape in shapes],
        compiler_params=params(),
        name="project",
    )(index, *operands)
    return out if last else out[0]


def columns_kernel(places, index_ref, mixed_ref, returned_ref, *refs):
    weights = list(refs[: sum(places)])
    out_ref, send_ref, held, sems = refs[-4:]
    block = mixed_ref.shape[0] // 2
    half = mixed_ref.shape[1] // 2
    width = weights[0].shape[-1]
    mine = pl.ds(pl.multiple_of(index_ref[0] * block, block), block)
    others = pl.ds(pl.multiple_of((1 - index_ref[0]) * block, block), block)
    near = pl.ds(pl.multiple_of(index_ref[1] * half, half), half)
    far = pl.ds(pl.multiple_of((1 - index_ref[1]) * half, half), half)
    rows_in = jnp.concatenate([mixed_ref[...], returned_ref[...]], axis=0)
    copies = []
    for place, parts in enumerate(places):
        if parts == 1:
            whole = weights.pop(0)
            low, high = whole[near, :], whole[far, :]
        else:
            low, high = weights.pop(0)[...], weights.pop(0)[...]
        weight = jnp.concatenate([low, high], axis=0)
        value = jnp.dot(rows_in, weight, preferred_element_type=jnp.float32)
        value = value.astype(jnp.bfloat16)
        columns = pl.ds(place * width, width)
        held[mine, columns] = value[:block]
        held[others, columns] = value[3 * block :]
        send_ref[mine, columns] = value[block : 2 * block]
        send_ref[others, columns] = value[2 * block : 3 * block]
        column = pl.multiple_of(index_ref[2 + place] * width, width)
        copy = pltpu.make_async_copy(
            held.at[:, columns], out_ref.at[:, pl.ds(column, width)], sems.at[place]
        )
        copy.start()
        copies.append(copy)
    for copy in copies:
        copy.wait()


def columns_of(index, mixed, returned, shards, result, width):
    rows = mixed.shape[0]
    out_cols = shards[0][0].shape[-1]
    operands = in_vmem(mixed, returned, *(part for shard in shards for part in shard))
    specs = [IN_SMEM] + [IN_VMEM] * len(operands)
    if result is not None:
        operands += in_hbm(result)
        specs.append(IN_HBM)
    sent = (rows, len(shards) * out_cols)
    return pl.pallas_call(
        functools.partial(columns_kernel, [len(shard) for shard in shards]),
        in_specs=specs,
        out_specs=[IN_HBM, IN_VMEM],
        scratch_shapes=[
            pltpu.VMEM(sent, jnp.bfloat16),
            pltpu.SemaphoreType.DMA((len(shards),)),
        ],
        out_shape=[pltpu.HBM((rows, width), jnp.bfloat16), pltpu.VMEM(sent, jnp.bfloat16)],
        input_output_aliases={} if result is None else {len(operands): 0},
        compiler_params=params(),
        name="columns_of",
    )(index, *operands)


def place_kernel(width, owners_ref, came_ref, _, out_ref, sems):
    copies = []
    for place in range(came_ref.shape[1] // width):
        column = pl.multiple_of(owners_ref[place] * width, width)
        copy = pltpu.make_async_copy(
            came_ref.at[:, pl.ds(place * width, width)],
            out_ref.at[:, pl.ds(column, width)],
            sems.at[place],
        )
        copy.start()
        copies.append(copy)
    for copy in copies:
        copy.wait()


def place_columns(owners, came, result, out_cols):
    return pl.pallas_call(
        functools.partial(place_kernel, out_cols),
        in_specs=[IN_SMEM, IN_VMEM, IN_HBM],
        out_specs=IN_HBM,
        scratch_shapes=[pltpu.SemaphoreType.DMA((came.shape[1] // out_cols,))],
        out_shape=pltpu.HBM(result.shape, result.dtype),
        input_output_aliases={2: 0},
        compiler_params=params(),
        name="place_columns",
    )(owners, *in_vmem(came), *in_hbm(result))


def on_device(hidden_in, segment_ids, w_query, w_key, w_value, w_out):
    count = lax.axis_size("ctx")
    me = lax.axis_index("ctx")
    plane = lax.axis_index("dp")
    core, chip = me % 2, me // 2
    rows, width = hidden_in.shape
    block = rows // 2
    head_dim = w_key.shape[1]
    q_rows, out_cols = w_out.shape
    q_half = q_rows // 2

    ringed = count <= RING_LIMIT
    if ringed:
        depth = w_query.shape[0]
        plane_index = plane.reshape(1).astype(jnp.int32)
        pairs = ring_pairs(count // 2)
        half = count // 4
        owners = shard_owners(me, count)

        def ring(value):
            return lax.ppermute(value, "ctx", pairs)

        own = (w_query, w_key, w_value)
        beside = tuple(core_swap(part, count) for part in own)
        near, common, own_far = join_projections(plane_index, own, beside)
        steps = [(1, (common, near, own_far))]
        other = core_swap(after(hidden_in, near), count)

        def add_projections(total, begin, end):
            place = 0 if begin == 0 else 2 * begin - 1
            used = sum(step[0] for step in steps[begin:end])
            index = jnp.stack([core, *owners[place : place + used]]).astype(jnp.int32)
            return project(index, (hidden_in, other), steps[begin:end], total, end == half + 1)

        total = None
        for step in range(1, half + 1):
            if step == half:
                near, common = near[:1], common[:1]
            if step > 2:
                near = after(near, steps[step - 2][1][2])
            near = ring(near)
            if step == 2:
                beside_near = lax.dynamic_slice(w_out, (plane * q_half, 0), (q_half, out_cols))
                beside_near = core_swap(after(beside_near, near), count)
            if step == 4:
                total = add_projections(None, 0, 2)
                common = after(common, total)
            common = ring(after(common, near))
            steps.append((near.shape[0], (common, near, plane_swap(near))))

        total = add_projections(total, 2, 3)
        out_near = after(beside_near, near, steps[half - 1][1][0], steps[half - 1][1][2])
        out_whole = after(w_out, common, total)
        shards = [(w_out,)]
        for step in range(1, half + 1):
            if step == 2:
                out_near = after(out_near, steps[half][1][2])
            if step > 2:
                out_near = after(out_near, shards[-1][1])
            if step < half:
                out_near = ring(out_near)
            out_whole = ring(out_whole)
            shards.append((out_whole,))
            if step < half:
                shards.append((out_near, plane_swap(out_near)))
        total = add_projections(total, 3, 4)
        kept, sent = add_projections(total, 4, 5)
        came = core_swap(sent, count)
    else:
        gathered = lax.all_gather(
            jnp.concatenate([w_key, w_value, w_query], axis=1), "ctx", axis=0, tiled=True
        )
        ordered = jnp.where(core == 0, hidden_in, jnp.roll(hidden_in, block, axis=0))
        pair_tokens = jnp.concatenate([ordered[:block], core_swap(ordered[block:], count)], axis=0)
        kept = jnp.dot(pair_tokens, gathered, preferred_element_type=jnp.float32)
        came = jnp.zeros_like(kept)

    if ringed:
        came = after(came, shards[1][0], shards[2][0])
    pair = jnp.where(core == 0, chip, count - 1 - chip)
    pair_pos = pair * rows + jnp.arange(rows, dtype=jnp.int32)
    joined, queries = rotate_sums(kept, came, pair_pos, head_dim)

    reach = REACH * block // rows
    windows = [joined]
    for back in range(1, reach + 1):
        sends = [
            (pair_device(m, count), pair_device(m + back, count)) for m in range(count - back)
        ]
        windows.append(lax.ppermute(joined, "ctx", sends))

    seg_blocks = segment_ids.reshape(2 * count, block)
    seq_block = pair * 2 - 2 * reach + jnp.arange(2 * reach + 2, dtype=jnp.int32)
    clipped = jnp.maximum(seq_block, 0)
    stored = jnp.where(clipped < count, 2 * clipped, 2 * (2 * count - 1 - clipped) + 1)
    seg_rows = seg_blocks[stored]
    key_seg = jnp.where(seq_block[:, None] >= 0, seg_rows, -1).reshape(-1)
    if ringed:
        queries = after(queries, shards[3][0], shards[4][0])
    mixed = attend(queries, windows[::-1], key_seg, seg_rows[-2:].reshape(-1), head_dim)

    returned = core_swap(mixed, count)
    if not ringed:
        kinds = (mixed[:block], returned[block:])
        own_rows = jnp.where(
            core == 0, jnp.concatenate(kinds, axis=0), jnp.concatenate(kinds[::-1], axis=0)
        )
        gathered = lax.all_gather(w_out, "ctx", axis=1, tiled=True)
        return jnp.dot(own_rows, gathered, preferred_element_type=jnp.float32).astype(jnp.bfloat16)

    returned = after(returned, shards[5][0], shards[6][0])
    other_owners = shard_owners(me ^ 1, count)
    arrivals = []
    result = None
    for begin, end in ((0, 5), (5, len(shards))):
        index = jnp.stack([core, plane, *owners[begin:end]]).astype(jnp.int32)
        result, sent = columns_of(index, mixed, returned, shards[begin:end], result, width)
        arrivals.append((other_owners[begin:end], core_swap(sent, count)))
    for senders, came in arrivals:
        result = place_columns(jnp.stack(senders).astype(jnp.int32), came, result, out_cols)
    return result


def solution(mesh):
    in_specs = (
        P(("dp", "ctx"), None),
        P("dp"),
        P("ctx", None),
        P("ctx", None),
        P("ctx", None),
        P(None, "ctx"),
    )
    out_specs = P(("dp", "ctx"), None)
    return jax.shard_map(
        on_device, mesh=mesh, in_specs=in_specs, out_specs=out_specs, check_vma=False
    )
```

```python
import functools
import math

import jax
import jax.numpy as jnp
from jax import lax
from jax.experimental import pallas as pl
from jax.experimental.pallas import tpu as pltpu
from jax.sharding import PartitionSpec as P

REACH = 8
ROPE_BASE = 500000.0
RING_LIMIT = 16
VMEM_LIMIT = 16 * 1024 * 1024


def chip_at(place, chips):
    place = place % chips
    return jnp.where(place < chips // 2, 2 * place, 2 * (chips - 1 - place) + 1)


def static_chip_at(place, chips):
    place %= chips
    return 2 * place if place < chips // 2 else 2 * (chips - 1 - place) + 1


def ring_pairs(chips):
    pairs = []
    for place in range(chips):
        here = static_chip_at(place, chips)
        pairs.append((2 * here, 2 * static_chip_at(place + 1, chips)))
        pairs.append((2 * here + 1, 2 * static_chip_at(place - 1, chips) + 1))
    return pairs


def core_swap(value, count):
    return lax.ppermute(value, "ctx", [(i, i ^ 1) for i in range(count)])


def plane_swap(value):
    return lax.ppermute(value, "dp", [(0, 1), (1, 0)])


def row_device(row, column, count):
    pair = 2 * row + (column if row < count // 4 else 1 - column)
    return 2 * pair if pair < count // 2 else 2 * (count - 1 - pair) + 1


def after(value, *others):
    return lax.optimization_barrier((value, *others))[0]


def shard_owners(me, count):
    chips = count // 2
    half = chips // 2
    core, chip = me % 2, me // 2
    place = jnp.where(chip % 2 == 0, chip // 2, chips - 1 - chip // 2)
    way = jnp.where(core == 0, -1, 1)
    owners = [me]
    for step in range(1, half + 1):
        source = chip_at(place + way * step + chips, chips)
        owners.append(2 * source + core)
        if step < half:
            owners.append(2 * source + 1 - core)
    return owners


def params(**settings):
    return pltpu.CompilerParams(vmem_limit_bytes=VMEM_LIMIT, **settings)


def in_vmem(*arrays):
    return [pltpu.with_memory_space_constraint(array, pltpu.VMEM) for array in arrays]


def in_hbm(*arrays):
    return [pltpu.with_memory_space_constraint(array, pltpu.HBM) for array in arrays]


IN_VMEM = pl.BlockSpec(memory_space=pltpu.VMEM)
IN_HBM = pl.BlockSpec(memory_space=pl.ANY)
IN_SMEM = pl.BlockSpec(memory_space=pltpu.SMEM)


def rotate_kernel(head_dim, kept_ref, came_ref, cos_ref, sin_ref, joined_ref, query_ref):
    cosine, sine = cos_ref[...], sin_ref[...]

    def rotated(column):
        span = pl.ds(column, head_dim)
        part = kept_ref[:, span] + came_ref[:, span]
        return (part * cosine + pltpu.roll(part, head_dim // 2, 1) * sine).astype(jnp.bfloat16)

    joined_ref[:, :head_dim] = rotated(0)
    values = pl.ds(head_dim, head_dim)
    joined_ref[:, values] = (kept_ref[:, values] + came_ref[:, values]).astype(jnp.bfloat16)
    for column in range(0, query_ref.shape[1], head_dim):
        query_ref[:, pl.ds(column, head_dim)] = rotated(2 * head_dim + column)


def rotary_tables(positions, head_dim):
    frequency = ROPE_BASE ** (
        -(jnp.arange(head_dim // 2, dtype=jnp.float32) * 2.0) / head_dim
    )
    angles = positions.astype(jnp.float32)[:, None] * frequency[None, :]
    cosine, sine = jnp.cos(angles), jnp.sin(angles)
    return jnp.concatenate([cosine, cosine], axis=1), jnp.concatenate([-sine, sine], axis=1)


def rotate_sums(kept, came, cosine, sine):
    rows, columns = kept.shape
    head_dim = cosine.shape[1]
    return pl.pallas_call(
        functools.partial(rotate_kernel, head_dim),
        out_shape=(
            pltpu.VMEM((rows, 2 * head_dim), jnp.bfloat16),
            pltpu.VMEM((rows, columns - 2 * head_dim), jnp.bfloat16),
        ),
        in_specs=[IN_VMEM] * 4,
        out_specs=(IN_VMEM, IN_VMEM),
        compiler_params=params(),
        name="rotate_sums",
    )(*in_vmem(kept, came, cosine, sine))


def join_row_kernel(index_ref, own_ref, beside_ref, out_ref):
    odd = index_ref[2]
    out_ref[odd] = own_ref[...]
    out_ref[1 - odd] = beside_ref[...]


def join_row(index, own, beside):
    return pl.pallas_call(
        join_row_kernel,
        in_specs=[IN_SMEM, IN_VMEM, IN_VMEM],
        out_specs=IN_VMEM,
        out_shape=pltpu.VMEM((2, *own.shape), own.dtype),
        compiler_params=params(),
        name="join_row",
    )(index, *in_vmem(own, beside))


def attend_kernel(head_dim, reach, index_ref, query_ref, key_seg_ref, *refs):
    row_refs, (mixed_ref, window) = refs[:-2], refs[-2:]
    rows = query_ref.shape[0]
    for place, row_ref in enumerate(row_refs):
        window[2 * place : 2 * place + 2] = row_ref[...]
    odd = index_ref[2]
    own_seg = key_seg_ref[:, pl.ds(reach * rows, rows)]
    query_seg = jnp.transpose(jnp.broadcast_to(own_seg, (rows, rows)))
    base = lax.broadcasted_iota(jnp.int32, (rows, rows), 0)
    offset = lax.broadcasted_iota(jnp.int32, (rows, rows), 1)
    allowed = []
    for piece in range(reach + 1):
        same = query_seg == key_seg_ref[:, pl.ds(piece * rows, rows)]
        if piece == reach:
            same = same & (offset <= base)
        allowed.append(same)
    for column in range(0, query_ref.shape[1], head_dim):
        span = pl.ds(column, head_dim)
        query = query_ref[:, span]
        scores = []
        for piece in range(reach + 1):
            score = lax.dot_general(
                query,
                window[odd + piece, :, :head_dim],
                (((1,), (1,)), ((), ())),
                preferred_element_type=jnp.float32,
            ) / math.sqrt(head_dim)
            scores.append(jnp.where(allowed[piece], score, -1e30))
        peak = scores[0]
        for score in scores[1:]:
            peak = jnp.maximum(peak, score)
        peak = jnp.max(peak, axis=1, keepdims=True)
        terms = [jnp.exp(score - peak) for score in scores]
        total = terms[0]
        for term in terms[1:]:
            total = total + term
        inverse = 1.0 / jnp.sum(total, axis=1, keepdims=True)
        mixed = jnp.zeros((rows, head_dim), jnp.float32)
        for piece in range(reach + 1):
            mixed += jnp.dot(
                (terms[piece] * inverse).astype(jnp.bfloat16),
                window[odd + piece, :, head_dim:],
                preferred_element_type=jnp.float32,
            )
        mixed_ref[:, span] = mixed.astype(jnp.bfloat16)


def attend(index, queries, row_windows, key_seg, head_dim):
    reach = 2 * len(row_windows) - 2
    rows = queries.shape[0]
    return pl.pallas_call(
        functools.partial(attend_kernel, head_dim, reach),
        out_shape=pltpu.VMEM(queries.shape, jnp.bfloat16),
        in_specs=[IN_SMEM] + [IN_VMEM] * (2 + len(row_windows)),
        out_specs=IN_VMEM,
        scratch_shapes=[pltpu.VMEM((reach + 2, rows, 2 * head_dim), jnp.bfloat16)],
        compiler_params=params(),
        name="attend",
    )(index, *in_vmem(queries, key_seg, *row_windows))


def join_projections_kernel(plane_ref, *refs):
    own, beside, refs = refs[:3], refs[3:6], refs[6:]
    near_out, common_out, far_out, sems = refs
    q_half, kv_half = near_out.shape[2], common_out.shape[2] // 2
    near = pl.ds(pl.multiple_of(plane_ref[0] * q_half, q_half), q_half)
    far = pl.ds(pl.multiple_of((1 - plane_ref[0]) * q_half, q_half), q_half)
    moves = [(own[0].at[:, far], far_out.at[0])]
    for slot, (query_ref, key_ref, value_ref) in enumerate((own, beside)):
        moves += [
            (query_ref.at[:, near], near_out.at[slot]),
            (key_ref, common_out.at[slot, :, :kv_half]),
            (value_ref, common_out.at[slot, :, kv_half:]),
        ]
    copies = [
        pltpu.make_async_copy(source, target, sems.at[place])
        for place, (source, target) in enumerate(moves)
    ]
    for copy in copies:
        copy.start()
    for copy in copies:
        copy.wait()


def join_projections(plane, own, beside):
    query, key, _ = own
    depth, q_half = query.shape[0], query.shape[1] // 2
    shapes = (
        (2, depth, q_half),
        (2, depth, 2 * key.shape[1]),
        (1, depth, q_half),
    )
    return pl.pallas_call(
        join_projections_kernel,
        in_specs=[IN_SMEM] + [IN_HBM] * 3 + [IN_VMEM] * 3,
        out_specs=[IN_VMEM] * 3,
        scratch_shapes=[pltpu.SemaphoreType.DMA((7,))],
        out_shape=[pltpu.VMEM(shape, jnp.bfloat16) for shape in shapes],
        compiler_params=params(),
        name="join_projections",
    )(plane, *in_hbm(*own), *in_vmem(*beside))


def first_kernel(pair_ref, out_ref):
    out_ref[...] = pair_ref[:1]


def first_of(pair):
    return pl.pallas_call(
        first_kernel,
        in_specs=[IN_VMEM],
        out_specs=IN_VMEM,
        out_shape=pltpu.VMEM((1, *pair.shape[1:]), pair.dtype),
        compiler_params=params(),
        name="first_of",
    )(*in_vmem(pair))


def project_kernel(slots, base, groups, first, last, index_ref, own_ref, other_ref, *refs):
    refs, (tokens, sems) = refs[:-2], refs[-2:]
    rows, depth = tokens.shape[1:]
    spans = [
        pl.ds(pl.multiple_of(index_ref[3 + base + place] * depth, depth), depth)
        for place in range(len(slots))
    ]
    copies = [
        pltpu.make_async_copy(own_ref.at[:, span], tokens.at[place], sems.at[place])
        for place, span in enumerate(spans)
    ]
    for copy in copies:
        copy.start()
    held_weights = groups * (1 + slots[-1][0])
    weights, refs = refs[:held_weights], refs[held_weights:]
    total_ref, refs = (None, refs) if first else (refs[0], refs[1:])
    block = rows // 2
    width = weights[0].shape[-1]
    out_ref = refs[2] if last else refs[0]
    for side in (1, 0):
        if side == 0:
            for copy in copies:
                copy.wait()
        for group in range(groups):
            columns = pl.ds(group * width, width)
            total = None if first else total_ref[side, :, columns]
            for place, (step, slot) in enumerate(slots):
                product = jnp.dot(
                    tokens[place] if side == 0 else other_ref[:, spans[place]],
                    weights[groups * step + group][slot],
                    preferred_element_type=jnp.float32,
                )
                total = product if total is None else total + product
            out_ref[side, :, columns] = total
    if last:
        kept_ref, sent_ref, held = refs
        mine = pl.ds(pl.multiple_of(index_ref[0] * block, block), block)
        others = pl.ds(pl.multiple_of((1 - index_ref[0]) * block, block), block)
        kept_ref[:block] = held[0, mine, :]
        kept_ref[block:] = held[1, mine, :]
        sent_ref[:block] = held[1, others, :]
        sent_ref[block:] = held[0, others, :]


def project(index, base, tokens, steps, total, last):
    groups = len(steps[0][1])
    slots = [(i, slot) for i, (used, _) in enumerate(steps) for slot in range(used)]
    rows = tokens[0].shape[0]
    depth = steps[0][1][0].shape[1]
    columns = sum(part.shape[2] for part in steps[0][1])
    operands = in_hbm(tokens[0]) + in_vmem(tokens[1], *(part for _, parts in steps for part in parts))
    if total is not None:
        operands += in_vmem(total)
    shapes = ((rows, columns), (rows, columns)) if last else ((2, rows, columns),)
    out = pl.pallas_call(
        functools.partial(project_kernel, slots, base, groups, total is None, last),
        in_specs=[IN_SMEM, IN_HBM] + [IN_VMEM] * (len(operands) - 1),
        out_specs=[IN_VMEM] * len(shapes),
        scratch_shapes=([pltpu.VMEM((2, rows, columns), jnp.float32)] if last else [])
        + [
            pltpu.VMEM((len(slots), rows, depth), jnp.bfloat16),
            pltpu.SemaphoreType.DMA((len(slots),)),
        ],
        out_shape=[pltpu.VMEM(shape, jnp.float32) for shape in shapes],
        compiler_params=params(),
        name="project",
    )(index, *operands)
    return out if last else out[0]


def columns_kernel(shards, base, index_ref, mixed_ref, returned_ref, *refs):
    weights = refs[:shards]
    out_ref, send_ref, held, sems = refs[-4:]
    block = mixed_ref.shape[0] // 2
    half = mixed_ref.shape[1] // 2
    width = weights[0].shape[-1]
    mine = pl.ds(pl.multiple_of(index_ref[0] * block, block), block)
    others = pl.ds(pl.multiple_of((1 - index_ref[0]) * block, block), block)
    rows_in = jnp.concatenate([mixed_ref[...], returned_ref[...]], axis=0)
    near, far = rows_in[:, :half], rows_in[:, half:]
    low = index_ref[1] == 0
    rows_in = jnp.concatenate([jnp.where(low, near, far), jnp.where(low, far, near)], axis=1)
    copies = []
    for place in range(shards):
        value = jnp.dot(rows_in, weights[place][...], preferred_element_type=jnp.float32)
        value = value.astype(jnp.bfloat16)
        columns = pl.ds(place * width, width)
        held[mine, columns] = value[:block]
        held[others, columns] = value[3 * block :]
        send_ref[mine, columns] = value[block : 2 * block]
        send_ref[others, columns] = value[2 * block : 3 * block]
        column = pl.multiple_of(index_ref[3 + base + place] * width, width)
        copy = pltpu.make_async_copy(
            held.at[:, columns], out_ref.at[:, pl.ds(column, width)], sems.at[place]
        )
        copy.start()
        copies.append(copy)
    for copy in copies:
        copy.wait()


def columns_of(index, base, mixed, returned, shards, result, width):
    rows = mixed.shape[0]
    out_cols = shards[0].shape[1]
    operands = in_vmem(mixed, returned, *shards)
    specs = [IN_SMEM] + [IN_VMEM] * len(operands)
    if result is not None:
        operands += in_hbm(result)
        specs.append(IN_HBM)
    sent = (rows, len(shards) * out_cols)
    return pl.pallas_call(
        functools.partial(columns_kernel, len(shards), base),
        in_specs=specs,
        out_specs=[IN_HBM, IN_VMEM],
        scratch_shapes=[
            pltpu.VMEM(sent, jnp.bfloat16),
            pltpu.SemaphoreType.DMA((len(shards),)),
        ],
        out_shape=[pltpu.HBM((rows, width), jnp.bfloat16), pltpu.VMEM(sent, jnp.bfloat16)],
        input_output_aliases={} if result is None else {len(operands): 0},
        compiler_params=params(),
        name="columns_of",
    )(index, *operands)


def place_kernel(width, base, index_ref, came_ref, _, out_ref, sems):
    copies = []
    for place in range(came_ref.shape[1] // width):
        column = pl.multiple_of(index_ref[base + place] * width, width)
        copy = pltpu.make_async_copy(
            came_ref.at[:, pl.ds(place * width, width)],
            out_ref.at[:, pl.ds(column, width)],
            sems.at[place],
        )
        copy.start()
        copies.append(copy)
    for copy in copies:
        copy.wait()


def place_columns(index, base, came, result, out_cols):
    return pl.pallas_call(
        functools.partial(place_kernel, out_cols, base),
        in_specs=[IN_SMEM, IN_VMEM, IN_HBM],
        out_specs=IN_HBM,
        scratch_shapes=[pltpu.SemaphoreType.DMA((came.shape[1] // out_cols,))],
        out_shape=pltpu.HBM(result.shape, result.dtype),
        input_output_aliases={2: 0},
        compiler_params=params(),
        name="place_columns",
    )(index, *in_vmem(came), *in_hbm(result))


def on_device(hidden_in, segment_ids, w_query, w_key, w_value, w_out):
    count = lax.axis_size("ctx")
    me = lax.axis_index("ctx")
    plane = lax.axis_index("dp")
    core, chip = me % 2, me // 2
    rows, width = hidden_in.shape
    block = rows // 2
    head_dim = w_key.shape[1]
    q_rows, out_cols = w_out.shape
    q_half = q_rows // 2

    reach = REACH * block // rows
    pair = jnp.where(core == 0, chip, count - 1 - chip)
    pair_pos = pair * rows + jnp.arange(rows, dtype=jnp.int32)
    cosine, sine = rotary_tables(pair_pos, head_dim)
    seg_blocks = segment_ids.reshape(2 * count, block)
    seq_block = pair * 2 - 2 * reach + jnp.arange(2 * reach + 2, dtype=jnp.int32)
    clipped = jnp.maximum(seq_block, 0)
    stored = jnp.where(clipped < count, 2 * clipped, 2 * (2 * count - 1 - clipped) + 1)
    seg_rows = seg_blocks[stored]
    key_seg = jnp.where(seq_block[:, None] >= 0, seg_rows, -1).reshape(1, -1)
    tables = (cosine, sine, key_seg)
    index = [core, plane, pair % 2]

    ringed = count <= RING_LIMIT
    if ringed:
        plane_index = plane.reshape(1).astype(jnp.int32)
        pairs = ring_pairs(count // 2)
        half = count // 4
        owners = shard_owners(me, count)
        index += [*owners, *shard_owners(me ^ 1, count)]
        index = jnp.stack(index).astype(jnp.int32)

        def ring(value):
            return lax.ppermute(value, "ctx", pairs)

        own = (w_query, w_key, w_value)
        beside = tuple(core_swap(part, count) for part in own)
        near, common, own_far = join_projections(plane_index, own, beside)
        steps = [(1, (common, near, own_far))]

        def add_projections(total, begin, end):
            base = 0 if begin == 0 else 2 * begin - 1
            return project(index, base, (hidden_in, other), steps[begin:end], total, end == half + 1)

        out_flows = [w_out, None]
        shards = [w_out]
        total = None
        for step in range(1, half + 1):
            if step == 2:
                near, index, *tables = lax.optimization_barrier((near, index, *tables))
                other = core_swap(after(hidden_in, near), count)
                out_flows[1] = core_swap(after(w_out, near), count)
            if step == half:
                near = first_of(after(near, steps[step - 2][1][2]))
            near = ring(near)
            if step > 1:
                common = after(common, steps[step - 1][1][2])
            if step > 2:
                held = after(steps[step - 3][1][0], shards[-1])
                steps[step - 3] = (steps[step - 3][0], (held, *steps[step - 3][1][1:]))
                total = add_projections(total, step - 3, step - 2)
                common = after(common, total)
            if step == half:
                common = first_of(common)
            common = ring(after(common, near))
            steps.append((near.shape[0], (common, near, plane_swap(near))))
            turn = (step - 1) % 2
            out_flows[turn] = ring(after(out_flows[turn], near))
            shards.append(out_flows[turn])

        held = after(steps[half - 2][1][0], shards[-1])
        steps[half - 2] = (steps[half - 2][0], (held, *steps[half - 2][1][1:]))
        total = add_projections(total, half - 2, half - 1)
        total = add_projections(total, half - 1, half)
        for step in range(half + 1, 2 * half):
            turn = (step - 1) % 2
            out_flows[turn] = ring(after(out_flows[turn], common))
            shards.append(out_flows[turn])
        kept, sent = add_projections(total, half, half + 1)
        came = core_swap(sent, count)
    else:
        gathered = lax.all_gather(
            jnp.concatenate([w_key, w_value, w_query], axis=1), "ctx", axis=0, tiled=True
        )
        ordered = jnp.where(core == 0, hidden_in, jnp.roll(hidden_in, block, axis=0))
        pair_tokens = jnp.concatenate([ordered[:block], core_swap(ordered[block:], count)], axis=0)
        kept = jnp.dot(pair_tokens, gathered, preferred_element_type=jnp.float32)
        came = jnp.zeros_like(kept)

    cosine, sine, key_seg = tables
    joined, queries = rotate_sums(kept, came, cosine, sine)

    if not ringed:
        index = jnp.stack(index).astype(jnp.int32)
    sends = [(device, device ^ 2) for device in range(count)]
    own_row = join_row(index, joined, lax.ppermute(joined, "ctx", sends))
    row_count = count // 2
    windows = [own_row]
    for back in range(1, reach // 2 + 1):
        sends = [
            (row_device(row, column, count), row_device(row + back, column, count))
            for row in range(row_count - back)
            for column in range(2)
        ]
        windows.append(lax.ppermute(own_row, "ctx", sends))

    if ringed:
        queries = after(queries, shards[5], shards[6])
    mixed = attend(index, queries, windows[::-1], key_seg, head_dim)

    returned = core_swap(mixed, count)
    if not ringed:
        kinds = (mixed[:block], returned[block:])
        own_rows = jnp.where(
            core == 0, jnp.concatenate(kinds, axis=0), jnp.concatenate(kinds[::-1], axis=0)
        )
        gathered = lax.all_gather(w_out, "ctx", axis=1, tiled=True)
        return jnp.dot(own_rows, gathered, preferred_element_type=jnp.float32).astype(jnp.bfloat16)

    arrivals = []
    result = None
    for begin, end in ((0, 5), (5, len(shards))):
        result, sent = columns_of(index, begin, mixed, returned, shards[begin:end], result, width)
        arrivals.append((3 + len(shards) + begin, core_swap(sent, count)))
    for base, came in arrivals:
        result = place_columns(index, base, came, result, out_cols)
    return result


def solution(mesh):
    in_specs = (
        P(("dp", "ctx"), None),
        P("dp"),
        P("ctx", None),
        P("ctx", None),
        P("ctx", None),
        P(None, "ctx"),
    )
    out_specs = P(("dp", "ctx"), None)
    return jax.shard_map(
        on_device, mesh=mesh, in_specs=in_specs, out_specs=out_specs, check_vma=False
    )
```

```python
import functools
import math

import jax
import jax.numpy as jnp
from jax import lax
from jax.experimental import pallas as pl
from jax.experimental.pallas import tpu as pltpu
from jax.sharding import PartitionSpec as P

REACH = 8
ROPE_BASE = 500000.0
RING_LIMIT = 16
VMEM_LIMIT = 16 * 1024 * 1024


def chip_at(place, chips):
    place = place % chips
    return jnp.where(place < chips // 2, 2 * place, 2 * (chips - 1 - place) + 1)


def static_chip_at(place, chips):
    place %= chips
    return 2 * place if place < chips // 2 else 2 * (chips - 1 - place) + 1


def ring_pairs(chips):
    pairs = []
    for place in range(chips):
        here = static_chip_at(place, chips)
        pairs.append((2 * here, 2 * static_chip_at(place + 1, chips)))
        pairs.append((2 * here + 1, 2 * static_chip_at(place - 1, chips) + 1))
    return pairs


def core_swap(value, count):
    return lax.ppermute(value, "ctx", [(i, i ^ 1) for i in range(count)])


def plane_swap(value):
    return lax.ppermute(value, "dp", [(0, 1), (1, 0)])


def row_device(row, column, count):
    pair = 2 * row + (column if row < count // 4 else 1 - column)
    return 2 * pair if pair < count // 2 else 2 * (count - 1 - pair) + 1


def after(value, *others):
    return lax.optimization_barrier((value, *others))[0]


def shard_owners(me, count):
    chips = count // 2
    half = chips // 2
    core, chip = me % 2, me // 2
    place = jnp.where(chip % 2 == 0, chip // 2, chips - 1 - chip // 2)
    way = jnp.where(core == 0, -1, 1)
    owners = [me]
    for step in range(1, half + 1):
        source = chip_at(place + way * step + chips, chips)
        owners.append(2 * source + core)
        if step < half:
            owners.append(2 * source + 1 - core)
    return owners


def params(**settings):
    return pltpu.CompilerParams(vmem_limit_bytes=VMEM_LIMIT, **settings)


def in_vmem(*arrays):
    return [pltpu.with_memory_space_constraint(array, pltpu.VMEM) for array in arrays]


def in_hbm(*arrays):
    return [pltpu.with_memory_space_constraint(array, pltpu.HBM) for array in arrays]


IN_VMEM = pl.BlockSpec(memory_space=pltpu.VMEM)
IN_HBM = pl.BlockSpec(memory_space=pl.ANY)
IN_SMEM = pl.BlockSpec(memory_space=pltpu.SMEM)


def rotate_kernel(head_dim, heads, kept_ref, came_ref, cos_ref, sin_ref, out_ref):
    cosine, sine = cos_ref[...], sin_ref[...]
    for column in range(0, kept_ref.shape[1], head_dim):
        span = pl.ds(column, head_dim)
        part = kept_ref[:, span] + came_ref[:, span]
        if column < heads * head_dim:
            part = part * cosine + pltpu.roll(part, head_dim // 2, 1) * sine
        out_ref[:, span] = part.astype(jnp.bfloat16)


def rotary_tables(positions, head_dim):
    frequency = ROPE_BASE ** (
        -(jnp.arange(head_dim // 2, dtype=jnp.float32) * 2.0) / head_dim
    )
    angles = positions.astype(jnp.float32)[:, None] * frequency[None, :]
    cosine, sine = jnp.cos(angles), jnp.sin(angles)
    return jnp.concatenate([cosine, cosine], axis=1), jnp.concatenate([-sine, sine], axis=1)


def rotate_sums(heads, kept, came, cosine, sine):
    return pl.pallas_call(
        functools.partial(rotate_kernel, cosine.shape[1], heads),
        out_shape=pltpu.VMEM(kept.shape, jnp.bfloat16),
        in_specs=[IN_VMEM] * 4,
        out_specs=IN_VMEM,
        compiler_params=params(),
        name="rotate_sums",
    )(*in_vmem(kept, came, cosine, sine))


def join_row_kernel(index_ref, own_ref, beside_ref, out_ref):
    odd = index_ref[2]
    out_ref[odd] = own_ref[...]
    out_ref[1 - odd] = beside_ref[...]


def join_row(index, own, beside):
    return pl.pallas_call(
        join_row_kernel,
        in_specs=[IN_SMEM, IN_VMEM, IN_VMEM],
        out_specs=IN_VMEM,
        out_shape=pltpu.VMEM((2, *own.shape), own.dtype),
        compiler_params=params(),
        name="join_row",
    )(index, *in_vmem(own, beside))


def attend_kernel(head_dim, reach, index_ref, query_ref, key_seg_ref, *refs):
    row_refs, (mixed_ref, window) = refs[:-2], refs[-2:]
    rows = query_ref.shape[0]
    for place, row_ref in enumerate(row_refs):
        window[2 * place : 2 * place + 2] = row_ref[...]
    odd = index_ref[2]
    own_seg = key_seg_ref[:, pl.ds(reach * rows, rows)]
    query_seg = jnp.transpose(jnp.broadcast_to(own_seg, (rows, rows)))
    base = lax.broadcasted_iota(jnp.int32, (rows, rows), 0)
    offset = lax.broadcasted_iota(jnp.int32, (rows, rows), 1)
    allowed = []
    for piece in range(reach + 1):
        same = query_seg == key_seg_ref[:, pl.ds(piece * rows, rows)]
        if piece == reach:
            same = same & (offset <= base)
        allowed.append(same)
    for column in range(0, query_ref.shape[1], head_dim):
        span = pl.ds(column, head_dim)
        query = query_ref[:, span]
        scores = []
        for piece in range(reach + 1):
            score = lax.dot_general(
                query,
                window[odd + piece, :, :head_dim],
                (((1,), (1,)), ((), ())),
                preferred_element_type=jnp.float32,
            ) / math.sqrt(head_dim)
            scores.append(jnp.where(allowed[piece], score, -1e30))
        peak = scores[0]
        for score in scores[1:]:
            peak = jnp.maximum(peak, score)
        peak = jnp.max(peak, axis=1, keepdims=True)
        terms = [jnp.exp(score - peak) for score in scores]
        total = terms[0]
        for term in terms[1:]:
            total = total + term
        inverse = 1.0 / jnp.sum(total, axis=1, keepdims=True)
        mixed = jnp.zeros((rows, head_dim), jnp.float32)
        for piece in range(reach + 1):
            mixed += jnp.dot(
                (terms[piece] * inverse).astype(jnp.bfloat16),
                window[odd + piece, :, head_dim:],
                preferred_element_type=jnp.float32,
            )
        mixed_ref[:, span] = mixed.astype(jnp.bfloat16)


def attend(index, queries, row_windows, key_seg, head_dim):
    reach = 2 * len(row_windows) - 2
    rows = queries.shape[0]
    return pl.pallas_call(
        functools.partial(attend_kernel, head_dim, reach),
        out_shape=pltpu.VMEM(queries.shape, jnp.bfloat16),
        in_specs=[IN_SMEM] + [IN_VMEM] * (2 + len(row_windows)),
        out_specs=IN_VMEM,
        scratch_shapes=[pltpu.VMEM((reach + 2, rows, 2 * head_dim), jnp.bfloat16)],
        compiler_params=params(),
        name="attend",
    )(index, *in_vmem(queries, key_seg, *row_windows))


def lay_out_kernel(plane_ref, query_ref, key_ref, value_ref, near_out, far_out, common_out, sems):
    q_half, kv_half = near_out.shape[2], common_out.shape[2] // 2
    near = pl.ds(pl.multiple_of(plane_ref[0] * q_half, q_half), q_half)
    far = pl.ds(pl.multiple_of((1 - plane_ref[0]) * q_half, q_half), q_half)
    moves = (
        (key_ref, common_out.at[0, :, :kv_half]),
        (value_ref, common_out.at[0, :, kv_half:]),
        (query_ref.at[:, near], near_out.at[0]),
        (query_ref.at[:, far], far_out.at[0]),
    )
    copies = [
        pltpu.make_async_copy(source, target, sems.at[place])
        for place, (source, target) in enumerate(moves)
    ]
    for copy in copies:
        copy.start()
    for copy in copies:
        copy.wait()


def lay_out(plane, query, key, value):
    depth, q_half = query.shape[0], query.shape[1] // 2
    shapes = ((1, depth, q_half), (1, depth, q_half), (1, depth, 2 * key.shape[1]))
    return pl.pallas_call(
        lay_out_kernel,
        in_specs=[IN_SMEM] + [IN_HBM] * 3,
        out_specs=[IN_VMEM] * 3,
        scratch_shapes=[pltpu.SemaphoreType.DMA((4,))],
        out_shape=[pltpu.VMEM(shape, jnp.bfloat16) for shape in shapes],
        compiler_params=params(),
        name="lay_out",
    )(plane, *in_hbm(query, key, value))


def both_kernel(first_ref, second_ref, out_ref):
    out_ref[0] = first_ref[0]
    out_ref[1] = second_ref[0]


def both_of(first, second):
    return pl.pallas_call(
        both_kernel,
        in_specs=[IN_VMEM] * 2,
        out_specs=IN_VMEM,
        out_shape=pltpu.VMEM((2, *first.shape[1:]), first.dtype),
        compiler_params=params(),
        name="both_of",
    )(*in_vmem(first, second))


def first_kernel(pair_ref, out_ref):
    out_ref[...] = pair_ref[:1]


def first_of(pair):
    return pl.pallas_call(
        first_kernel,
        in_specs=[IN_VMEM],
        out_specs=IN_VMEM,
        out_shape=pltpu.VMEM((1, *pair.shape[1:]), pair.dtype),
        compiler_params=params(),
        name="first_of",
    )(*in_vmem(pair))


def project_kernel(slots, base, groups, first, last, index_ref, own_ref, other_ref, *refs):
    refs, (tokens, sems) = refs[:-2], refs[-2:]
    rows, depth = tokens.shape[1:]
    spans = [
        pl.ds(pl.multiple_of(index_ref[3 + base + place] * depth, depth), depth)
        for place in range(len(slots))
    ]
    copies = [
        pltpu.make_async_copy(own_ref.at[:, span], tokens.at[place], sems.at[place])
        for place, span in enumerate(spans)
    ]
    for copy in copies:
        copy.start()
    held_weights = groups * (1 + slots[-1][0])
    weights, refs = refs[:held_weights], refs[held_weights:]
    total_ref, refs = (None, refs) if first else (refs[0], refs[1:])
    block = rows // 2
    width = weights[0].shape[-1]
    out_ref = refs[2] if last else refs[0]
    for side in (1, 0):
        if side == 0:
            for copy in copies:
                copy.wait()
        for group in range(groups):
            columns = pl.ds(group * width, width)
            total = None if first else total_ref[side, :, columns]
            for place, (step, slot) in enumerate(slots):
                product = jnp.dot(
                    tokens[place] if side == 0 else other_ref[:, spans[place]],
                    weights[groups * step + group][slot],
                    preferred_element_type=jnp.float32,
                )
                total = product if total is None else total + product
            out_ref[side, :, columns] = total
    if last:
        kept_ref, sent_ref, held = refs
        mine = pl.ds(pl.multiple_of(index_ref[0] * block, block), block)
        others = pl.ds(pl.multiple_of((1 - index_ref[0]) * block, block), block)
        kept_ref[:block] = held[0, mine, :]
        kept_ref[block:] = held[1, mine, :]
        sent_ref[:block] = held[1, others, :]
        sent_ref[block:] = held[0, others, :]


def project(index, base, tokens, steps, total, last):
    groups = len(steps[0][1])
    slots = [(i, slot) for i, (used, _) in enumerate(steps) for slot in range(used)]
    rows = tokens[0].shape[0]
    depth = steps[0][1][0].shape[1]
    columns = sum(part.shape[2] for part in steps[0][1])
    operands = in_hbm(tokens[0]) + in_vmem(tokens[1], *(part for _, parts in steps for part in parts))
    if total is not None:
        operands += in_vmem(total)
    shapes = ((rows, columns), (rows, columns)) if last else ((2, rows, columns),)
    out = pl.pallas_call(
        functools.partial(project_kernel, slots, base, groups, total is None, last),
        in_specs=[IN_SMEM, IN_HBM] + [IN_VMEM] * (len(operands) - 1),
        out_specs=[IN_VMEM] * len(shapes),
        scratch_shapes=([pltpu.VMEM((2, rows, columns), jnp.float32)] if last else [])
        + [
            pltpu.VMEM((len(slots), rows, depth), jnp.bfloat16),
            pltpu.SemaphoreType.DMA((len(slots),)),
        ],
        out_shape=[pltpu.VMEM(shape, jnp.float32) for shape in shapes],
        compiler_params=params(),
        name="project",
    )(index, *operands)
    return out if last else out[0]


def columns_kernel(shards, base, index_ref, mixed_ref, returned_ref, *refs):
    weights = refs[:shards]
    out_ref, send_ref, held, sems = refs[-4:]
    block = mixed_ref.shape[0] // 2
    half = mixed_ref.shape[1] // 2
    width = weights[0].shape[-1]
    mine = pl.ds(pl.multiple_of(index_ref[0] * block, block), block)
    others = pl.ds(pl.multiple_of((1 - index_ref[0]) * block, block), block)
    rows_in = jnp.concatenate([mixed_ref[...], returned_ref[...]], axis=0)
    near, far = rows_in[:, :half], rows_in[:, half:]
    low = index_ref[1] == 0
    rows_in = jnp.concatenate([jnp.where(low, near, far), jnp.where(low, far, near)], axis=1)
    copies = []
    for place in range(shards):
        value = jnp.dot(rows_in, weights[place][...], preferred_element_type=jnp.float32)
        value = value.astype(jnp.bfloat16)
        columns = pl.ds(place * width, width)
        held[mine, columns] = value[:block]
        held[others, columns] = value[3 * block :]
        send_ref[mine, columns] = value[block : 2 * block]
        send_ref[others, columns] = value[2 * block : 3 * block]
        column = pl.multiple_of(index_ref[3 + base + place] * width, width)
        copy = pltpu.make_async_copy(
            held.at[:, columns], out_ref.at[:, pl.ds(column, width)], sems.at[place]
        )
        copy.start()
        copies.append(copy)
    for copy in copies:
        copy.wait()


def columns_of(index, base, mixed, returned, shards, result, width):
    rows = mixed.shape[0]
    out_cols = shards[0].shape[1]
    operands = in_vmem(mixed, returned, *shards)
    specs = [IN_SMEM] + [IN_VMEM] * len(operands)
    if result is not None:
        operands += in_hbm(result)
        specs.append(IN_HBM)
    sent = (rows, len(shards) * out_cols)
    return pl.pallas_call(
        functools.partial(columns_kernel, len(shards), base),
        in_specs=specs,
        out_specs=[IN_HBM, IN_VMEM],
        scratch_shapes=[
            pltpu.VMEM(sent, jnp.bfloat16),
            pltpu.SemaphoreType.DMA((len(shards),)),
        ],
        out_shape=[pltpu.HBM((rows, width), jnp.bfloat16), pltpu.VMEM(sent, jnp.bfloat16)],
        input_output_aliases={} if result is None else {len(operands): 0},
        compiler_params=params(),
        name="columns_of",
    )(index, *operands)


def place_kernel(width, base, index_ref, came_ref, _, out_ref, sems):
    copies = []
    for place in range(came_ref.shape[1] // width):
        column = pl.multiple_of(index_ref[base + place] * width, width)
        copy = pltpu.make_async_copy(
            came_ref.at[:, pl.ds(place * width, width)],
            out_ref.at[:, pl.ds(column, width)],
            sems.at[place],
        )
        copy.start()
        copies.append(copy)
    for copy in copies:
        copy.wait()


def place_columns(index, base, came, result, out_cols):
    return pl.pallas_call(
        functools.partial(place_kernel, out_cols, base),
        in_specs=[IN_SMEM, IN_VMEM, IN_HBM],
        out_specs=IN_HBM,
        scratch_shapes=[pltpu.SemaphoreType.DMA((came.shape[1] // out_cols,))],
        out_shape=pltpu.HBM(result.shape, result.dtype),
        input_output_aliases={2: 0},
        compiler_params=params(),
        name="place_columns",
    )(index, *in_vmem(came), *in_hbm(result))


def on_device(hidden_in, segment_ids, w_query, w_key, w_value, w_out):
    count = lax.axis_size("ctx")
    me = lax.axis_index("ctx")
    plane = lax.axis_index("dp")
    core, chip = me % 2, me // 2
    rows, width = hidden_in.shape
    block = rows // 2
    head_dim = w_key.shape[1]
    q_rows, out_cols = w_out.shape

    reach = REACH * block // rows
    pair = jnp.where(core == 0, chip, count - 1 - chip)
    pair_pos = pair * rows + jnp.arange(rows, dtype=jnp.int32)
    cosine, sine = rotary_tables(pair_pos, head_dim)
    seg_blocks = segment_ids.reshape(2 * count, block)
    seq_block = pair * 2 - 2 * reach + jnp.arange(2 * reach + 2, dtype=jnp.int32)
    clipped = jnp.maximum(seq_block, 0)
    stored = jnp.where(clipped < count, 2 * clipped, 2 * (2 * count - 1 - clipped) + 1)
    seg_rows = seg_blocks[stored]
    key_seg = jnp.where(seq_block[:, None] >= 0, seg_rows, -1).reshape(1, -1)
    tables = (cosine, sine, cosine, sine, key_seg)
    index = [core, plane, pair % 2]

    def row_windows(joined):
        sends = [(device, device ^ 2) for device in range(count)]
        own_row = join_row(index, joined, lax.ppermute(joined, "ctx", sends))
        windows = []
        for back in range(1, reach // 2 + 1):
            sends = [
                (row_device(row, column, count), row_device(row + back, column, count))
                for row in range(count // 2 - back)
                for column in range(2)
            ]
            windows.append(lax.ppermute(own_row, "ctx", sends))
        return own_row, windows

    ringed = count <= RING_LIMIT
    if ringed:
        plane_index = plane.reshape(1).astype(jnp.int32)
        pairs = ring_pairs(count // 2)
        half = count // 4
        owners = shard_owners(me, count)
        index += [*owners, *shard_owners(me ^ 1, count)]
        index = jnp.stack(index).astype(jnp.int32)

        def ring(value):
            return lax.ppermute(value, "ctx", pairs)

        def add_projections(total, steps, begin, end, last=False):
            base = 0 if begin == 0 else 2 * begin - 1
            return project(index, base, (hidden_in, other), steps[begin:end], total, last)

        own_near, own_far, own_common = lay_out(plane_index, w_query, w_key, w_value)
        common = both_of(own_common, core_swap(own_common, count))
        common_steps = [(1, (own_common,))]
        steps = [(1, (own_near, own_far))]
        near = None
        for step in range(1, half + 1):
            if step == 2:
                common, index, *tables = lax.optimization_barrier((common, index, *tables))
                near = both_of(own_near, core_swap(after(own_near, common), count))
                other = core_swap(after(hidden_in, near), count)
                out_second = core_swap(after(w_out, near), count)
            if step == half:
                common = first_of(common)
            common = ring(common)
            common_steps.append((common.shape[0], (common,)))
            if step > 1:
                if step > 3:
                    near = after(near, steps[step - 3][1][1])
                near = ring(after(near, *common_steps[step - 1][1]))
                steps.append((2, (near, plane_swap(near))))
        cosine, sine, query_cosine, query_sine, key_seg = tables

        total = add_projections(None, common_steps, 0, 3)
        kept, sent = add_projections(total, common_steps, 3, half + 1, True)
        joined = rotate_sums(1, kept, core_swap(sent, count), cosine, sine)
        own_row, windows = row_windows(joined)

        near = first_of(after(near, common, steps[half - 2][1][1]))
        near = ring(near)
        steps.append((1, (near, plane_swap(near))))
        held = [after(w_out, *common_steps[half][1]), after(out_second, near)]
        shards = [w_out]
        waits = {3: (joined, steps[half - 1][1][1]), 4: (own_row,), 5: (*windows, steps[half][1][1])}
        for step in range(1, 2 * half):
            turn = (step - 1) % 2
            held[turn] = ring(after(held[turn], *waits.get(step, ())))
            shards.append(held[turn])
        total = add_projections(None, steps, 0, 2)
        total = add_projections(total, steps, 2, 3)
        total = add_projections(total, steps, 3, 4)
        kept, sent = add_projections(total, steps, 4, 5, True)
        queries = rotate_sums(
            q_rows // head_dim, kept, core_swap(sent, count), query_cosine, query_sine
        )
        queries = after(queries, shards[5])
    else:
        index = jnp.stack(index).astype(jnp.int32)
        cosine, sine, query_cosine, query_sine, key_seg = tables
        gathered = lax.all_gather(
            jnp.concatenate([w_key, w_value, w_query], axis=1), "ctx", axis=0, tiled=True
        )
        ordered = jnp.where(core == 0, hidden_in, jnp.roll(hidden_in, block, axis=0))
        pair_tokens = jnp.concatenate([ordered[:block], core_swap(ordered[block:], count)], axis=0)
        sums = jnp.dot(pair_tokens, gathered, preferred_element_type=jnp.float32)
        kv_sums, query_sums = sums[:, : 2 * head_dim], sums[:, 2 * head_dim :]
        joined = rotate_sums(1, kv_sums, jnp.zeros_like(kv_sums), cosine, sine)
        queries = rotate_sums(
            q_rows // head_dim, query_sums, jnp.zeros_like(query_sums), query_cosine, query_sine
        )
        own_row, windows = row_windows(joined)

    mixed = attend(index, queries, [*windows[::-1], own_row], key_seg, head_dim)

    returned = core_swap(mixed, count)
    if not ringed:
        kinds = (mixed[:block], returned[block:])
        own_rows = jnp.where(
            core == 0, jnp.concatenate(kinds, axis=0), jnp.concatenate(kinds[::-1], axis=0)
        )
        gathered = lax.all_gather(w_out, "ctx", axis=1, tiled=True)
        return jnp.dot(own_rows, gathered, preferred_element_type=jnp.float32).astype(jnp.bfloat16)

    arrivals = []
    result = None
    for begin, end in ((0, 5), (5, len(shards))):
        result, sent = columns_of(index, begin, mixed, returned, shards[begin:end], result, width)
        arrivals.append((3 + len(shards) + begin, core_swap(sent, count)))
    for base, came in arrivals:
        result = place_columns(index, base, came, result, out_cols)
    return result


def solution(mesh):
    in_specs = (
        P(("dp", "ctx"), None),
        P("dp"),
        P("ctx", None),
        P("ctx", None),
        P("ctx", None),
        P(None, "ctx"),
    )
    out_specs = P(("dp", "ctx"), None)
    return jax.shard_map(
        on_device, mesh=mesh, in_specs=in_specs, out_specs=out_specs, check_vma=False
    )
```

```python
import functools
import math

import jax
import jax.numpy as jnp
from jax import lax
from jax.experimental import pallas as pl
from jax.experimental.pallas import tpu as pltpu
from jax.sharding import PartitionSpec as P

REACH = 8
ROPE_BASE = 500000.0
RING_LIMIT = 16
VMEM_LIMIT = 16 * 1024 * 1024
HALVED = True
PLAN = (
    "first0",
    "near0",
    "near1",
    "common0",
    "tables0",
    "second0 near1",
    "tokens0 near1 common0",
    "other0",
    "near2",
    "common1 near1",
    "far1",
    "first1 near2",
    "near3",
    "common2 near2 far1",
    "far2",
    "second1 near3",
    "cross1",
    "queries1 first1",
    "near4 far2",
    "common3 near3 far2 queries1",
    "far3",
    "first2 near4",
    "queries2 second1",
    "common4 near4 queries2",
    "keys1",
    "far4",
    "keys2 first2",
    "second2 near4",
    "cross2 far4",
    "first3 common4",
    "second3 common4",
    "keys3",
    "queries3",
    "queries4 first3",
    "row0 second3",
    "row1",
    "row2",
    "cross3",
    "first4 row0",
    "mixed0",
    "mixed1",
    "columns0",
    "place0",
    "columns1",
    "place1",
)
MICROS = {}
PROJECTIONS = {
    "keys1": (0, 2, False),
    "keys2": (2, 4, False),
    "keys3": (4, 5, True),
    "queries1": (0, 2, False),
    "queries2": (2, 3, False),
    "queries3": (3, 4, False),
    "queries4": (4, 5, True),
}
COLUMNS = {"columns0": (0, 5), "columns1": (5, 8)}


def chip_at(place, chips):
    place = place % chips
    return jnp.where(place < chips // 2, 2 * place, 2 * (chips - 1 - place) + 1)


def static_chip_at(place, chips):
    place %= chips
    return 2 * place if place < chips // 2 else 2 * (chips - 1 - place) + 1


def ring_pairs(chips):
    pairs = []
    for place in range(chips):
        here = static_chip_at(place, chips)
        pairs.append((2 * here, 2 * static_chip_at(place + 1, chips)))
        pairs.append((2 * here + 1, 2 * static_chip_at(place - 1, chips) + 1))
    return pairs


def core_swap(value, count):
    return lax.ppermute(value, "ctx", [(i, i ^ 1) for i in range(count)])


def plane_swap(value):
    return lax.ppermute(value, "dp", [(0, 1), (1, 0)])


def row_device(row, column, count):
    pair = 2 * row + (column if row < count // 4 else 1 - column)
    return 2 * pair if pair < count // 2 else 2 * (count - 1 - pair) + 1


def after(value, *others):
    return lax.optimization_barrier((value, *others))[0]


def shard_owners(me, count):
    chips = count // 2
    half = chips // 2
    core, chip = me % 2, me // 2
    place = jnp.where(chip % 2 == 0, chip // 2, chips - 1 - chip // 2)
    way = jnp.where(core == 0, -1, 1)
    owners = [me]
    for step in range(1, half + 1):
        source = chip_at(place + way * step + chips, chips)
        owners.append(2 * source + core)
        if step < half:
            owners.append(2 * source + 1 - core)
    return owners


def params(**settings):
    return pltpu.CompilerParams(vmem_limit_bytes=VMEM_LIMIT, **settings)


def in_vmem(*arrays):
    return [pltpu.with_memory_space_constraint(array, pltpu.VMEM) for array in arrays]


def in_hbm(*arrays):
    return [pltpu.with_memory_space_constraint(array, pltpu.HBM) for array in arrays]


def estimate(micros):
    return pl.CostEstimate(flops=int(micros * 1.1535e9), bytes_accessed=0, transcendentals=0)


IN_VMEM = pl.BlockSpec(memory_space=pltpu.VMEM)
IN_HBM = pl.BlockSpec(memory_space=pl.ANY)
IN_SMEM = pl.BlockSpec(memory_space=pltpu.SMEM)


def rotate_kernel(head_dim, heads, kept_ref, came_ref, cos_ref, sin_ref, out_ref):
    cosine, sine = cos_ref[...], sin_ref[...]
    for column in range(0, kept_ref.shape[1], head_dim):
        span = pl.ds(column, head_dim)
        part = kept_ref[:, span] + came_ref[:, span]
        if column < heads * head_dim:
            part = part * cosine + pltpu.roll(part, head_dim // 2, 1) * sine
        out_ref[:, span] = part.astype(jnp.bfloat16)


def rotary_tables(positions, head_dim):
    frequency = ROPE_BASE ** (
        -(jnp.arange(head_dim // 2, dtype=jnp.float32) * 2.0) / head_dim
    )
    angles = positions.astype(jnp.float32)[:, None] * frequency[None, :]
    cosine, sine = jnp.cos(angles), jnp.sin(angles)
    return jnp.concatenate([cosine, cosine], axis=1), jnp.concatenate([-sine, sine], axis=1)


def rotate_sums(heads, kept, came, cosine, sine):
    return pl.pallas_call(
        functools.partial(rotate_kernel, cosine.shape[1], heads),
        out_shape=pltpu.VMEM(kept.shape, jnp.bfloat16),
        in_specs=[IN_VMEM] * 4,
        out_specs=IN_VMEM,
        compiler_params=params(),
        name="rotate_sums",
    )(*in_vmem(kept, came, cosine, sine))


def join_row_kernel(index_ref, own_ref, beside_ref, out_ref):
    odd = index_ref[2]
    out_ref[odd] = own_ref[...]
    out_ref[1 - odd] = beside_ref[...]


def join_row(index, own, beside):
    return pl.pallas_call(
        join_row_kernel,
        in_specs=[IN_SMEM, IN_VMEM, IN_VMEM],
        out_specs=IN_VMEM,
        out_shape=pltpu.VMEM((2, *own.shape), own.dtype),
        compiler_params=params(),
        name="join_row",
    )(index, *in_vmem(own, beside))


def attend_kernel(head_dim, reach, index_ref, query_ref, key_seg_ref, *refs):
    row_refs, (mixed_ref, window) = refs[:-2], refs[-2:]
    rows = query_ref.shape[0]
    for place, row_ref in enumerate(row_refs):
        window[2 * place : 2 * place + 2] = row_ref[...]
    odd = index_ref[2]
    own_seg = key_seg_ref[:, pl.ds(reach * rows, rows)]
    query_seg = jnp.transpose(jnp.broadcast_to(own_seg, (rows, rows)))
    base = lax.broadcasted_iota(jnp.int32, (rows, rows), 0)
    offset = lax.broadcasted_iota(jnp.int32, (rows, rows), 1)
    allowed = []
    for piece in range(reach + 1):
        same = query_seg == key_seg_ref[:, pl.ds(piece * rows, rows)]
        if piece == reach:
            same = same & (offset <= base)
        allowed.append(same)
    for column in range(0, query_ref.shape[1], head_dim):
        span = pl.ds(column, head_dim)
        query = query_ref[:, span]
        scores = []
        for piece in range(reach + 1):
            score = lax.dot_general(
                query,
                window[odd + piece, :, :head_dim],
                (((1,), (1,)), ((), ())),
                preferred_element_type=jnp.float32,
            ) / math.sqrt(head_dim)
            scores.append(jnp.where(allowed[piece], score, -1e30))
        peak = scores[0]
        for score in scores[1:]:
            peak = jnp.maximum(peak, score)
        peak = jnp.max(peak, axis=1, keepdims=True)
        terms = [jnp.exp(score - peak) for score in scores]
        total = terms[0]
        for term in terms[1:]:
            total = total + term
        inverse = 1.0 / jnp.sum(total, axis=1, keepdims=True)
        mixed = jnp.zeros((rows, head_dim), jnp.float32)
        for piece in range(reach + 1):
            mixed += jnp.dot(
                (terms[piece] * inverse).astype(jnp.bfloat16),
                window[odd + piece, :, head_dim:],
                preferred_element_type=jnp.float32,
            )
        mixed_ref[:, span] = mixed.astype(jnp.bfloat16)


def attend(index, queries, row_windows, key_seg, head_dim, micros):
    reach = 2 * len(row_windows) - 2
    rows = queries.shape[0]
    return pl.pallas_call(
        functools.partial(attend_kernel, head_dim, reach),
        out_shape=pltpu.VMEM(queries.shape, jnp.bfloat16),
        in_specs=[IN_SMEM] + [IN_VMEM] * (2 + len(row_windows)),
        out_specs=IN_VMEM,
        scratch_shapes=[pltpu.VMEM((reach + 2, rows, 2 * head_dim), jnp.bfloat16)],
        compiler_params=params(),
        cost_estimate=estimate(micros),
        name="attend",
    )(index, *in_vmem(queries, key_seg, *row_windows))


def lay_out_kernel(plane_ref, query_ref, key_ref, value_ref, near_out, far_out, common_out, sems):
    q_half, kv_half = near_out.shape[2], common_out.shape[2] // 2
    near = pl.ds(pl.multiple_of(plane_ref[0] * q_half, q_half), q_half)
    far = pl.ds(pl.multiple_of((1 - plane_ref[0]) * q_half, q_half), q_half)
    moves = (
        (key_ref, common_out.at[0, :, :kv_half]),
        (value_ref, common_out.at[0, :, kv_half:]),
        (query_ref.at[:, near], near_out.at[0]),
        (query_ref.at[:, far], far_out.at[0]),
    )
    copies = [
        pltpu.make_async_copy(source, target, sems.at[place])
        for place, (source, target) in enumerate(moves)
    ]
    for copy in copies:
        copy.start()
    for copy in copies:
        copy.wait()


def lay_out(plane, query, key, value):
    depth, q_half = query.shape[0], query.shape[1] // 2
    shapes = ((1, depth, q_half), (1, depth, q_half), (1, depth, 2 * key.shape[1]))
    return pl.pallas_call(
        lay_out_kernel,
        in_specs=[IN_SMEM] + [IN_HBM] * 3,
        out_specs=[IN_VMEM] * 3,
        scratch_shapes=[pltpu.SemaphoreType.DMA((4,))],
        out_shape=[pltpu.VMEM(shape, jnp.bfloat16) for shape in shapes],
        compiler_params=params(),
        name="lay_out",
    )(plane, *in_hbm(query, key, value))


def rows_near_kernel(plane_ref, weight_ref, out_ref, sem):
    half = out_ref.shape[0]
    near = pl.ds(pl.multiple_of(plane_ref[0] * half, half), half)
    copy = pltpu.make_async_copy(weight_ref.at[near, :], out_ref, sem)
    copy.start()
    copy.wait()


def rows_near_of(plane, weight):
    rows, columns = weight.shape
    return pl.pallas_call(
        rows_near_kernel,
        in_specs=[IN_SMEM, IN_HBM],
        out_specs=IN_VMEM,
        scratch_shapes=[pltpu.SemaphoreType.DMA],
        out_shape=pltpu.VMEM((rows // 2, columns), weight.dtype),
        compiler_params=params(),
        name="rows_near",
    )(plane, *in_hbm(weight))


def both_kernel(first_ref, second_ref, out_ref):
    out_ref[0] = first_ref[0]
    out_ref[1] = second_ref[0]


def both_of(first, second):
    return pl.pallas_call(
        both_kernel,
        in_specs=[IN_VMEM] * 2,
        out_specs=IN_VMEM,
        out_shape=pltpu.VMEM((2, *first.shape[1:]), first.dtype),
        compiler_params=params(),
        name="both_of",
    )(*in_vmem(first, second))


def first_kernel(pair_ref, out_ref):
    out_ref[...] = pair_ref[:1]


def first_of(pair):
    return pl.pallas_call(
        first_kernel,
        in_specs=[IN_VMEM],
        out_specs=IN_VMEM,
        out_shape=pltpu.VMEM((1, *pair.shape[1:]), pair.dtype),
        compiler_params=params(),
        name="first_of",
    )(*in_vmem(pair))


def bring_kernel(source_ref, out_ref, sem):
    copy = pltpu.make_async_copy(source_ref, out_ref, sem)
    copy.start()
    copy.wait()


def bring(tokens, micros):
    return pl.pallas_call(
        bring_kernel,
        in_specs=[IN_HBM],
        out_specs=IN_VMEM,
        scratch_shapes=[pltpu.SemaphoreType.DMA],
        out_shape=pltpu.VMEM(tokens.shape, tokens.dtype),
        compiler_params=params(),
        cost_estimate=estimate(micros),
        name="bring",
    )(*in_hbm(tokens))


def project_kernel(slots, base, groups, first, last, index_ref, own_ref, other_ref, *refs):
    held_weights = groups * (1 + slots[-1][0])
    weights, refs = refs[:held_weights], refs[held_weights:]
    total_ref, refs = (None, refs) if first else (refs[0], refs[1:])
    rows = own_ref.shape[0]
    depth, width = weights[0].shape[-2:]
    block = rows // 2
    spans = [
        pl.ds(pl.multiple_of(index_ref[3 + base + place] * depth, depth), depth)
        for place in range(len(slots))
    ]
    out_ref = refs[2] if last else refs[0]
    for side, source_ref in enumerate((own_ref, other_ref)):
        for group in range(groups):
            columns = pl.ds(group * width, width)
            total = None if first else total_ref[side, :, columns]
            for place, (step, slot) in enumerate(slots):
                product = jnp.dot(
                    source_ref[:, spans[place]],
                    weights[groups * step + group][slot],
                    preferred_element_type=jnp.float32,
                )
                total = product if total is None else total + product
            out_ref[side, :, columns] = total
    if last:
        kept_ref, sent_ref, held = refs
        mine = pl.ds(pl.multiple_of(index_ref[0] * block, block), block)
        others = pl.ds(pl.multiple_of((1 - index_ref[0]) * block, block), block)
        kept_ref[:block] = held[0, mine, :]
        kept_ref[block:] = held[1, mine, :]
        sent_ref[:block] = held[1, others, :]
        sent_ref[block:] = held[0, others, :]


def project(index, base, tokens, steps, total, last, micros):
    groups = len(steps[0][1])
    slots = [(i, slot) for i, (used, _) in enumerate(steps) for slot in range(used)]
    rows = tokens[0].shape[0]
    columns = sum(part.shape[2] for part in steps[0][1])
    operands = in_vmem(*tokens, *(part for _, parts in steps for part in parts))
    if total is not None:
        operands += in_vmem(total)
    shapes = ((rows, columns), (rows, columns)) if last else ((2, rows, columns),)
    out = pl.pallas_call(
        functools.partial(project_kernel, slots, base, groups, total is None, last),
        in_specs=[IN_SMEM] + [IN_VMEM] * len(operands),
        out_specs=[IN_VMEM] * len(shapes),
        scratch_shapes=[pltpu.VMEM((2, rows, columns), jnp.float32)] if last else [],
        out_shape=[pltpu.VMEM(shape, jnp.float32) for shape in shapes],
        compiler_params=params(),
        cost_estimate=estimate(micros),
        name="project",
    )(index, *operands)
    return out if last else out[0]


def columns_kernel(places, base, index_ref, mixed_ref, returned_ref, *refs):
    weights = list(refs[: sum(places)])
    out_ref, send_ref, held, sems = refs[-4:]
    block = mixed_ref.shape[0] // 2
    half = mixed_ref.shape[1] // 2
    width = weights[0].shape[-1]
    mine = pl.ds(pl.multiple_of(index_ref[0] * block, block), block)
    others = pl.ds(pl.multiple_of((1 - index_ref[0]) * block, block), block)
    near = pl.ds(pl.multiple_of(index_ref[1] * half, half), half)
    far = pl.ds(pl.multiple_of((1 - index_ref[1]) * half, half), half)
    rows_in = jnp.concatenate([mixed_ref[...], returned_ref[...]], axis=0)
    copies = []
    for place, parts in enumerate(places):
        if parts == 1:
            whole = weights.pop(0)
            low, high = whole[near, :], whole[far, :]
        else:
            low, high = weights.pop(0)[...], weights.pop(0)[...]
        weight = jnp.concatenate([low, high], axis=0)
        value = jnp.dot(rows_in, weight, preferred_element_type=jnp.float32)
        value = value.astype(jnp.bfloat16)
        columns = pl.ds(place * width, width)
        held[mine, columns] = value[:block]
        held[others, columns] = value[3 * block :]
        send_ref[mine, columns] = value[block : 2 * block]
        send_ref[others, columns] = value[2 * block : 3 * block]
        column = pl.multiple_of(index_ref[3 + base + place] * width, width)
        copy = pltpu.make_async_copy(
            held.at[:, columns], out_ref.at[:, pl.ds(column, width)], sems.at[place]
        )
        copy.start()
        copies.append(copy)
    for copy in copies:
        copy.wait()


def columns_of(index, base, mixed, returned, shards, result, width, micros):
    rows = mixed.shape[0]
    out_cols = shards[0][0].shape[-1]
    operands = in_vmem(mixed, returned, *(part for shard in shards for part in shard))
    specs = [IN_SMEM] + [IN_VMEM] * len(operands)
    if result is not None:
        operands += in_hbm(result)
        specs.append(IN_HBM)
    sent = (rows, len(shards) * out_cols)
    return pl.pallas_call(
        functools.partial(columns_kernel, [len(shard) for shard in shards], base),
        in_specs=specs,
        out_specs=[IN_HBM, IN_VMEM],
        scratch_shapes=[
            pltpu.VMEM(sent, jnp.bfloat16),
            pltpu.SemaphoreType.DMA((len(shards),)),
        ],
        out_shape=[pltpu.HBM((rows, width), jnp.bfloat16), pltpu.VMEM(sent, jnp.bfloat16)],
        input_output_aliases={} if result is None else {len(operands): 0},
        compiler_params=params(),
        cost_estimate=estimate(micros),
        name="columns_of",
    )(index, *operands)


def place_kernel(width, base, index_ref, came_ref, _, out_ref, sems):
    copies = []
    for place in range(came_ref.shape[1] // width):
        column = pl.multiple_of(index_ref[base + place] * width, width)
        copy = pltpu.make_async_copy(
            came_ref.at[:, pl.ds(place * width, width)],
            out_ref.at[:, pl.ds(column, width)],
            sems.at[place],
        )
        copy.start()
        copies.append(copy)
    for copy in copies:
        copy.wait()


def place_columns(index, base, came, result, out_cols):
    return pl.pallas_call(
        functools.partial(place_kernel, out_cols, base),
        in_specs=[IN_SMEM, IN_VMEM, IN_HBM],
        out_specs=IN_HBM,
        scratch_shapes=[pltpu.SemaphoreType.DMA((came.shape[1] // out_cols,))],
        out_shape=pltpu.HBM(result.shape, result.dtype),
        input_output_aliases={2: 0},
        compiler_params=params(),
        name="place_columns",
    )(index, *in_vmem(came), *in_hbm(result))


def on_device(hidden_in, segment_ids, w_query, w_key, w_value, w_out):
    count = lax.axis_size("ctx")
    me = lax.axis_index("ctx")
    plane = lax.axis_index("dp")
    core, chip = me % 2, me // 2
    rows, width = hidden_in.shape
    block = rows // 2
    head_dim = w_key.shape[1]
    q_rows, out_cols = w_out.shape

    reach = REACH * block // rows
    pair = jnp.where(core == 0, chip, count - 1 - chip)
    pair_pos = pair * rows + jnp.arange(rows, dtype=jnp.int32)
    cosine, sine = rotary_tables(pair_pos, head_dim)
    seg_blocks = segment_ids.reshape(2 * count, block)
    seq_block = pair * 2 - 2 * reach + jnp.arange(2 * reach + 2, dtype=jnp.int32)
    clipped = jnp.maximum(seq_block, 0)
    stored = jnp.where(clipped < count, 2 * clipped, 2 * (2 * count - 1 - clipped) + 1)
    seg_rows = seg_blocks[stored]
    key_seg = jnp.where(seq_block[:, None] >= 0, seg_rows, -1).reshape(1, -1)
    tables = (cosine, sine, cosine, sine, key_seg)
    index = [core, plane, pair % 2]

    def row_windows(joined):
        sends = [(device, device ^ 2) for device in range(count)]
        own_row = join_row(index, joined, lax.ppermute(joined, "ctx", sends))
        windows = []
        for back in range(1, reach // 2 + 1):
            sends = [
                (row_device(row, column, count), row_device(row + back, column, count))
                for row in range(count // 2 - back)
                for column in range(2)
            ]
            windows.append(lax.ppermute(own_row, "ctx", sends))
        return own_row, windows

    ringed = count <= RING_LIMIT
    if ringed:
        plane_index = plane.reshape(1).astype(jnp.int32)
        pairs = ring_pairs(count // 2)
        half = count // 4
        owners = shard_owners(me, count)
        index += [*owners, *shard_owners(me ^ 1, count)]
        index = jnp.stack(index).astype(jnp.int32)

        def ring(value):
            return lax.ppermute(value, "ctx", pairs)

        def add_projections(total, steps, begin, end, last=False):
            base = 0 if begin == 0 else 2 * begin - 1
            return project(index, base, (hidden_in, other), steps[begin:end], total, last)

        own_near, own_far, own_common = lay_out(plane_index, w_query, w_key, w_value)
        done = {"w_out": w_out}
        common_steps = [(1, (own_common,))]
        query_steps = [(1, (own_near, own_far))]
        sent_sums = {}
        outputs = {}

        def run(name, *ties):
            nonlocal index, cosine, sine, query_cosine, query_sine, key_seg

            def tied(value):
                return after(value, *(done[tie] for tie in ties)) if ties else value

            kind, step = name[:-1], int(name[-1])
            micros = MICROS.get(kind, 2)
            if name == "tables0":
                first, index, cosine, sine, query_cosine, query_sine, key_seg = (
                    lax.optimization_barrier(
                        (done["common0"], index, cosine, sine, query_cosine, query_sine, key_seg)
                    )
                )
                done["common0"] = value = first
            elif name == "common0":
                value = both_of(own_common, core_swap(tied(own_common), count))
            elif name == "near0":
                value = both_of(own_near, core_swap(tied(own_near), count))
            elif name == "other0":
                value = core_swap(tied(done["tokens0"]), count)
            elif name == "tokens0":
                value = bring(tied(hidden_in), micros)
            elif name == "second0":
                rows_near = w_out
                if HALVED:
                    rows_near = own_rows_near
                value = core_swap(tied(rows_near), count)
            elif name == "first0":
                value = w_out
            elif kind in ("common", "near"):
                value = done[f"{kind}{step - 1}"]
                value = ring(tied(first_of(value) if step == half else value))
                if kind == "common":
                    common_steps.append((value.shape[0], (value,)))
            elif kind == "far":
                near = done[f"near{step}"]
                value = plane_swap(tied(near))
                query_steps.append((near.shape[0], (near, value)))
            elif kind in ("first", "second"):
                value = ring(tied(done[f"{kind}{step - 1}"]))
            elif kind == "cross":
                value = plane_swap(tied(done[f"second{step}"]))
            elif kind in ("keys", "queries"):
                begin, end, last = PROJECTIONS[name]
                steps = list(common_steps if kind == "keys" else query_steps)
                if ties:
                    used, parts = steps[begin]
                    steps[begin] = (used, (tied(parts[0]), *parts[1:]))
                value = project(
                    index,
                    0 if begin == 0 else 2 * begin - 1,
                    (done["tokens0"], done["other0"]),
                    steps[begin:end],
                    done.get(f"{kind}{step - 1}"),
                    last,
                    micros,
                )
                if last:
                    kept, sent = value
                    came = core_swap(sent, count)
                    if kind == "keys":
                        value = rotate_sums(1, kept, came, cosine, sine)
                    else:
                        value = rotate_sums(
                            q_rows // head_dim, kept, came, query_cosine, query_sine
                        )
            elif name == "row0":
                sends = [(device, device ^ 2) for device in range(count)]
                joined = done["keys3"]
                value = join_row(index, joined, lax.ppermute(tied(joined), "ctx", sends))
            elif kind == "row":
                sends = [
                    (row_device(row, column, count), row_device(row + step, column, count))
                    for row in range(count // 2 - step)
                    for column in range(2)
                ]
                value = lax.ppermute(tied(done["row0"]), "ctx", sends)
            elif name == "mixed0":
                windows = [done["row2"], done["row1"], done["row0"]]
                value = attend(index, tied(done["queries4"]), windows, key_seg, head_dim, micros)
            elif name == "mixed1":
                value = core_swap(done["mixed0"], count)
            elif kind == "columns":
                begin, end = COLUMNS[name]
                shards = [(w_out,)]
                for turn in range(1, half + 1):
                    if f"first{turn}" in done:
                        shards.append((done[f"first{turn}"],))
                    if f"second{turn}" in done:
                        pair = (done[f"second{turn}"],)
                        if HALVED:
                            pair += (done[f"cross{turn}"],)
                        shards.append(pair)
                result, sent = columns_of(
                    index,
                    begin,
                    done["mixed0"],
                    tied(done["mixed1"]),
                    shards[begin:end],
                    outputs.get("result"),
                    width,
                    micros,
                )
                outputs["result"] = result
                value = core_swap(sent, count)
            elif kind == "place":
                begin, _ = COLUMNS[f"columns{step}"]
                value = place_columns(
                    index, 3 + 2 * half + begin, done[f"columns{step}"], outputs["result"], out_cols
                )
                outputs["result"] = value
            done[name] = value

        own_rows_near = None
        cosine, sine, query_cosine, query_sine, key_seg = tables
        if HALVED:
            own_rows_near = rows_near_of(plane_index, w_out)
        for entry in PLAN:
            run(*entry.split())
        return outputs["result"]
    else:
        index = jnp.stack(index).astype(jnp.int32)
        cosine, sine, query_cosine, query_sine, key_seg = tables
        gathered = lax.all_gather(
            jnp.concatenate([w_key, w_value, w_query], axis=1), "ctx", axis=0, tiled=True
        )
        ordered = jnp.where(core == 0, hidden_in, jnp.roll(hidden_in, block, axis=0))
        pair_tokens = jnp.concatenate([ordered[:block], core_swap(ordered[block:], count)], axis=0)
        sums = jnp.dot(pair_tokens, gathered, preferred_element_type=jnp.float32)
        kv_sums, query_sums = sums[:, : 2 * head_dim], sums[:, 2 * head_dim :]
        joined = rotate_sums(1, kv_sums, jnp.zeros_like(kv_sums), cosine, sine)
        queries = rotate_sums(
            q_rows // head_dim, query_sums, jnp.zeros_like(query_sums), query_cosine, query_sine
        )
        own_row, windows = row_windows(joined)

    mixed = attend(index, queries, [*windows[::-1], own_row], key_seg, head_dim, 4)
    returned = core_swap(mixed, count)
    kinds = (mixed[:block], returned[block:])
    own_rows = jnp.where(
        core == 0, jnp.concatenate(kinds, axis=0), jnp.concatenate(kinds[::-1], axis=0)
    )
    gathered = lax.all_gather(w_out, "ctx", axis=1, tiled=True)
    return jnp.dot(own_rows, gathered, preferred_element_type=jnp.float32).astype(jnp.bfloat16)


def solution(mesh):
    in_specs = (
        P(("dp", "ctx"), None),
        P("dp"),
        P("ctx", None),
        P("ctx", None),
        P("ctx", None),
        P(None, "ctx"),
    )
    out_specs = P(("dp", "ctx"), None)
    return jax.shard_map(
        on_device, mesh=mesh, in_specs=in_specs, out_specs=out_specs, check_vma=False
    )
```

```python
import functools
import math

import jax
import jax.numpy as jnp
from jax import lax
from jax.experimental import pallas as pl
from jax.experimental.pallas import tpu as pltpu
from jax.sharding import PartitionSpec as P

REACH = 8
ROPE_BASE = 500000.0
RING_LIMIT = 16
VMEM_LIMIT = 16 * 1024 * 1024
HALVED = True
PLAN = (
    "first0",
    "near0",
    "near1",
    "common0",
    "tables0",
    "second0 near1",
    "tokens0 near1 common0",
    "other0",
    "near2",
    "common1 near1",
    "far1",
    "first1 near2",
    "near3",
    "common2 near2 far1",
    "far2",
    "second1 near3",
    "cross1",
    "queries1 first1",
    "near4 far2",
    "common3 near3 far2 queries1",
    "far3",
    "first2 near4",
    "queries2 second1",
    "common4 near4 queries2 far3",
    "keys1",
    "far4",
    "keys2 first2",
    "second2 near4",
    "cross2 far4",
    "first3 common4",
    "second3 common4",
    "keys3 cross1",
    "queries3",
    "queries4 first3",
    "row0 second3 cross2",
    "row1",
    "row2",
    "cross3",
    "first4 row0 row1",
    "mixed0 cross3",
    "mixed1",
    "columns0 first4",
    "columns1",
    "place0",
    "place1",
)
MICROS = {}
PROJECTIONS = {
    "keys1": (0, 2, False),
    "keys2": (2, 4, False),
    "keys3": (4, 5, True),
    "queries1": (0, 2, False),
    "queries2": (2, 3, False),
    "queries3": (3, 4, False),
    "queries4": (4, 5, True),
}
COLUMNS = {"columns0": (0, 5), "columns1": (5, 8)}


def chip_at(place, chips):
    place = place % chips
    return jnp.where(place < chips // 2, 2 * place, 2 * (chips - 1 - place) + 1)


def static_chip_at(place, chips):
    place %= chips
    return 2 * place if place < chips // 2 else 2 * (chips - 1 - place) + 1


def ring_pairs(chips):
    pairs = []
    for place in range(chips):
        here = static_chip_at(place, chips)
        pairs.append((2 * here, 2 * static_chip_at(place + 1, chips)))
        pairs.append((2 * here + 1, 2 * static_chip_at(place - 1, chips) + 1))
    return pairs


def core_swap(value, count):
    return lax.ppermute(value, "ctx", [(i, i ^ 1) for i in range(count)])


def plane_swap(value):
    return lax.ppermute(value, "dp", [(0, 1), (1, 0)])


def row_device(row, column, count):
    pair = 2 * row + (column if row < count // 4 else 1 - column)
    return 2 * pair if pair < count // 2 else 2 * (count - 1 - pair) + 1


def after(value, *others):
    return lax.optimization_barrier((value, *others))[0]


def shard_owners(me, count):
    chips = count // 2
    half = chips // 2
    core, chip = me % 2, me // 2
    place = jnp.where(chip % 2 == 0, chip // 2, chips - 1 - chip // 2)
    way = jnp.where(core == 0, -1, 1)
    owners = [me]
    for step in range(1, half + 1):
        source = chip_at(place + way * step + chips, chips)
        owners.append(2 * source + core)
        if step < half:
            owners.append(2 * source + 1 - core)
    return owners


def params(**settings):
    return pltpu.CompilerParams(vmem_limit_bytes=VMEM_LIMIT, **settings)


def in_vmem(*arrays):
    return [pltpu.with_memory_space_constraint(array, pltpu.VMEM) for array in arrays]


def in_hbm(*arrays):
    return [pltpu.with_memory_space_constraint(array, pltpu.HBM) for array in arrays]


def estimate(micros):
    return pl.CostEstimate(flops=int(micros * 1.1535e9), bytes_accessed=0, transcendentals=0)


IN_VMEM = pl.BlockSpec(memory_space=pltpu.VMEM)
IN_HBM = pl.BlockSpec(memory_space=pl.ANY)
IN_SMEM = pl.BlockSpec(memory_space=pltpu.SMEM)


def rotate_kernel(head_dim, heads, kept_ref, came_ref, cos_ref, sin_ref, out_ref):
    cosine, sine = cos_ref[...], sin_ref[...]
    for column in range(0, kept_ref.shape[1], head_dim):
        span = pl.ds(column, head_dim)
        part = kept_ref[:, span] + came_ref[:, span]
        if column < heads * head_dim:
            part = part * cosine + pltpu.roll(part, head_dim // 2, 1) * sine
        out_ref[:, span] = part.astype(jnp.bfloat16)


def rotary_tables(positions, head_dim):
    frequency = ROPE_BASE ** (
        -(jnp.arange(head_dim // 2, dtype=jnp.float32) * 2.0) / head_dim
    )
    angles = positions.astype(jnp.float32)[:, None] * frequency[None, :]
    cosine, sine = jnp.cos(angles), jnp.sin(angles)
    return jnp.concatenate([cosine, cosine], axis=1), jnp.concatenate([-sine, sine], axis=1)


def rotate_sums(heads, kept, came, cosine, sine):
    return pl.pallas_call(
        functools.partial(rotate_kernel, cosine.shape[1], heads),
        out_shape=pltpu.VMEM(kept.shape, jnp.bfloat16),
        in_specs=[IN_VMEM] * 4,
        out_specs=IN_VMEM,
        compiler_params=params(),
        name="rotate_sums",
    )(*in_vmem(kept, came, cosine, sine))


def join_row_kernel(index_ref, own_ref, beside_ref, out_ref):
    odd = index_ref[2]
    out_ref[odd] = own_ref[...]
    out_ref[1 - odd] = beside_ref[...]


def join_row(index, own, beside):
    return pl.pallas_call(
        join_row_kernel,
        in_specs=[IN_SMEM, IN_VMEM, IN_VMEM],
        out_specs=IN_VMEM,
        out_shape=pltpu.VMEM((2, *own.shape), own.dtype),
        compiler_params=params(),
        name="join_row",
    )(index, *in_vmem(own, beside))


def attend_kernel(head_dim, reach, index_ref, query_ref, key_seg_ref, *refs):
    row_refs, (mixed_ref, window) = refs[:-2], refs[-2:]
    rows = query_ref.shape[0]
    for place, row_ref in enumerate(row_refs):
        window[2 * place : 2 * place + 2] = row_ref[...]
    odd = index_ref[2]
    own_seg = key_seg_ref[:, pl.ds(reach * rows, rows)]
    query_seg = jnp.transpose(jnp.broadcast_to(own_seg, (rows, rows)))
    base = lax.broadcasted_iota(jnp.int32, (rows, rows), 0)
    offset = lax.broadcasted_iota(jnp.int32, (rows, rows), 1)
    allowed = []
    for piece in range(reach + 1):
        same = query_seg == key_seg_ref[:, pl.ds(piece * rows, rows)]
        if piece == reach:
            same = same & (offset <= base)
        allowed.append(same)
    for column in range(0, query_ref.shape[1], head_dim):
        span = pl.ds(column, head_dim)
        query = query_ref[:, span]
        scores = []
        for piece in range(reach + 1):
            score = lax.dot_general(
                query,
                window[odd + piece, :, :head_dim],
                (((1,), (1,)), ((), ())),
                preferred_element_type=jnp.float32,
            ) / math.sqrt(head_dim)
            scores.append(jnp.where(allowed[piece], score, -1e30))
        peak = scores[0]
        for score in scores[1:]:
            peak = jnp.maximum(peak, score)
        peak = jnp.max(peak, axis=1, keepdims=True)
        terms = [jnp.exp(score - peak) for score in scores]
        total = terms[0]
        for term in terms[1:]:
            total = total + term
        inverse = 1.0 / jnp.sum(total, axis=1, keepdims=True)
        mixed = jnp.zeros((rows, head_dim), jnp.float32)
        for piece in range(reach + 1):
            mixed += jnp.dot(
                (terms[piece] * inverse).astype(jnp.bfloat16),
                window[odd + piece, :, head_dim:],
                preferred_element_type=jnp.float32,
            )
        mixed_ref[:, span] = mixed.astype(jnp.bfloat16)


def attend(index, queries, row_windows, key_seg, head_dim, micros):
    reach = 2 * len(row_windows) - 2
    rows = queries.shape[0]
    return pl.pallas_call(
        functools.partial(attend_kernel, head_dim, reach),
        out_shape=pltpu.VMEM(queries.shape, jnp.bfloat16),
        in_specs=[IN_SMEM] + [IN_VMEM] * (2 + len(row_windows)),
        out_specs=IN_VMEM,
        scratch_shapes=[pltpu.VMEM((reach + 2, rows, 2 * head_dim), jnp.bfloat16)],
        compiler_params=params(),
        cost_estimate=estimate(micros),
        name="attend",
    )(index, *in_vmem(queries, key_seg, *row_windows))


def lay_out_kernel(plane_ref, query_ref, key_ref, value_ref, near_out, far_out, common_out, sems):
    q_half, kv_half = near_out.shape[2], common_out.shape[2] // 2
    near = pl.ds(pl.multiple_of(plane_ref[0] * q_half, q_half), q_half)
    far = pl.ds(pl.multiple_of((1 - plane_ref[0]) * q_half, q_half), q_half)
    moves = (
        (key_ref, common_out.at[0, :, :kv_half]),
        (value_ref, common_out.at[0, :, kv_half:]),
        (query_ref.at[:, near], near_out.at[0]),
        (query_ref.at[:, far], far_out.at[0]),
    )
    copies = [
        pltpu.make_async_copy(source, target, sems.at[place])
        for place, (source, target) in enumerate(moves)
    ]
    for copy in copies:
        copy.start()
    for copy in copies:
        copy.wait()


def lay_out(plane, query, key, value):
    depth, q_half = query.shape[0], query.shape[1] // 2
    shapes = ((1, depth, q_half), (1, depth, q_half), (1, depth, 2 * key.shape[1]))
    return pl.pallas_call(
        lay_out_kernel,
        in_specs=[IN_SMEM] + [IN_HBM] * 3,
        out_specs=[IN_VMEM] * 3,
        scratch_shapes=[pltpu.SemaphoreType.DMA((4,))],
        out_shape=[pltpu.VMEM(shape, jnp.bfloat16) for shape in shapes],
        compiler_params=params(),
        name="lay_out",
    )(plane, *in_hbm(query, key, value))


def rows_near_kernel(plane_ref, weight_ref, out_ref, sem):
    half = out_ref.shape[0]
    near = pl.ds(pl.multiple_of(plane_ref[0] * half, half), half)
    copy = pltpu.make_async_copy(weight_ref.at[near, :], out_ref, sem)
    copy.start()
    copy.wait()


def rows_near_of(plane, weight):
    rows, columns = weight.shape
    return pl.pallas_call(
        rows_near_kernel,
        in_specs=[IN_SMEM, IN_HBM],
        out_specs=IN_VMEM,
        scratch_shapes=[pltpu.SemaphoreType.DMA],
        out_shape=pltpu.VMEM((rows // 2, columns), weight.dtype),
        compiler_params=params(),
        name="rows_near",
    )(plane, *in_hbm(weight))


def both_kernel(first_ref, second_ref, out_ref):
    out_ref[0] = first_ref[0]
    out_ref[1] = second_ref[0]


def both_of(first, second):
    return pl.pallas_call(
        both_kernel,
        in_specs=[IN_VMEM] * 2,
        out_specs=IN_VMEM,
        out_shape=pltpu.VMEM((2, *first.shape[1:]), first.dtype),
        compiler_params=params(),
        name="both_of",
    )(*in_vmem(first, second))


def first_kernel(pair_ref, out_ref):
    out_ref[...] = pair_ref[:1]


def first_of(pair):
    return pl.pallas_call(
        first_kernel,
        in_specs=[IN_VMEM],
        out_specs=IN_VMEM,
        out_shape=pltpu.VMEM((1, *pair.shape[1:]), pair.dtype),
        compiler_params=params(),
        name="first_of",
    )(*in_vmem(pair))


def bring_kernel(source_ref, out_ref, sem):
    copy = pltpu.make_async_copy(source_ref, out_ref, sem)
    copy.start()
    copy.wait()


def bring(tokens, micros):
    return pl.pallas_call(
        bring_kernel,
        in_specs=[IN_HBM],
        out_specs=IN_VMEM,
        scratch_shapes=[pltpu.SemaphoreType.DMA],
        out_shape=pltpu.VMEM(tokens.shape, tokens.dtype),
        compiler_params=params(),
        cost_estimate=estimate(micros),
        name="bring",
    )(*in_hbm(tokens))


def project_kernel(slots, base, groups, first, last, index_ref, own_ref, other_ref, *refs):
    held_weights = groups * (1 + slots[-1][0])
    weights, refs = refs[:held_weights], refs[held_weights:]
    total_ref, refs = (None, refs) if first else (refs[0], refs[1:])
    rows = own_ref.shape[0]
    depth, width = weights[0].shape[-2:]
    block = rows // 2
    spans = [
        pl.ds(pl.multiple_of(index_ref[3 + base + place] * depth, depth), depth)
        for place in range(len(slots))
    ]
    out_ref = refs[2] if last else refs[0]
    for side, source_ref in enumerate((own_ref, other_ref)):
        for group in range(groups):
            columns = pl.ds(group * width, width)
            total = None if first else total_ref[side, :, columns]
            for place, (step, slot) in enumerate(slots):
                product = jnp.dot(
                    source_ref[:, spans[place]],
                    weights[groups * step + group][slot],
                    preferred_element_type=jnp.float32,
                )
                total = product if total is None else total + product
            out_ref[side, :, columns] = total
    if last:
        kept_ref, sent_ref, held = refs
        mine = pl.ds(pl.multiple_of(index_ref[0] * block, block), block)
        others = pl.ds(pl.multiple_of((1 - index_ref[0]) * block, block), block)
        kept_ref[:block] = held[0, mine, :]
        kept_ref[block:] = held[1, mine, :]
        sent_ref[:block] = held[1, others, :]
        sent_ref[block:] = held[0, others, :]


def project(index, base, tokens, steps, total, last, micros):
    groups = len(steps[0][1])
    slots = [(i, slot) for i, (used, _) in enumerate(steps) for slot in range(used)]
    rows = tokens[0].shape[0]
    columns = sum(part.shape[2] for part in steps[0][1])
    operands = in_vmem(*tokens, *(part for _, parts in steps for part in parts))
    if total is not None:
        operands += in_vmem(total)
    shapes = ((rows, columns), (rows, columns)) if last else ((2, rows, columns),)
    out = pl.pallas_call(
        functools.partial(project_kernel, slots, base, groups, total is None, last),
        in_specs=[IN_SMEM] + [IN_VMEM] * len(operands),
        out_specs=[IN_VMEM] * len(shapes),
        scratch_shapes=[pltpu.VMEM((2, rows, columns), jnp.float32)] if last else [],
        out_shape=[pltpu.VMEM(shape, jnp.float32) for shape in shapes],
        compiler_params=params(),
        cost_estimate=estimate(micros),
        name="project",
    )(index, *operands)
    return out if last else out[0]


def columns_kernel(places, base, index_ref, mixed_ref, returned_ref, *refs):
    weights = list(refs[: sum(places)])
    out_ref, send_ref, held, sems = refs[-4:]
    block = mixed_ref.shape[0] // 2
    half = mixed_ref.shape[1] // 2
    width = weights[0].shape[-1]
    mine = pl.ds(pl.multiple_of(index_ref[0] * block, block), block)
    others = pl.ds(pl.multiple_of((1 - index_ref[0]) * block, block), block)
    near = pl.ds(pl.multiple_of(index_ref[1] * half, half), half)
    far = pl.ds(pl.multiple_of((1 - index_ref[1]) * half, half), half)
    rows_in = jnp.concatenate([mixed_ref[...], returned_ref[...]], axis=0)
    copies = []
    for place, parts in enumerate(places):
        if parts == 1:
            whole = weights.pop(0)
            low, high = whole[near, :], whole[far, :]
        else:
            low, high = weights.pop(0)[...], weights.pop(0)[...]
        weight = jnp.concatenate([low, high], axis=0)
        value = jnp.dot(rows_in, weight, preferred_element_type=jnp.float32)
        value = value.astype(jnp.bfloat16)
        columns = pl.ds(place * width, width)
        held[mine, columns] = value[:block]
        held[others, columns] = value[3 * block :]
        send_ref[mine, columns] = value[block : 2 * block]
        send_ref[others, columns] = value[2 * block : 3 * block]
        column = pl.multiple_of(index_ref[3 + base + place] * width, width)
        copy = pltpu.make_async_copy(
            held.at[:, columns], out_ref.at[:, pl.ds(column, width)], sems.at[place]
        )
        copy.start()
        copies.append(copy)
    for copy in copies:
        copy.wait()


def columns_of(index, base, mixed, returned, shards, result, width, micros):
    rows = mixed.shape[0]
    out_cols = shards[0][0].shape[-1]
    operands = in_vmem(mixed, returned, *(part for shard in shards for part in shard))
    specs = [IN_SMEM] + [IN_VMEM] * len(operands)
    if result is not None:
        operands += in_hbm(result)
        specs.append(IN_HBM)
    sent = (rows, len(shards) * out_cols)
    return pl.pallas_call(
        functools.partial(columns_kernel, [len(shard) for shard in shards], base),
        in_specs=specs,
        out_specs=[IN_HBM, IN_VMEM],
        scratch_shapes=[
            pltpu.VMEM(sent, jnp.bfloat16),
            pltpu.SemaphoreType.DMA((len(shards),)),
        ],
        out_shape=[pltpu.HBM((rows, width), jnp.bfloat16), pltpu.VMEM(sent, jnp.bfloat16)],
        input_output_aliases={} if result is None else {len(operands): 0},
        compiler_params=params(),
        cost_estimate=estimate(micros),
        name="columns_of",
    )(index, *operands)


def place_kernel(width, base, index_ref, came_ref, _, out_ref, sems):
    copies = []
    for place in range(came_ref.shape[1] // width):
        column = pl.multiple_of(index_ref[base + place] * width, width)
        copy = pltpu.make_async_copy(
            came_ref.at[:, pl.ds(place * width, width)],
            out_ref.at[:, pl.ds(column, width)],
            sems.at[place],
        )
        copy.start()
        copies.append(copy)
    for copy in copies:
        copy.wait()


def place_columns(index, base, came, result, out_cols):
    return pl.pallas_call(
        functools.partial(place_kernel, out_cols, base),
        in_specs=[IN_SMEM, IN_VMEM, IN_HBM],
        out_specs=IN_HBM,
        scratch_shapes=[pltpu.SemaphoreType.DMA((came.shape[1] // out_cols,))],
        out_shape=pltpu.HBM(result.shape, result.dtype),
        input_output_aliases={2: 0},
        compiler_params=params(),
        name="place_columns",
    )(index, *in_vmem(came), *in_hbm(result))


def on_device(hidden_in, segment_ids, w_query, w_key, w_value, w_out):
    count = lax.axis_size("ctx")
    me = lax.axis_index("ctx")
    plane = lax.axis_index("dp")
    core, chip = me % 2, me // 2
    rows, width = hidden_in.shape
    block = rows // 2
    head_dim = w_key.shape[1]
    q_rows, out_cols = w_out.shape

    reach = REACH * block // rows
    pair = jnp.where(core == 0, chip, count - 1 - chip)
    pair_pos = pair * rows + jnp.arange(rows, dtype=jnp.int32)
    cosine, sine = rotary_tables(pair_pos, head_dim)
    seg_blocks = segment_ids.reshape(2 * count, block)
    seq_block = pair * 2 - 2 * reach + jnp.arange(2 * reach + 2, dtype=jnp.int32)
    clipped = jnp.maximum(seq_block, 0)
    stored = jnp.where(clipped < count, 2 * clipped, 2 * (2 * count - 1 - clipped) + 1)
    seg_rows = seg_blocks[stored]
    key_seg = jnp.where(seq_block[:, None] >= 0, seg_rows, -1).reshape(1, -1)
    tables = (cosine, sine, cosine, sine, key_seg)
    index = [core, plane, pair % 2]

    def row_windows(joined):
        sends = [(device, device ^ 2) for device in range(count)]
        own_row = join_row(index, joined, lax.ppermute(joined, "ctx", sends))
        windows = []
        for back in range(1, reach // 2 + 1):
            sends = [
                (row_device(row, column, count), row_device(row + back, column, count))
                for row in range(count // 2 - back)
                for column in range(2)
            ]
            windows.append(lax.ppermute(own_row, "ctx", sends))
        return own_row, windows

    ringed = count <= RING_LIMIT
    if ringed:
        plane_index = plane.reshape(1).astype(jnp.int32)
        pairs = ring_pairs(count // 2)
        half = count // 4
        owners = shard_owners(me, count)
        index += [*owners, *shard_owners(me ^ 1, count)]
        index = jnp.stack(index).astype(jnp.int32)

        def ring(value):
            return lax.ppermute(value, "ctx", pairs)

        def add_projections(total, steps, begin, end, last=False):
            base = 0 if begin == 0 else 2 * begin - 1
            return project(index, base, (hidden_in, other), steps[begin:end], total, last)

        own_near, own_far, own_common = lay_out(plane_index, w_query, w_key, w_value)
        done = {"w_out": w_out}
        common_steps = [(1, (own_common,))]
        query_steps = [(1, (own_near, own_far))]
        sent_sums = {}
        outputs = {}

        def run(name, *ties):
            nonlocal index, cosine, sine, query_cosine, query_sine, key_seg

            def tied(value):
                return after(value, *(done[tie] for tie in ties)) if ties else value

            kind, step = name[:-1], int(name[-1])
            micros = MICROS.get(kind, 2)
            if name == "tables0":
                first, index, cosine, sine, query_cosine, query_sine, key_seg = (
                    lax.optimization_barrier(
                        (done["common0"], index, cosine, sine, query_cosine, query_sine, key_seg)
                    )
                )
                done["common0"] = value = first
            elif name == "common0":
                value = both_of(own_common, core_swap(tied(own_common), count))
            elif name == "near0":
                value = both_of(own_near, core_swap(tied(own_near), count))
            elif name == "other0":
                value = core_swap(tied(done["tokens0"]), count)
            elif name == "tokens0":
                value = bring(tied(hidden_in), micros)
            elif name == "second0":
                rows_near = w_out
                if HALVED:
                    rows_near = own_rows_near
                value = core_swap(tied(rows_near), count)
            elif name == "first0":
                value = w_out
            elif kind in ("common", "near"):
                value = done[f"{kind}{step - 1}"]
                value = ring(tied(first_of(value) if step == half else value))
                if kind == "common":
                    common_steps.append((value.shape[0], (value,)))
            elif kind == "far":
                near = done[f"near{step}"]
                value = plane_swap(tied(near))
                query_steps.append((near.shape[0], (near, value)))
            elif kind in ("first", "second"):
                value = ring(tied(done[f"{kind}{step - 1}"]))
            elif kind == "cross":
                value = plane_swap(tied(done[f"second{step}"]))
            elif kind in ("keys", "queries"):
                begin, end, last = PROJECTIONS[name]
                steps = list(common_steps if kind == "keys" else query_steps)
                if ties:
                    used, parts = steps[begin]
                    steps[begin] = (used, (tied(parts[0]), *parts[1:]))
                value = project(
                    index,
                    0 if begin == 0 else 2 * begin - 1,
                    (done["tokens0"], done["other0"]),
                    steps[begin:end],
                    done.get(f"{kind}{step - 1}"),
                    last,
                    micros,
                )
                if last:
                    kept, sent = value
                    came = core_swap(sent, count)
                    if kind == "keys":
                        value = rotate_sums(1, kept, came, cosine, sine)
                    else:
                        value = rotate_sums(
                            q_rows // head_dim, kept, came, query_cosine, query_sine
                        )
            elif name == "row0":
                sends = [(device, device ^ 2) for device in range(count)]
                joined = done["keys3"]
                value = join_row(index, joined, lax.ppermute(tied(joined), "ctx", sends))
            elif kind == "row":
                sends = [
                    (row_device(row, column, count), row_device(row + step, column, count))
                    for row in range(count // 2 - step)
                    for column in range(2)
                ]
                value = lax.ppermute(tied(done["row0"]), "ctx", sends)
            elif name == "mixed0":
                windows = [done["row2"], done["row1"], done["row0"]]
                value = attend(index, tied(done["queries4"]), windows, key_seg, head_dim, micros)
            elif name == "mixed1":
                value = core_swap(done["mixed0"], count)
            elif kind == "columns":
                begin, end = COLUMNS[name]
                shards = [(w_out,)]
                for turn in range(1, half + 1):
                    if f"first{turn}" in done:
                        shards.append((done[f"first{turn}"],))
                    if f"second{turn}" in done:
                        pair = (done[f"second{turn}"],)
                        if HALVED:
                            pair += (done[f"cross{turn}"],)
                        shards.append(pair)
                result, sent = columns_of(
                    index,
                    begin,
                    done["mixed0"],
                    tied(done["mixed1"]),
                    shards[begin:end],
                    outputs.get("result"),
                    width,
                    micros,
                )
                outputs["result"] = result
                value = core_swap(sent, count)
            elif kind == "place":
                begin, _ = COLUMNS[f"columns{step}"]
                value = place_columns(
                    index, 3 + 2 * half + begin, done[f"columns{step}"], outputs["result"], out_cols
                )
                outputs["result"] = value
            done[name] = value

        own_rows_near = None
        cosine, sine, query_cosine, query_sine, key_seg = tables
        if HALVED:
            own_rows_near = rows_near_of(plane_index, w_out)
        for entry in PLAN:
            run(*entry.split())
        return outputs["result"]
    else:
        index = jnp.stack(index).astype(jnp.int32)
        cosine, sine, query_cosine, query_sine, key_seg = tables
        gathered = lax.all_gather(
            jnp.concatenate([w_key, w_value, w_query], axis=1), "ctx", axis=0, tiled=True
        )
        ordered = jnp.where(core == 0, hidden_in, jnp.roll(hidden_in, block, axis=0))
        pair_tokens = jnp.concatenate([ordered[:block], core_swap(ordered[block:], count)], axis=0)
        sums = jnp.dot(pair_tokens, gathered, preferred_element_type=jnp.float32)
        kv_sums, query_sums = sums[:, : 2 * head_dim], sums[:, 2 * head_dim :]
        joined = rotate_sums(1, kv_sums, jnp.zeros_like(kv_sums), cosine, sine)
        queries = rotate_sums(
            q_rows // head_dim, query_sums, jnp.zeros_like(query_sums), query_cosine, query_sine
        )
        own_row, windows = row_windows(joined)

    mixed = attend(index, queries, [*windows[::-1], own_row], key_seg, head_dim, 4)
    returned = core_swap(mixed, count)
    kinds = (mixed[:block], returned[block:])
    own_rows = jnp.where(
        core == 0, jnp.concatenate(kinds, axis=0), jnp.concatenate(kinds[::-1], axis=0)
    )
    gathered = lax.all_gather(w_out, "ctx", axis=1, tiled=True)
    return jnp.dot(own_rows, gathered, preferred_element_type=jnp.float32).astype(jnp.bfloat16)


def solution(mesh):
    in_specs = (
        P(("dp", "ctx"), None),
        P("dp"),
        P("ctx", None),
        P("ctx", None),
        P("ctx", None),
        P(None, "ctx"),
    )
    out_specs = P(("dp", "ctx"), None)
    return jax.shard_map(
        on_device, mesh=mesh, in_specs=in_specs, out_specs=out_specs, check_vma=False
    )
```

```python
import functools
import math

import jax
import jax.numpy as jnp
from jax import lax
from jax.experimental import pallas as pl
from jax.experimental.pallas import tpu as pltpu
from jax.sharding import PartitionSpec as P

REACH = 8
ROPE_BASE = 500000.0
RING_LIMIT = 16
VMEM_LIMIT = 16 * 1024 * 1024
HALVED = True
PLAN = (
    "A0",
    "N0",
    "N1",
    "C0",
    "T0",
    "B0 N1",
    "H0 N1 C0",
    "S0",
    "N2",
    "C1 N1",
    "F1",
    "A1",
    "N3",
    "C2 N2 F1",
    "F2",
    "B1 N3",
    "X1",
    "N4 F2",
    "Q1 A1",
    "C3 N3 F2 Q1",
    "F3",
    "A2 N4",
    "F4",
    "Q2 B1",
    "C4 N4 Q2 F3",
    "K1",
    "K2 A2 Q2",
    "B2 N4",
    "X2 F4",
    "A3 C4 K2",
    "B3 C4",
    "K3 X1",
    "Q3 K3",
    "Q4 A3",
    "R0 X2",
    "R1",
    "R2",
    "X3",
    "A4 R0",
    "M0 X3 R2",
    "M1",
    "W0 M0",
    "W1 B3",
    "W2",
    "W3",
    "O0",
    "W4",
    "O1",
)
MICROS = {}
PROJECTIONS = {
    "K1": (0, 2, False),
    "K2": (2, 4, False),
    "K3": (4, 5, True),
    "Q1": (0, 2, False),
    "Q2": (2, 3, False),
    "Q3": (3, 4, False),
    "Q4": (4, 5, True),
}
COLUMNS = ((0, 1, 2, 3), (4,))


def step_shards(turn, half):
    if turn == 0 or turn == half:
        return (f"A{turn}",)
    return (f"A{turn}", f"B{turn}", f"X{turn}")


def chip_at(place, chips):
    place = place % chips
    return jnp.where(place < chips // 2, 2 * place, 2 * (chips - 1 - place) + 1)


def static_chip_at(place, chips):
    place %= chips
    return 2 * place if place < chips // 2 else 2 * (chips - 1 - place) + 1


def ring_pairs(chips):
    pairs = []
    for place in range(chips):
        here = static_chip_at(place, chips)
        pairs.append((2 * here, 2 * static_chip_at(place + 1, chips)))
        pairs.append((2 * here + 1, 2 * static_chip_at(place - 1, chips) + 1))
    return pairs


def core_swap(value, count):
    return lax.ppermute(value, "ctx", [(i, i ^ 1) for i in range(count)])


def plane_swap(value):
    return lax.ppermute(value, "dp", [(0, 1), (1, 0)])


def row_device(row, column, count):
    pair = 2 * row + (column if row < count // 4 else 1 - column)
    return 2 * pair if pair < count // 2 else 2 * (count - 1 - pair) + 1


def after(value, *others):
    return lax.optimization_barrier((value, *others))[0]


def shard_owners(me, count):
    chips = count // 2
    half = chips // 2
    core, chip = me % 2, me // 2
    place = jnp.where(chip % 2 == 0, chip // 2, chips - 1 - chip // 2)
    way = jnp.where(core == 0, -1, 1)
    owners = [me]
    for step in range(1, half + 1):
        source = chip_at(place + way * step + chips, chips)
        owners.append(2 * source + core)
        if step < half:
            owners.append(2 * source + 1 - core)
    return owners


def params(**settings):
    return pltpu.CompilerParams(vmem_limit_bytes=VMEM_LIMIT, **settings)


def in_vmem(*arrays):
    return [pltpu.with_memory_space_constraint(array, pltpu.VMEM) for array in arrays]


def in_hbm(*arrays):
    return [pltpu.with_memory_space_constraint(array, pltpu.HBM) for array in arrays]


def estimate(micros):
    return pl.CostEstimate(flops=int(micros * 1.1535e9), bytes_accessed=0, transcendentals=0)


IN_VMEM = pl.BlockSpec(memory_space=pltpu.VMEM)
IN_HBM = pl.BlockSpec(memory_space=pl.ANY)
IN_SMEM = pl.BlockSpec(memory_space=pltpu.SMEM)


def rotate_kernel(head_dim, heads, kept_ref, came_ref, cos_ref, sin_ref, out_ref):
    cosine, sine = cos_ref[...], sin_ref[...]
    for column in range(0, kept_ref.shape[1], head_dim):
        span = pl.ds(column, head_dim)
        part = kept_ref[:, span] + came_ref[:, span]
        if column < heads * head_dim:
            part = part * cosine + pltpu.roll(part, head_dim // 2, 1) * sine
        out_ref[:, span] = part.astype(jnp.bfloat16)


def rotary_tables(positions, head_dim):
    frequency = ROPE_BASE ** (
        -(jnp.arange(head_dim // 2, dtype=jnp.float32) * 2.0) / head_dim
    )
    angles = positions.astype(jnp.float32)[:, None] * frequency[None, :]
    cosine, sine = jnp.cos(angles), jnp.sin(angles)
    return jnp.concatenate([cosine, cosine], axis=1), jnp.concatenate([-sine, sine], axis=1)


def rotate_sums(heads, kept, came, cosine, sine):
    return pl.pallas_call(
        functools.partial(rotate_kernel, cosine.shape[1], heads),
        out_shape=pltpu.VMEM(kept.shape, jnp.bfloat16),
        in_specs=[IN_VMEM] * 4,
        out_specs=IN_VMEM,
        compiler_params=params(),
        name="rotate_sums",
    )(*in_vmem(kept, came, cosine, sine))


def join_row_kernel(index_ref, own_ref, beside_ref, out_ref):
    odd = index_ref[2]
    out_ref[odd] = own_ref[...]
    out_ref[1 - odd] = beside_ref[...]


def join_row(index, own, beside):
    return pl.pallas_call(
        join_row_kernel,
        in_specs=[IN_SMEM, IN_VMEM, IN_VMEM],
        out_specs=IN_VMEM,
        out_shape=pltpu.VMEM((2, *own.shape), own.dtype),
        compiler_params=params(),
        name="join_row",
    )(index, *in_vmem(own, beside))


def attend_kernel(head_dim, reach, index_ref, query_ref, key_seg_ref, *refs):
    row_refs, (mixed_ref, window) = refs[:-2], refs[-2:]
    rows = query_ref.shape[0]
    for place, row_ref in enumerate(row_refs):
        window[2 * place : 2 * place + 2] = row_ref[...]
    odd = index_ref[2]
    own_seg = key_seg_ref[:, pl.ds(reach * rows, rows)]
    query_seg = jnp.transpose(jnp.broadcast_to(own_seg, (rows, rows)))
    base = lax.broadcasted_iota(jnp.int32, (rows, rows), 0)
    offset = lax.broadcasted_iota(jnp.int32, (rows, rows), 1)
    allowed = []
    for piece in range(reach + 1):
        same = query_seg == key_seg_ref[:, pl.ds(piece * rows, rows)]
        if piece == reach:
            same = same & (offset <= base)
        allowed.append(same)
    scale = math.log2(math.e) / math.sqrt(head_dim)
    for column in range(0, query_ref.shape[1], head_dim):
        span = pl.ds(column, head_dim)
        query = query_ref[:, span]
        scores = []
        for piece in range(reach + 1):
            score = lax.dot_general(
                query,
                window[odd + piece, :, :head_dim],
                (((1,), (1,)), ((), ())),
                preferred_element_type=jnp.float32,
            )
            scores.append(jnp.where(allowed[piece], score, -1e30))
        peak = scores[0]
        for score in scores[1:]:
            peak = jnp.maximum(peak, score)
        peak = jnp.max(peak, axis=1, keepdims=True)
        terms = [jnp.exp2((score - peak) * scale) for score in scores]
        total = terms[0]
        for term in terms[1:]:
            total = total + term
        mixed = jnp.zeros((rows, head_dim), jnp.float32)
        for piece in range(reach + 1):
            mixed += jnp.dot(
                terms[piece].astype(jnp.bfloat16),
                window[odd + piece, :, head_dim:],
                preferred_element_type=jnp.float32,
            )
        mixed = mixed / jnp.sum(total, axis=1, keepdims=True)
        mixed_ref[:, span] = mixed.astype(jnp.bfloat16)


def attend(index, queries, row_windows, key_seg, head_dim, micros):
    reach = 2 * len(row_windows) - 2
    rows = queries.shape[0]
    return pl.pallas_call(
        functools.partial(attend_kernel, head_dim, reach),
        out_shape=pltpu.VMEM(queries.shape, jnp.bfloat16),
        in_specs=[IN_SMEM] + [IN_VMEM] * (2 + len(row_windows)),
        out_specs=IN_VMEM,
        scratch_shapes=[pltpu.VMEM((reach + 2, rows, 2 * head_dim), jnp.bfloat16)],
        compiler_params=params(),
        cost_estimate=estimate(micros),
        name="attend",
    )(index, *in_vmem(queries, key_seg, *row_windows))


def lay_out_kernel(plane_ref, query_ref, key_ref, value_ref, near_out, far_out, common_out, sems):
    q_half, kv_half = near_out.shape[2], common_out.shape[2] // 2
    near = pl.ds(pl.multiple_of(plane_ref[0] * q_half, q_half), q_half)
    far = pl.ds(pl.multiple_of((1 - plane_ref[0]) * q_half, q_half), q_half)
    moves = (
        (key_ref, common_out.at[0, :, :kv_half]),
        (value_ref, common_out.at[0, :, kv_half:]),
        (query_ref.at[:, near], near_out.at[0]),
        (query_ref.at[:, far], far_out.at[0]),
    )
    copies = [
        pltpu.make_async_copy(source, target, sems.at[place])
        for place, (source, target) in enumerate(moves)
    ]
    for copy in copies:
        copy.start()
    for copy in copies:
        copy.wait()


def lay_out(plane, query, key, value):
    depth, q_half = query.shape[0], query.shape[1] // 2
    shapes = ((1, depth, q_half), (1, depth, q_half), (1, depth, 2 * key.shape[1]))
    return pl.pallas_call(
        lay_out_kernel,
        in_specs=[IN_SMEM] + [IN_HBM] * 3,
        out_specs=[IN_VMEM] * 3,
        scratch_shapes=[pltpu.SemaphoreType.DMA((4,))],
        out_shape=[pltpu.VMEM(shape, jnp.bfloat16) for shape in shapes],
        compiler_params=params(),
        name="lay_out",
    )(plane, *in_hbm(query, key, value))


def rows_near_kernel(plane_ref, weight_ref, out_ref, sem):
    half = out_ref.shape[0]
    near = pl.ds(pl.multiple_of(plane_ref[0] * half, half), half)
    copy = pltpu.make_async_copy(weight_ref.at[near, :], out_ref, sem)
    copy.start()
    copy.wait()


def rows_near_of(plane, weight):
    rows, columns = weight.shape
    return pl.pallas_call(
        rows_near_kernel,
        in_specs=[IN_SMEM, IN_HBM],
        out_specs=IN_VMEM,
        scratch_shapes=[pltpu.SemaphoreType.DMA],
        out_shape=pltpu.VMEM((rows // 2, columns), weight.dtype),
        compiler_params=params(),
        name="rows_near",
    )(plane, *in_hbm(weight))


def both_kernel(first_ref, second_ref, out_ref):
    out_ref[0] = first_ref[0]
    out_ref[1] = second_ref[0]


def both_of(first, second):
    return pl.pallas_call(
        both_kernel,
        in_specs=[IN_VMEM] * 2,
        out_specs=IN_VMEM,
        out_shape=pltpu.VMEM((2, *first.shape[1:]), first.dtype),
        compiler_params=params(),
        name="both_of",
    )(*in_vmem(first, second))


def first_kernel(pair_ref, out_ref):
    out_ref[...] = pair_ref[:1]


def first_of(pair):
    return pl.pallas_call(
        first_kernel,
        in_specs=[IN_VMEM],
        out_specs=IN_VMEM,
        out_shape=pltpu.VMEM((1, *pair.shape[1:]), pair.dtype),
        compiler_params=params(),
        name="first_of",
    )(*in_vmem(pair))


def bring_kernel(source_ref, out_ref, sem):
    copy = pltpu.make_async_copy(source_ref, out_ref, sem)
    copy.start()
    copy.wait()


def bring(tokens, micros):
    return pl.pallas_call(
        bring_kernel,
        in_specs=[IN_HBM],
        out_specs=IN_VMEM,
        scratch_shapes=[pltpu.SemaphoreType.DMA],
        out_shape=pltpu.VMEM(tokens.shape, tokens.dtype),
        compiler_params=params(),
        cost_estimate=estimate(micros),
        name="bring",
    )(*in_hbm(tokens))


def project_kernel(slots, base, groups, first, last, index_ref, own_ref, other_ref, *refs):
    held_weights = groups * (1 + slots[-1][0])
    weights, refs = refs[:held_weights], refs[held_weights:]
    total_ref, refs = (None, refs) if first else (refs[0], refs[1:])
    rows = own_ref.shape[0]
    depth, width = weights[0].shape[-2:]
    block = rows // 2
    spans = [
        pl.ds(pl.multiple_of(index_ref[3 + base + place] * depth, depth), depth)
        for place in range(len(slots))
    ]
    out_ref = refs[2] if last else refs[0]
    for side, source_ref in enumerate((own_ref, other_ref)):
        for group in range(groups):
            columns = pl.ds(group * width, width)
            total = None if first else total_ref[side, :, columns]
            for place, (step, slot) in enumerate(slots):
                product = jnp.dot(
                    source_ref[:, spans[place]],
                    weights[groups * step + group][slot],
                    preferred_element_type=jnp.float32,
                )
                total = product if total is None else total + product
            out_ref[side, :, columns] = total
    if last:
        kept_ref, sent_ref, held = refs
        mine = pl.ds(pl.multiple_of(index_ref[0] * block, block), block)
        others = pl.ds(pl.multiple_of((1 - index_ref[0]) * block, block), block)
        kept_ref[:block] = held[0, mine, :]
        kept_ref[block:] = held[1, mine, :]
        sent_ref[:block] = held[1, others, :]
        sent_ref[block:] = held[0, others, :]


def project(index, base, tokens, steps, total, last, micros):
    groups = len(steps[0][1])
    slots = [(i, slot) for i, (used, _) in enumerate(steps) for slot in range(used)]
    rows = tokens[0].shape[0]
    columns = sum(part.shape[2] for part in steps[0][1])
    operands = in_vmem(*tokens, *(part for _, parts in steps for part in parts))
    if total is not None:
        operands += in_vmem(total)
    shapes = ((rows, columns), (rows, columns)) if last else ((2, rows, columns),)
    out = pl.pallas_call(
        functools.partial(project_kernel, slots, base, groups, total is None, last),
        in_specs=[IN_SMEM] + [IN_VMEM] * len(operands),
        out_specs=[IN_VMEM] * len(shapes),
        scratch_shapes=[pltpu.VMEM((2, rows, columns), jnp.float32)] if last else [],
        out_shape=[pltpu.VMEM(shape, jnp.float32) for shape in shapes],
        compiler_params=params(),
        cost_estimate=estimate(micros),
        name="project",
    )(index, *operands)
    return out if last else out[0]


def columns_kernel(entries, index_ref, mixed_ref, returned_ref, *refs):
    weights = list(refs[: sum(parts for _, parts in entries)])
    out_ref, held, sems = refs[-3:]
    block = mixed_ref.shape[0] // 2
    half = mixed_ref.shape[1] // 2
    width = weights[0].shape[-1]
    mine = pl.ds(pl.multiple_of(index_ref[0] * block, block), block)
    others = pl.ds(pl.multiple_of((1 - index_ref[0]) * block, block), block)
    near = pl.ds(pl.multiple_of(index_ref[1] * half, half), half)
    far = pl.ds(pl.multiple_of((1 - index_ref[1]) * half, half), half)
    rows_in = jnp.concatenate([mixed_ref[:block], returned_ref[block:]], axis=0)
    near_in, far_in = rows_in[:, :half], rows_in[:, half:]
    copies = []
    for place, (owner, parts) in enumerate(entries):
        if parts == 1:
            whole = weights.pop(0)
            low, high = whole[near, :], whole[far, :]
        else:
            low, high = weights.pop(0)[...], weights.pop(0)[...]
        value = jnp.dot(near_in, low, preferred_element_type=jnp.float32)
        value += jnp.dot(far_in, high, preferred_element_type=jnp.float32)
        value = value.astype(jnp.bfloat16)
        columns = pl.ds(place * width, width)
        held[mine, columns] = value[:block]
        held[others, columns] = value[block:]
        column = pl.multiple_of(index_ref[owner] * width, width)
        copy = pltpu.make_async_copy(
            held.at[:, columns], out_ref.at[:, pl.ds(column, width)], sems.at[place]
        )
        copy.start()
        copies.append(copy)
    for copy in copies:
        copy.wait()


def columns_of(index, mixed, returned, shards, result, width, micros):
    rows = mixed.shape[0]
    out_cols = shards[0][1][0].shape[-1]
    entries = [(owner, len(parts)) for owner, parts in shards]
    operands = in_vmem(mixed, returned, *(part for _, parts in shards for part in parts))
    specs = [IN_SMEM] + [IN_VMEM] * len(operands)
    if result is not None:
        operands += in_hbm(result)
        specs.append(IN_HBM)
    return pl.pallas_call(
        functools.partial(columns_kernel, entries),
        in_specs=specs,
        out_specs=IN_HBM,
        scratch_shapes=[
            pltpu.VMEM((rows, len(shards) * out_cols), jnp.bfloat16),
            pltpu.SemaphoreType.DMA((len(shards),)),
        ],
        out_shape=pltpu.HBM((rows, width), jnp.bfloat16),
        input_output_aliases={} if result is None else {len(operands): 0},
        compiler_params=params(),
        cost_estimate=estimate(micros),
        name="columns_of",
    )(index, *operands)


def on_device(hidden_in, segment_ids, w_query, w_key, w_value, w_out):
    count = lax.axis_size("ctx")
    me = lax.axis_index("ctx")
    plane = lax.axis_index("dp")
    core, chip = me % 2, me // 2
    rows, width = hidden_in.shape
    block = rows // 2
    head_dim = w_key.shape[1]
    q_rows, out_cols = w_out.shape

    reach = REACH * block // rows
    pair = jnp.where(core == 0, chip, count - 1 - chip)
    pair_pos = pair * rows + jnp.arange(rows, dtype=jnp.int32)
    cosine, sine = rotary_tables(pair_pos, head_dim)
    seg_blocks = segment_ids.reshape(2 * count, block)
    seq_block = pair * 2 - 2 * reach + jnp.arange(2 * reach + 2, dtype=jnp.int32)
    clipped = jnp.maximum(seq_block, 0)
    stored = jnp.where(clipped < count, 2 * clipped, 2 * (2 * count - 1 - clipped) + 1)
    seg_rows = seg_blocks[stored]
    key_seg = jnp.where(seq_block[:, None] >= 0, seg_rows, -1).reshape(1, -1)
    tables = (cosine, sine, cosine, sine, key_seg)
    index = [core, plane, pair % 2]

    def row_windows(joined):
        sends = [(device, device ^ 2) for device in range(count)]
        own_row = join_row(index, joined, lax.ppermute(joined, "ctx", sends))
        windows = []
        for back in range(1, reach // 2 + 1):
            sends = [
                (row_device(row, column, count), row_device(row + back, column, count))
                for row in range(count // 2 - back)
                for column in range(2)
            ]
            windows.append(lax.ppermute(own_row, "ctx", sends))
        return own_row, windows

    ringed = count <= RING_LIMIT
    if ringed:
        plane_index = plane.reshape(1).astype(jnp.int32)
        pairs = ring_pairs(count // 2)
        half = count // 4
        owners = shard_owners(me, count)
        index += [*owners, *shard_owners(me ^ 1, count)]
        index = jnp.stack(index).astype(jnp.int32)

        def ring(value):
            return lax.ppermute(value, "ctx", pairs)

        def add_projections(total, steps, begin, end, last=False):
            base = 0 if begin == 0 else 2 * begin - 1
            return project(index, base, (hidden_in, other), steps[begin:end], total, last)

        own_near, own_far, own_common = lay_out(plane_index, w_query, w_key, w_value)
        done = {"w_out": w_out}
        common_steps = [(1, (own_common,))]
        query_steps = [(1, (own_near, own_far))]

        def run(name, *ties):
            nonlocal index, cosine, sine, query_cosine, query_sine, key_seg

            def tied(value):
                return after(value, *(done[tie] for tie in ties)) if ties else value

            kind, step = name[:-1], int(name[-1])
            micros = MICROS.get(kind, 2)
            if name == "T0":
                first, index, cosine, sine, query_cosine, query_sine, key_seg = (
                    lax.optimization_barrier(
                        (done["C0"], index, cosine, sine, query_cosine, query_sine, key_seg)
                    )
                )
                done["C0"] = value = first
            elif name == "C0":
                value = both_of(own_common, core_swap(tied(own_common), count))
            elif name == "N0":
                value = both_of(own_near, core_swap(tied(own_near), count))
            elif name == "S0":
                value = core_swap(tied(done["H0"]), count)
            elif name == "H0":
                value = bring(tied(hidden_in), micros)
            elif name == "B0":
                rows_near = w_out
                if HALVED:
                    rows_near = own_rows_near
                value = core_swap(tied(rows_near), count)
            elif name == "A0":
                value = w_out
            elif kind in ("C", "N"):
                value = done[f"{kind}{step - 1}"]
                value = ring(tied(first_of(value) if step == half else value))
                if kind == "C":
                    common_steps.append((value.shape[0], (value,)))
            elif kind == "F":
                near = done[f"N{step}"]
                value = plane_swap(tied(near))
                query_steps.append((near.shape[0], (near, value)))
            elif kind in ("A", "B"):
                value = ring(tied(done[f"{kind}{step - 1}"]))
            elif kind == "X":
                value = plane_swap(tied(done[f"B{step}"]))
            elif kind in ("K", "Q"):
                begin, end, last = PROJECTIONS[name]
                steps = list(common_steps if kind == "K" else query_steps)
                if ties:
                    used, parts = steps[begin]
                    steps[begin] = (used, (tied(parts[0]), *parts[1:]))
                value = project(
                    index,
                    0 if begin == 0 else 2 * begin - 1,
                    (done["H0"], done["S0"]),
                    steps[begin:end],
                    done.get(f"{kind}{step - 1}"),
                    last,
                    micros,
                )
                if last:
                    kept, sent = value
                    came = core_swap(sent, count)
                    if kind == "K":
                        value = rotate_sums(1, kept, came, cosine, sine)
                    else:
                        value = rotate_sums(
                            q_rows // head_dim, kept, came, query_cosine, query_sine
                        )
            elif name == "R0":
                sends = [(device, device ^ 2) for device in range(count)]
                joined = done["K3"]
                value = join_row(index, joined, lax.ppermute(tied(joined), "ctx", sends))
            elif kind == "R":
                sends = [
                    (row_device(row, column, count), row_device(row + step, column, count))
                    for row in range(count // 2 - step)
                    for column in range(2)
                ]
                value = lax.ppermute(tied(done["R0"]), "ctx", sends)
            elif name == "M0":
                windows = [done["R2"], done["R1"], done["R0"]]
                value = attend(index, tied(done["Q4"]), windows, key_seg, head_dim, micros)
            elif name == "M1":
                value = core_swap(done["M0"], count)
            elif kind == "W":
                if step == 0:
                    value = (core_swap(tied(w_out), count),)
                else:
                    value = [core_swap(tied(done[f"A{step}"]), count)]
                    if step < half:
                        value.append(core_swap(done[f"B{step}"], count))
                        value.append(core_swap(done[f"X{step}"], count))
            elif kind == "O":
                shards = []
                for turn in COLUMNS[step]:
                    for base, held in (
                        (3, [done[key] for key in step_shards(turn, half)]),
                        (3 + 2 * half, done[f"W{turn}"]),
                    ):
                        place = base + (2 * turn - 1 if turn else 0)
                        shards.append((place, held[:1]))
                        if len(held) > 1:
                            shards.append((place + 1, held[1:]))
                value = columns_of(
                    index,
                    done["M0"],
                    tied(done["M1"]),
                    shards,
                    done.get("O0"),
                    width,
                    micros,
                )
            done[name] = value

        own_rows_near = None
        cosine, sine, query_cosine, query_sine, key_seg = tables
        if HALVED:
            own_rows_near = rows_near_of(plane_index, w_out)
        for entry in PLAN:
            run(*entry.split())
        return done["O1"]
    else:
        index = jnp.stack(index).astype(jnp.int32)
        cosine, sine, query_cosine, query_sine, key_seg = tables
        gathered = lax.all_gather(
            jnp.concatenate([w_key, w_value, w_query], axis=1), "ctx", axis=0, tiled=True
        )
        ordered = jnp.where(core == 0, hidden_in, jnp.roll(hidden_in, block, axis=0))
        pair_tokens = jnp.concatenate([ordered[:block], core_swap(ordered[block:], count)], axis=0)
        sums = jnp.dot(pair_tokens, gathered, preferred_element_type=jnp.float32)
        kv_sums, query_sums = sums[:, : 2 * head_dim], sums[:, 2 * head_dim :]
        joined = rotate_sums(1, kv_sums, jnp.zeros_like(kv_sums), cosine, sine)
        queries = rotate_sums(
            q_rows // head_dim, query_sums, jnp.zeros_like(query_sums), query_cosine, query_sine
        )
        own_row, windows = row_windows(joined)

    mixed = attend(index, queries, [*windows[::-1], own_row], key_seg, head_dim, 4)
    returned = core_swap(mixed, count)
    kinds = (mixed[:block], returned[block:])
    own_rows = jnp.where(
        core == 0, jnp.concatenate(kinds, axis=0), jnp.concatenate(kinds[::-1], axis=0)
    )
    gathered = lax.all_gather(w_out, "ctx", axis=1, tiled=True)
    return jnp.dot(own_rows, gathered, preferred_element_type=jnp.float32).astype(jnp.bfloat16)


def solution(mesh):
    in_specs = (
        P(("dp", "ctx"), None),
        P("dp"),
        P("ctx", None),
        P("ctx", None),
        P("ctx", None),
        P(None, "ctx"),
    )
    out_specs = P(("dp", "ctx"), None)
    return jax.shard_map(
        on_device, mesh=mesh, in_specs=in_specs, out_specs=out_specs, check_vma=False
    )
```

```python
import functools
import math

import jax
import jax.numpy as jnp
from jax import lax
from jax.experimental import pallas as pl
from jax.experimental.pallas import tpu as pltpu
from jax.sharding import PartitionSpec as P

REACH = 8
ROPE_BASE = 500000.0
RING_LIMIT = 16
VMEM_LIMIT = 16 * 1024 * 1024
HALVED = True
PLAN = (
    "A0",
    "N0",
    "N1",
    "C0",
    "T0",
    "B0 N1",
    "H0 C0",
    "S0 N1",
    "N2",
    "C1 N1",
    "F1",
    "A1",
    "N3",
    "C2 N2 F1",
    "F2",
    "B1 N3",
    "X1",
    "N4 F2",
    "Q1 A1",
    "C3 N3 F2 Q1",
    "F3",
    "A2 N4",
    "F4",
    "Q2 B1",
    "C4 N4 Q2 F3",
    "K1",
    "K2 A2 Q2",
    "B2 N4",
    "X2 F4",
    "A3 C4 K2",
    "B3 C4",
    "K3 X1",
    "Q3 K3",
    "Q4 A3",
    "R0 X2",
    "R1",
    "R2",
    "X3",
    "A4 R0",
    "M0 X3 R2",
    "M1",
    "W1 M0",
    "W2",
    "W3",
    "O0",
    "W4",
    "O1",
)
MICROS = {}
PROJECTIONS = {
    "K1": (0, 2, False),
    "K2": (2, 4, False),
    "K3": (4, 5, True),
    "Q1": (0, 2, False),
    "Q2": (2, 3, False),
    "Q3": (3, 4, False),
    "Q4": (4, 5, True),
}
COLUMNS = ((0, 1, 2, 3), (4,))


def step_shards(turn, half):
    if turn == 0 or turn == half:
        return (f"A{turn}",)
    return (f"A{turn}", f"B{turn}", f"X{turn}")


def chip_at(place, chips):
    place = place % chips
    return jnp.where(place < chips // 2, 2 * place, 2 * (chips - 1 - place) + 1)


def static_chip_at(place, chips):
    place %= chips
    return 2 * place if place < chips // 2 else 2 * (chips - 1 - place) + 1


def ring_pairs(chips):
    pairs = []
    for place in range(chips):
        here = static_chip_at(place, chips)
        pairs.append((2 * here, 2 * static_chip_at(place + 1, chips)))
        pairs.append((2 * here + 1, 2 * static_chip_at(place - 1, chips) + 1))
    return pairs


def core_swap(value, count):
    return lax.ppermute(value, "ctx", [(i, i ^ 1) for i in range(count)])


def plane_swap(value):
    return lax.ppermute(value, "dp", [(0, 1), (1, 0)])


def row_device(row, column, count):
    pair = 2 * row + (column if row < count // 4 else 1 - column)
    return 2 * pair if pair < count // 2 else 2 * (count - 1 - pair) + 1


def after(value, *others):
    return lax.optimization_barrier((value, *others))[0]


def shard_owners(me, count):
    chips = count // 2
    half = chips // 2
    core, chip = me % 2, me // 2
    place = jnp.where(chip % 2 == 0, chip // 2, chips - 1 - chip // 2)
    way = jnp.where(core == 0, -1, 1)
    owners = [me]
    for step in range(1, half + 1):
        source = chip_at(place + way * step + chips, chips)
        owners.append(2 * source + core)
        if step < half:
            owners.append(2 * source + 1 - core)
    return owners


def params(**settings):
    return pltpu.CompilerParams(vmem_limit_bytes=VMEM_LIMIT, **settings)


def in_vmem(*arrays):
    return [pltpu.with_memory_space_constraint(array, pltpu.VMEM) for array in arrays]


def in_hbm(*arrays):
    return [pltpu.with_memory_space_constraint(array, pltpu.HBM) for array in arrays]


def estimate(micros):
    return pl.CostEstimate(flops=int(micros * 1.1535e9), bytes_accessed=0, transcendentals=0)


IN_VMEM = pl.BlockSpec(memory_space=pltpu.VMEM)
IN_HBM = pl.BlockSpec(memory_space=pl.ANY)
IN_SMEM = pl.BlockSpec(memory_space=pltpu.SMEM)


def rotate_kernel(head_dim, heads, kept_ref, came_ref, cos_ref, sin_ref, out_ref):
    cosine, sine = cos_ref[...], sin_ref[...]
    for column in range(0, kept_ref.shape[1], head_dim):
        span = pl.ds(column, head_dim)
        part = kept_ref[:, span] + came_ref[:, span]
        if column < heads * head_dim:
            part = part * cosine + pltpu.roll(part, head_dim // 2, 1) * sine
        out_ref[:, span] = part.astype(jnp.bfloat16)


def rotary_tables(positions, head_dim):
    frequency = ROPE_BASE ** (
        -(jnp.arange(head_dim // 2, dtype=jnp.float32) * 2.0) / head_dim
    )
    angles = positions.astype(jnp.float32)[:, None] * frequency[None, :]
    cosine, sine = jnp.cos(angles), jnp.sin(angles)
    return jnp.concatenate([cosine, cosine], axis=1), jnp.concatenate([-sine, sine], axis=1)


def rotate_sums(heads, kept, came, cosine, sine):
    return pl.pallas_call(
        functools.partial(rotate_kernel, cosine.shape[1], heads),
        out_shape=pltpu.VMEM(kept.shape, jnp.bfloat16),
        in_specs=[IN_VMEM] * 4,
        out_specs=IN_VMEM,
        compiler_params=params(),
        name="rotate_sums",
    )(*in_vmem(kept, came, cosine, sine))


def join_row_kernel(index_ref, own_ref, beside_ref, out_ref):
    odd = index_ref[2]
    out_ref[odd] = own_ref[...]
    out_ref[1 - odd] = beside_ref[...]


def join_row(index, own, beside):
    return pl.pallas_call(
        join_row_kernel,
        in_specs=[IN_SMEM, IN_VMEM, IN_VMEM],
        out_specs=IN_VMEM,
        out_shape=pltpu.VMEM((2, *own.shape), own.dtype),
        compiler_params=params(),
        name="join_row",
    )(index, *in_vmem(own, beside))


def attend_kernel(head_dim, reach, index_ref, query_ref, key_seg_ref, *refs):
    row_refs, (mixed_ref, window) = refs[:-2], refs[-2:]
    rows = query_ref.shape[0]
    for place, row_ref in enumerate(row_refs):
        window[2 * place : 2 * place + 2] = row_ref[...]
    odd = index_ref[2]
    own_seg = key_seg_ref[:, pl.ds(reach * rows, rows)]
    query_seg = jnp.transpose(jnp.broadcast_to(own_seg, (rows, rows)))
    base = lax.broadcasted_iota(jnp.int32, (rows, rows), 0)
    offset = lax.broadcasted_iota(jnp.int32, (rows, rows), 1)
    allowed = []
    for piece in range(reach + 1):
        same = query_seg == key_seg_ref[:, pl.ds(piece * rows, rows)]
        if piece == reach:
            same = same & (offset <= base)
        allowed.append(same)
    scale = math.log2(math.e) / math.sqrt(head_dim)
    for column in range(0, query_ref.shape[1], head_dim):
        span = pl.ds(column, head_dim)
        query = query_ref[:, span]
        scores = []
        for piece in range(reach + 1):
            score = lax.dot_general(
                query,
                window[odd + piece, :, :head_dim],
                (((1,), (1,)), ((), ())),
                preferred_element_type=jnp.float32,
            )
            scores.append(jnp.where(allowed[piece], score, -1e30))
        peak = scores[0]
        for score in scores[1:]:
            peak = jnp.maximum(peak, score)
        peak = jnp.max(peak, axis=1, keepdims=True)
        terms = [jnp.exp2((score - peak) * scale) for score in scores]
        total = terms[0]
        for term in terms[1:]:
            total = total + term
        mixed = jnp.zeros((rows, head_dim), jnp.float32)
        for piece in range(reach + 1):
            mixed += jnp.dot(
                terms[piece].astype(jnp.bfloat16),
                window[odd + piece, :, head_dim:],
                preferred_element_type=jnp.float32,
            )
        mixed = mixed / jnp.sum(total, axis=1, keepdims=True)
        mixed_ref[:, span] = mixed.astype(jnp.bfloat16)


def attend(index, queries, row_windows, key_seg, head_dim, micros):
    reach = 2 * len(row_windows) - 2
    rows = queries.shape[0]
    return pl.pallas_call(
        functools.partial(attend_kernel, head_dim, reach),
        out_shape=pltpu.VMEM(queries.shape, jnp.bfloat16),
        in_specs=[IN_SMEM] + [IN_VMEM] * (2 + len(row_windows)),
        out_specs=IN_VMEM,
        scratch_shapes=[pltpu.VMEM((reach + 2, rows, 2 * head_dim), jnp.bfloat16)],
        compiler_params=params(),
        cost_estimate=estimate(micros),
        name="attend",
    )(index, *in_vmem(queries, key_seg, *row_windows))


def lay_out_kernel(plane_ref, query_ref, key_ref, value_ref, near_out, far_out, common_out, sems):
    q_half, kv_half = near_out.shape[2], common_out.shape[2] // 2
    near = pl.ds(pl.multiple_of(plane_ref[0] * q_half, q_half), q_half)
    far = pl.ds(pl.multiple_of((1 - plane_ref[0]) * q_half, q_half), q_half)
    moves = (
        (key_ref, common_out.at[0, :, :kv_half]),
        (value_ref, common_out.at[0, :, kv_half:]),
        (query_ref.at[:, near], near_out.at[0]),
        (query_ref.at[:, far], far_out.at[0]),
    )
    copies = [
        pltpu.make_async_copy(source, target, sems.at[place])
        for place, (source, target) in enumerate(moves)
    ]
    for copy in copies:
        copy.start()
    for copy in copies:
        copy.wait()


def lay_out(plane, query, key, value):
    depth, q_half = query.shape[0], query.shape[1] // 2
    shapes = ((1, depth, q_half), (1, depth, q_half), (1, depth, 2 * key.shape[1]))
    return pl.pallas_call(
        lay_out_kernel,
        in_specs=[IN_SMEM] + [IN_HBM] * 3,
        out_specs=[IN_VMEM] * 3,
        scratch_shapes=[pltpu.SemaphoreType.DMA((4,))],
        out_shape=[pltpu.VMEM(shape, jnp.bfloat16) for shape in shapes],
        compiler_params=params(),
        name="lay_out",
    )(plane, *in_hbm(query, key, value))


def rows_near_kernel(plane_ref, weight_ref, out_ref):
    half = out_ref.shape[0]
    near = pl.ds(pl.multiple_of(plane_ref[0] * half, half), half)
    out_ref[...] = weight_ref[near, :]


def rows_near_of(plane, weight):
    rows, columns = weight.shape
    return pl.pallas_call(
        rows_near_kernel,
        in_specs=[IN_SMEM, IN_VMEM],
        out_specs=IN_VMEM,
        out_shape=pltpu.VMEM((rows // 2, columns), weight.dtype),
        compiler_params=params(),
        name="rows_near",
    )(plane, *in_vmem(weight))


def both_kernel(first_ref, second_ref, out_ref):
    out_ref[0] = first_ref[0]
    out_ref[1] = second_ref[0]


def both_of(first, second):
    return pl.pallas_call(
        both_kernel,
        in_specs=[IN_VMEM] * 2,
        out_specs=IN_VMEM,
        out_shape=pltpu.VMEM((2, *first.shape[1:]), first.dtype),
        compiler_params=params(),
        name="both_of",
    )(*in_vmem(first, second))


def first_kernel(pair_ref, out_ref):
    out_ref[...] = pair_ref[:1]


def first_of(pair):
    return pl.pallas_call(
        first_kernel,
        in_specs=[IN_VMEM],
        out_specs=IN_VMEM,
        out_shape=pltpu.VMEM((1, *pair.shape[1:]), pair.dtype),
        compiler_params=params(),
        name="first_of",
    )(*in_vmem(pair))


def bring_kernel(source_ref, out_ref, sem):
    copy = pltpu.make_async_copy(source_ref, out_ref, sem)
    copy.start()
    copy.wait()


def bring(tokens, micros):
    return pl.pallas_call(
        bring_kernel,
        in_specs=[IN_HBM],
        out_specs=IN_VMEM,
        scratch_shapes=[pltpu.SemaphoreType.DMA],
        out_shape=pltpu.VMEM(tokens.shape, tokens.dtype),
        compiler_params=params(),
        cost_estimate=estimate(micros),
        name="bring",
    )(*in_hbm(tokens))


def project_kernel(slots, base, groups, first, last, index_ref, own_ref, other_ref, *refs):
    held_weights = groups * (1 + slots[-1][0])
    weights, refs = refs[:held_weights], refs[held_weights:]
    total_ref, refs = (None, refs) if first else (refs[0], refs[1:])
    rows = own_ref.shape[0]
    depth, width = weights[0].shape[-2:]
    block = rows // 2
    spans = [
        pl.ds(pl.multiple_of(index_ref[3 + base + place] * depth, depth), depth)
        for place in range(len(slots))
    ]
    out_ref = refs[2] if last else refs[0]
    for side, source_ref in enumerate((own_ref, other_ref)):
        for group in range(groups):
            columns = pl.ds(group * width, width)
            total = None if first else total_ref[side, :, columns]
            for place, (step, slot) in enumerate(slots):
                product = jnp.dot(
                    source_ref[:, spans[place]],
                    weights[groups * step + group][slot],
                    preferred_element_type=jnp.float32,
                )
                total = product if total is None else total + product
            out_ref[side, :, columns] = total
    if last:
        kept_ref, sent_ref, held = refs
        mine = pl.ds(pl.multiple_of(index_ref[0] * block, block), block)
        others = pl.ds(pl.multiple_of((1 - index_ref[0]) * block, block), block)
        kept_ref[:block] = held[0, mine, :]
        kept_ref[block:] = held[1, mine, :]
        sent_ref[:block] = held[1, others, :]
        sent_ref[block:] = held[0, others, :]


def project(index, base, tokens, steps, total, last, micros):
    groups = len(steps[0][1])
    slots = [(i, slot) for i, (used, _) in enumerate(steps) for slot in range(used)]
    rows = tokens[0].shape[0]
    columns = sum(part.shape[2] for part in steps[0][1])
    operands = in_vmem(*tokens, *(part for _, parts in steps for part in parts))
    if total is not None:
        operands += in_vmem(total)
    shapes = ((rows, columns), (rows, columns)) if last else ((2, rows, columns),)
    out = pl.pallas_call(
        functools.partial(project_kernel, slots, base, groups, total is None, last),
        in_specs=[IN_SMEM] + [IN_VMEM] * len(operands),
        out_specs=[IN_VMEM] * len(shapes),
        scratch_shapes=[pltpu.VMEM((2, rows, columns), jnp.float32)] if last else [],
        out_shape=[pltpu.VMEM(shape, jnp.float32) for shape in shapes],
        compiler_params=params(),
        cost_estimate=estimate(micros),
        name="project",
    )(index, *operands)
    return out if last else out[0]


def columns_kernel(entries, index_ref, mixed_ref, returned_ref, *refs):
    weights = list(refs[: sum(parts for _, parts in entries)])
    out_ref, held, sems = refs[-3:]
    block = mixed_ref.shape[0] // 2
    half = mixed_ref.shape[1] // 2
    width = weights[0].shape[-1]
    mine = pl.ds(pl.multiple_of(index_ref[0] * block, block), block)
    others = pl.ds(pl.multiple_of((1 - index_ref[0]) * block, block), block)
    near = pl.ds(pl.multiple_of(index_ref[1] * half, half), half)
    far = pl.ds(pl.multiple_of((1 - index_ref[1]) * half, half), half)
    rows_in = jnp.concatenate([mixed_ref[:block], returned_ref[block:]], axis=0)
    near_in, far_in = rows_in[:, :half], rows_in[:, half:]
    copies = []
    for place, (owner, parts) in enumerate(entries):
        if parts == 1:
            whole = weights.pop(0)
            low, high = whole[near, :], whole[far, :]
        else:
            low, high = weights.pop(0)[...], weights.pop(0)[...]
        value = jnp.dot(near_in, low, preferred_element_type=jnp.float32)
        value += jnp.dot(far_in, high, preferred_element_type=jnp.float32)
        value = value.astype(jnp.bfloat16)
        columns = pl.ds(place * width, width)
        held[mine, columns] = value[:block]
        held[others, columns] = value[block:]
        column = pl.multiple_of(index_ref[owner] * width, width)
        copy = pltpu.make_async_copy(
            held.at[:, columns], out_ref.at[:, pl.ds(column, width)], sems.at[place]
        )
        copy.start()
        copies.append(copy)
    for copy in copies:
        copy.wait()


def columns_of(index, mixed, returned, shards, result, width, micros):
    rows = mixed.shape[0]
    out_cols = shards[0][1][0].shape[-1]
    entries = [(owner, len(parts)) for owner, parts in shards]
    operands = in_vmem(mixed, returned, *(part for _, parts in shards for part in parts))
    specs = [IN_SMEM] + [IN_VMEM] * len(operands)
    if result is not None:
        operands += in_hbm(result)
        specs.append(IN_HBM)
    return pl.pallas_call(
        functools.partial(columns_kernel, entries),
        in_specs=specs,
        out_specs=IN_HBM,
        scratch_shapes=[
            pltpu.VMEM((rows, len(shards) * out_cols), jnp.bfloat16),
            pltpu.SemaphoreType.DMA((len(shards),)),
        ],
        out_shape=pltpu.HBM((rows, width), jnp.bfloat16),
        input_output_aliases={} if result is None else {len(operands): 0},
        compiler_params=params(),
        cost_estimate=estimate(micros),
        name="columns_of",
    )(index, *operands)


def on_device(hidden_in, segment_ids, w_query, w_key, w_value, w_out):
    count = lax.axis_size("ctx")
    me = lax.axis_index("ctx")
    plane = lax.axis_index("dp")
    core, chip = me % 2, me // 2
    rows, width = hidden_in.shape
    block = rows // 2
    head_dim = w_key.shape[1]
    q_rows, out_cols = w_out.shape

    reach = REACH * block // rows
    pair = jnp.where(core == 0, chip, count - 1 - chip)
    pair_pos = pair * rows + jnp.arange(rows, dtype=jnp.int32)
    cosine, sine = rotary_tables(pair_pos, head_dim)
    seg_blocks = segment_ids.reshape(2 * count, block)
    seq_block = pair * 2 - 2 * reach + jnp.arange(2 * reach + 2, dtype=jnp.int32)
    clipped = jnp.maximum(seq_block, 0)
    stored = jnp.where(clipped < count, 2 * clipped, 2 * (2 * count - 1 - clipped) + 1)
    seg_rows = seg_blocks[stored]
    key_seg = jnp.where(seq_block[:, None] >= 0, seg_rows, -1).reshape(1, -1)
    tables = (cosine, sine, cosine, sine, key_seg)
    index = [core, plane, pair % 2]

    def row_windows(joined):
        sends = [(device, device ^ 2) for device in range(count)]
        own_row = join_row(index, joined, lax.ppermute(joined, "ctx", sends))
        windows = []
        for back in range(1, reach // 2 + 1):
            sends = [
                (row_device(row, column, count), row_device(row + back, column, count))
                for row in range(count // 2 - back)
                for column in range(2)
            ]
            windows.append(lax.ppermute(own_row, "ctx", sends))
        return own_row, windows

    ringed = count <= RING_LIMIT
    if ringed:
        plane_index = plane.reshape(1).astype(jnp.int32)
        pairs = ring_pairs(count // 2)
        half = count // 4
        owners = shard_owners(me, count)
        index += [*owners, *shard_owners(me ^ 1, count)]
        index = jnp.stack(index).astype(jnp.int32)

        def ring(value):
            return lax.ppermute(value, "ctx", pairs)

        def add_projections(total, steps, begin, end, last=False):
            base = 0 if begin == 0 else 2 * begin - 1
            return project(index, base, (hidden_in, other), steps[begin:end], total, last)

        own_near, own_far, own_common = lay_out(plane_index, w_query, w_key, w_value)
        done = {"w_out": w_out}
        common_steps = [(1, (own_common,))]
        query_steps = [(1, (own_near, own_far))]

        def run(name, *ties):
            nonlocal index, cosine, sine, query_cosine, query_sine, key_seg

            def tied(value):
                return after(value, *(done[tie] for tie in ties)) if ties else value

            kind, step = name[:-1], int(name[-1])
            micros = MICROS.get(kind, 2)
            if name == "T0":
                first, index, cosine, sine, query_cosine, query_sine, key_seg = (
                    lax.optimization_barrier(
                        (done["C0"], index, cosine, sine, query_cosine, query_sine, key_seg)
                    )
                )
                done["C0"] = value = first
            elif name == "C0":
                value = both_of(own_common, core_swap(tied(own_common), count))
            elif name == "N0":
                value = both_of(own_near, core_swap(tied(own_near), count))
            elif name == "S0":
                value = core_swap(tied(done["H0"]), count)
            elif name == "H0":
                value = bring(tied(hidden_in), micros)
            elif name == "B0":
                done["W0"] = (core_swap(tied(w_out), count),)
                value = done["W0"][0]
                if HALVED:
                    value = rows_near_of(plane_index, value)
            elif name == "A0":
                value = w_out
            elif kind in ("C", "N"):
                value = done[f"{kind}{step - 1}"]
                value = ring(tied(first_of(value) if step == half else value))
                if kind == "C":
                    common_steps.append((value.shape[0], (value,)))
            elif kind == "F":
                near = done[f"N{step}"]
                value = plane_swap(tied(near))
                query_steps.append((near.shape[0], (near, value)))
            elif kind in ("A", "B"):
                value = ring(tied(done[f"{kind}{step - 1}"]))
            elif kind == "X":
                value = plane_swap(tied(done[f"B{step}"]))
            elif kind in ("K", "Q"):
                begin, end, last = PROJECTIONS[name]
                steps = list(common_steps if kind == "K" else query_steps)
                if ties:
                    used, parts = steps[begin]
                    steps[begin] = (used, (tied(parts[0]), *parts[1:]))
                value = project(
                    index,
                    0 if begin == 0 else 2 * begin - 1,
                    (done["H0"], done["S0"]),
                    steps[begin:end],
                    done.get(f"{kind}{step - 1}"),
                    last,
                    micros,
                )
                if last:
                    kept, sent = value
                    came = core_swap(sent, count)
                    if kind == "K":
                        value = rotate_sums(1, kept, came, cosine, sine)
                    else:
                        value = rotate_sums(
                            q_rows // head_dim, kept, came, query_cosine, query_sine
                        )
            elif name == "R0":
                sends = [(device, device ^ 2) for device in range(count)]
                joined = done["K3"]
                value = join_row(index, joined, lax.ppermute(tied(joined), "ctx", sends))
            elif kind == "R":
                sends = [
                    (row_device(row, column, count), row_device(row + step, column, count))
                    for row in range(count // 2 - step)
                    for column in range(2)
                ]
                value = lax.ppermute(tied(done["R0"]), "ctx", sends)
            elif name == "M0":
                windows = [done["R2"], done["R1"], done["R0"]]
                value = attend(index, tied(done["Q4"]), windows, key_seg, head_dim, micros)
            elif name == "M1":
                value = core_swap(done["M0"], count)
            elif kind == "W":
                value = [core_swap(tied(done[f"A{step}"]), count)]
                if step < half:
                    value.append(core_swap(done[f"B{step}"], count))
                    value.append(core_swap(done[f"X{step}"], count))
            elif kind == "O":
                shards = []
                for turn in COLUMNS[step]:
                    for base, held in (
                        (3, [done[key] for key in step_shards(turn, half)]),
                        (3 + 2 * half, done[f"W{turn}"]),
                    ):
                        place = base + (2 * turn - 1 if turn else 0)
                        shards.append((place, held[:1]))
                        if len(held) > 1:
                            shards.append((place + 1, held[1:]))
                value = columns_of(
                    index,
                    done["M0"],
                    tied(done["M1"]),
                    shards,
                    done.get("O0"),
                    width,
                    micros,
                )
            done[name] = value

        cosine, sine, query_cosine, query_sine, key_seg = tables
        for entry in PLAN:
            run(*entry.split())
        return done["O1"]
    else:
        index = jnp.stack(index).astype(jnp.int32)
        cosine, sine, query_cosine, query_sine, key_seg = tables
        gathered = lax.all_gather(
            jnp.concatenate([w_key, w_value, w_query], axis=1), "ctx", axis=0, tiled=True
        )
        ordered = jnp.where(core == 0, hidden_in, jnp.roll(hidden_in, block, axis=0))
        pair_tokens = jnp.concatenate([ordered[:block], core_swap(ordered[block:], count)], axis=0)
        sums = jnp.dot(pair_tokens, gathered, preferred_element_type=jnp.float32)
        kv_sums, query_sums = sums[:, : 2 * head_dim], sums[:, 2 * head_dim :]
        joined = rotate_sums(1, kv_sums, jnp.zeros_like(kv_sums), cosine, sine)
        queries = rotate_sums(
            q_rows // head_dim, query_sums, jnp.zeros_like(query_sums), query_cosine, query_sine
        )
        own_row, windows = row_windows(joined)

    mixed = attend(index, queries, [*windows[::-1], own_row], key_seg, head_dim, 4)
    returned = core_swap(mixed, count)
    kinds = (mixed[:block], returned[block:])
    own_rows = jnp.where(
        core == 0, jnp.concatenate(kinds, axis=0), jnp.concatenate(kinds[::-1], axis=0)
    )
    gathered = lax.all_gather(w_out, "ctx", axis=1, tiled=True)
    return jnp.dot(own_rows, gathered, preferred_element_type=jnp.float32).astype(jnp.bfloat16)


def solution(mesh):
    in_specs = (
        P(("dp", "ctx"), None),
        P("dp"),
        P("ctx", None),
        P("ctx", None),
        P("ctx", None),
        P(None, "ctx"),
    )
    out_specs = P(("dp", "ctx"), None)
    return jax.shard_map(
        on_device, mesh=mesh, in_specs=in_specs, out_specs=out_specs, check_vma=False
    )
```

```python
import functools
import math

import jax
import jax.numpy as jnp
from jax import lax
from jax.experimental import pallas as pl
from jax.experimental.pallas import tpu as pltpu
from jax.sharding import PartitionSpec as P

REACH = 8
ROPE_BASE = 500000.0
RING_LIMIT = 16
VMEM_LIMIT = 16 * 1024 * 1024
HALVED = True
PLAN = (
    "A0",
    "N0",
    "N1",
    "C0 N0",
    "T0",
    "B0 N1",
    "H0 C0",
    "S0 N1",
    "N2",
    "C1 N1",
    "F1",
    "A1",
    "N3 S0",
    "C2 N2 F1 N1",
    "F2",
    "B1 N3",
    "X1",
    "N4",
    "Q1",
    "C3 N3 F2 Q1",
    "F3",
    "A2 N4",
    "K1 F2",
    "F4",
    "Q2 B1",
    "C4 N4 Q2 F3",
    "K2 A2 Q2",
    "B2 N4",
    "X2 F4",
    "A3 C4 K2",
    "B3",
    "K3 X1",
    "Q3 K3",
    "Q4 A3",
    "R0 X2 Q3",
    "R1",
    "R2",
    "X3",
    "A4 R0",
    "M0 X3 R2",
    "M1",
    "W1 M0",
    "W2",
    "W3",
    "O0",
    "W4",
    "O1",
)
MICROS = {}
PROJECTIONS = {
    "K1": (0, 2, False),
    "K2": (2, 4, False),
    "K3": (4, 5, True),
    "Q1": (0, 2, False),
    "Q2": (2, 3, False),
    "Q3": (3, 4, False),
    "Q4": (4, 5, True),
}
COLUMNS = ((0, 1, 2, 3), (4,))


def step_shards(turn, half):
    if turn == 0 or turn == half:
        return (f"A{turn}",)
    return (f"A{turn}", f"B{turn}", f"X{turn}")


def chip_at(place, chips):
    place = place % chips
    return jnp.where(place < chips // 2, 2 * place, 2 * (chips - 1 - place) + 1)


def static_chip_at(place, chips):
    place %= chips
    return 2 * place if place < chips // 2 else 2 * (chips - 1 - place) + 1


def ring_pairs(chips):
    pairs = []
    for place in range(chips):
        here = static_chip_at(place, chips)
        pairs.append((2 * here, 2 * static_chip_at(place + 1, chips)))
        pairs.append((2 * here + 1, 2 * static_chip_at(place - 1, chips) + 1))
    return pairs


def core_swap(value, count):
    return lax.ppermute(value, "ctx", [(i, i ^ 1) for i in range(count)])


def plane_swap(value):
    return lax.ppermute(value, "dp", [(0, 1), (1, 0)])


def row_device(row, column, count):
    pair = 2 * row + (column if row < count // 4 else 1 - column)
    return 2 * pair if pair < count // 2 else 2 * (count - 1 - pair) + 1


def after(value, *others):
    return lax.optimization_barrier((value, *others))[0]


def shard_owners(me, count):
    chips = count // 2
    half = chips // 2
    core, chip = me % 2, me // 2
    place = jnp.where(chip % 2 == 0, chip // 2, chips - 1 - chip // 2)
    way = jnp.where(core == 0, -1, 1)
    owners = [me]
    for step in range(1, half + 1):
        source = chip_at(place + way * step + chips, chips)
        owners.append(2 * source + core)
        if step < half:
            owners.append(2 * source + 1 - core)
    return owners


def params(**settings):
    return pltpu.CompilerParams(vmem_limit_bytes=VMEM_LIMIT, **settings)


def in_vmem(*arrays):
    return [pltpu.with_memory_space_constraint(array, pltpu.VMEM) for array in arrays]


def in_hbm(*arrays):
    return [pltpu.with_memory_space_constraint(array, pltpu.HBM) for array in arrays]


def estimate(micros):
    return pl.CostEstimate(flops=int(micros * 1.1535e9), bytes_accessed=0, transcendentals=0)


IN_VMEM = pl.BlockSpec(memory_space=pltpu.VMEM)
IN_HBM = pl.BlockSpec(memory_space=pl.ANY)
IN_SMEM = pl.BlockSpec(memory_space=pltpu.SMEM)


def rotate_kernel(head_dim, heads, kept_ref, came_ref, cos_ref, sin_ref, out_ref):
    cosine, sine = cos_ref[...], sin_ref[...]
    for column in range(0, kept_ref.shape[1], head_dim):
        span = pl.ds(column, head_dim)
        part = kept_ref[:, span] + came_ref[:, span]
        if column < heads * head_dim:
            part = part * cosine + pltpu.roll(part, head_dim // 2, 1) * sine
        out_ref[:, span] = part.astype(jnp.bfloat16)


def rotary_tables(positions, head_dim):
    frequency = ROPE_BASE ** (
        -(jnp.arange(head_dim // 2, dtype=jnp.float32) * 2.0) / head_dim
    )
    angles = positions.astype(jnp.float32)[:, None] * frequency[None, :]
    cosine, sine = jnp.cos(angles), jnp.sin(angles)
    return jnp.concatenate([cosine, cosine], axis=1), jnp.concatenate([-sine, sine], axis=1)


def rotate_sums(heads, kept, came, cosine, sine):
    return pl.pallas_call(
        functools.partial(rotate_kernel, cosine.shape[1], heads),
        out_shape=pltpu.VMEM(kept.shape, jnp.bfloat16),
        in_specs=[IN_VMEM] * 4,
        out_specs=IN_VMEM,
        compiler_params=params(),
        name="rotate_sums",
    )(*in_vmem(kept, came, cosine, sine))


def join_row_kernel(index_ref, own_ref, beside_ref, out_ref):
    odd = index_ref[2]
    out_ref[odd] = own_ref[...]
    out_ref[1 - odd] = beside_ref[...]


def join_row(index, own, beside):
    return pl.pallas_call(
        join_row_kernel,
        in_specs=[IN_SMEM, IN_VMEM, IN_VMEM],
        out_specs=IN_VMEM,
        out_shape=pltpu.VMEM((2, *own.shape), own.dtype),
        compiler_params=params(),
        name="join_row",
    )(index, *in_vmem(own, beside))


def attend_kernel(head_dim, reach, index_ref, query_ref, key_seg_ref, *refs):
    row_refs, (mixed_ref, window) = refs[:-2], refs[-2:]
    rows = query_ref.shape[0]
    for place, row_ref in enumerate(row_refs):
        window[2 * place : 2 * place + 2] = row_ref[...]
    odd = index_ref[2]
    own_seg = key_seg_ref[:, pl.ds(reach * rows, rows)]
    query_seg = jnp.transpose(jnp.broadcast_to(own_seg, (rows, rows)))
    base = lax.broadcasted_iota(jnp.int32, (rows, rows), 0)
    offset = lax.broadcasted_iota(jnp.int32, (rows, rows), 1)
    allowed = []
    for piece in range(reach + 1):
        same = query_seg == key_seg_ref[:, pl.ds(piece * rows, rows)]
        if piece == reach:
            same = same & (offset <= base)
        allowed.append(same)
    scale = math.log2(math.e) / math.sqrt(head_dim)
    for column in range(0, query_ref.shape[1], head_dim):
        span = pl.ds(column, head_dim)
        query = query_ref[:, span]
        scores = []
        for piece in range(reach + 1):
            score = lax.dot_general(
                query,
                window[odd + piece, :, :head_dim],
                (((1,), (1,)), ((), ())),
                preferred_element_type=jnp.float32,
            )
            scores.append(jnp.where(allowed[piece], score, -1e30))
        peak = scores[0]
        for score in scores[1:]:
            peak = jnp.maximum(peak, score)
        peak = jnp.max(peak, axis=1, keepdims=True)
        terms = [jnp.exp2((score - peak) * scale) for score in scores]
        total = terms[0]
        for term in terms[1:]:
            total = total + term
        mixed = jnp.zeros((rows, head_dim), jnp.float32)
        for piece in range(reach + 1):
            mixed += jnp.dot(
                terms[piece].astype(jnp.bfloat16),
                window[odd + piece, :, head_dim:],
                preferred_element_type=jnp.float32,
            )
        mixed = mixed / jnp.sum(total, axis=1, keepdims=True)
        mixed_ref[:, span] = mixed.astype(jnp.bfloat16)


def attend(index, queries, row_windows, key_seg, head_dim, micros):
    reach = 2 * len(row_windows) - 2
    rows = queries.shape[0]
    return pl.pallas_call(
        functools.partial(attend_kernel, head_dim, reach),
        out_shape=pltpu.VMEM(queries.shape, jnp.bfloat16),
        in_specs=[IN_SMEM] + [IN_VMEM] * (2 + len(row_windows)),
        out_specs=IN_VMEM,
        scratch_shapes=[pltpu.VMEM((reach + 2, rows, 2 * head_dim), jnp.bfloat16)],
        compiler_params=params(),
        cost_estimate=estimate(micros),
        name="attend",
    )(index, *in_vmem(queries, key_seg, *row_windows))


def lay_out_kernel(plane_ref, query_ref, key_ref, value_ref, near_out, far_out, common_out, sems):
    q_half, kv_half = near_out.shape[2], common_out.shape[2] // 2
    near = pl.ds(pl.multiple_of(plane_ref[0] * q_half, q_half), q_half)
    far = pl.ds(pl.multiple_of((1 - plane_ref[0]) * q_half, q_half), q_half)
    moves = (
        (key_ref, common_out.at[0, :, :kv_half]),
        (value_ref, common_out.at[0, :, kv_half:]),
        (query_ref.at[:, near], near_out.at[0]),
        (query_ref.at[:, far], far_out.at[0]),
    )
    copies = [
        pltpu.make_async_copy(source, target, sems.at[place])
        for place, (source, target) in enumerate(moves)
    ]
    for copy in copies:
        copy.start()
    for copy in copies:
        copy.wait()


def lay_out(plane, query, key, value):
    depth, q_half = query.shape[0], query.shape[1] // 2
    shapes = ((1, depth, q_half), (1, depth, q_half), (1, depth, 2 * key.shape[1]))
    return pl.pallas_call(
        lay_out_kernel,
        in_specs=[IN_SMEM] + [IN_HBM] * 3,
        out_specs=[IN_VMEM] * 3,
        scratch_shapes=[pltpu.SemaphoreType.DMA((4,))],
        out_shape=[pltpu.VMEM(shape, jnp.bfloat16) for shape in shapes],
        compiler_params=params(),
        name="lay_out",
    )(plane, *in_hbm(query, key, value))


def rows_near_kernel(plane_ref, weight_ref, out_ref):
    half = out_ref.shape[0]
    near = pl.ds(pl.multiple_of(plane_ref[0] * half, half), half)
    out_ref[...] = weight_ref[near, :]


def rows_near_of(plane, weight):
    rows, columns = weight.shape
    return pl.pallas_call(
        rows_near_kernel,
        in_specs=[IN_SMEM, IN_VMEM],
        out_specs=IN_VMEM,
        out_shape=pltpu.VMEM((rows // 2, columns), weight.dtype),
        compiler_params=params(),
        name="rows_near",
    )(plane, *in_vmem(weight))


def both_kernel(first_ref, second_ref, out_ref):
    out_ref[0] = first_ref[0]
    out_ref[1] = second_ref[0]


def both_of(first, second):
    return pl.pallas_call(
        both_kernel,
        in_specs=[IN_VMEM] * 2,
        out_specs=IN_VMEM,
        out_shape=pltpu.VMEM((2, *first.shape[1:]), first.dtype),
        compiler_params=params(),
        name="both_of",
    )(*in_vmem(first, second))


def first_kernel(pair_ref, out_ref):
    out_ref[...] = pair_ref[:1]


def first_of(pair):
    return pl.pallas_call(
        first_kernel,
        in_specs=[IN_VMEM],
        out_specs=IN_VMEM,
        out_shape=pltpu.VMEM((1, *pair.shape[1:]), pair.dtype),
        compiler_params=params(),
        name="first_of",
    )(*in_vmem(pair))


def bring_kernel(source_ref, out_ref, sem):
    copy = pltpu.make_async_copy(source_ref, out_ref, sem)
    copy.start()
    copy.wait()


def bring(tokens, micros):
    return pl.pallas_call(
        bring_kernel,
        in_specs=[IN_HBM],
        out_specs=IN_VMEM,
        scratch_shapes=[pltpu.SemaphoreType.DMA],
        out_shape=pltpu.VMEM(tokens.shape, tokens.dtype),
        compiler_params=params(),
        cost_estimate=estimate(micros),
        name="bring",
    )(*in_hbm(tokens))


def project_kernel(slots, base, groups, first, last, index_ref, own_ref, other_ref, *refs):
    held_weights = groups * (1 + slots[-1][0])
    weights, refs = refs[:held_weights], refs[held_weights:]
    total_ref, refs = (None, refs) if first else (refs[0], refs[1:])
    rows = own_ref.shape[0]
    depth, width = weights[0].shape[-2:]
    block = rows // 2
    spans = [
        pl.ds(pl.multiple_of(index_ref[3 + base + place] * depth, depth), depth)
        for place in range(len(slots))
    ]
    out_ref = refs[2] if last else refs[0]
    for side, source_ref in enumerate((own_ref, other_ref)):
        for group in range(groups):
            columns = pl.ds(group * width, width)
            total = None if first else total_ref[side, :, columns]
            for place, (step, slot) in enumerate(slots):
                product = jnp.dot(
                    source_ref[:, spans[place]],
                    weights[groups * step + group][slot],
                    preferred_element_type=jnp.float32,
                )
                total = product if total is None else total + product
            out_ref[side, :, columns] = total
    if last:
        kept_ref, sent_ref, held = refs
        mine = pl.ds(pl.multiple_of(index_ref[0] * block, block), block)
        others = pl.ds(pl.multiple_of((1 - index_ref[0]) * block, block), block)
        kept_ref[:block] = held[0, mine, :]
        kept_ref[block:] = held[1, mine, :]
        sent_ref[:block] = held[1, others, :]
        sent_ref[block:] = held[0, others, :]


def project(index, base, tokens, steps, total, last, micros):
    groups = len(steps[0][1])
    slots = [(i, slot) for i, (used, _) in enumerate(steps) for slot in range(used)]
    rows = tokens[0].shape[0]
    columns = sum(part.shape[2] for part in steps[0][1])
    operands = in_vmem(*tokens, *(part for _, parts in steps for part in parts))
    if total is not None:
        operands += in_vmem(total)
    shapes = ((rows, columns), (rows, columns)) if last else ((2, rows, columns),)
    out = pl.pallas_call(
        functools.partial(project_kernel, slots, base, groups, total is None, last),
        in_specs=[IN_SMEM] + [IN_VMEM] * len(operands),
        out_specs=[IN_VMEM] * len(shapes),
        scratch_shapes=[pltpu.VMEM((2, rows, columns), jnp.float32)] if last else [],
        out_shape=[pltpu.VMEM(shape, jnp.float32) for shape in shapes],
        compiler_params=params(),
        cost_estimate=estimate(micros),
        name="project",
    )(index, *operands)
    return out if last else out[0]


def columns_kernel(entries, index_ref, mixed_ref, returned_ref, *refs):
    weights = list(refs[: sum(parts for _, parts in entries)])
    out_ref, held, sems = refs[-3:]
    block = mixed_ref.shape[0] // 2
    half = mixed_ref.shape[1] // 2
    width = weights[0].shape[-1]
    mine = pl.ds(pl.multiple_of(index_ref[0] * block, block), block)
    others = pl.ds(pl.multiple_of((1 - index_ref[0]) * block, block), block)
    near = pl.ds(pl.multiple_of(index_ref[1] * half, half), half)
    far = pl.ds(pl.multiple_of((1 - index_ref[1]) * half, half), half)
    rows_in = jnp.concatenate([mixed_ref[:block], returned_ref[block:]], axis=0)
    near_in, far_in = rows_in[:, :half], rows_in[:, half:]
    copies = []
    for place, (owner, parts) in enumerate(entries):
        if parts == 1:
            whole = weights.pop(0)
            low, high = whole[near, :], whole[far, :]
        else:
            low, high = weights.pop(0)[...], weights.pop(0)[...]
        value = jnp.dot(near_in, low, preferred_element_type=jnp.float32)
        value += jnp.dot(far_in, high, preferred_element_type=jnp.float32)
        value = value.astype(jnp.bfloat16)
        columns = pl.ds(place * width, width)
        held[mine, columns] = value[:block]
        held[others, columns] = value[block:]
        column = pl.multiple_of(index_ref[owner] * width, width)
        copy = pltpu.make_async_copy(
            held.at[:, columns], out_ref.at[:, pl.ds(column, width)], sems.at[place]
        )
        copy.start()
        copies.append(copy)
    for copy in copies:
        copy.wait()


def columns_of(index, mixed, returned, shards, result, width, micros):
    rows = mixed.shape[0]
    out_cols = shards[0][1][0].shape[-1]
    entries = [(owner, len(parts)) for owner, parts in shards]
    operands = in_vmem(mixed, returned, *(part for _, parts in shards for part in parts))
    specs = [IN_SMEM] + [IN_VMEM] * len(operands)
    if result is not None:
        operands += in_hbm(result)
        specs.append(IN_HBM)
    return pl.pallas_call(
        functools.partial(columns_kernel, entries),
        in_specs=specs,
        out_specs=IN_HBM,
        scratch_shapes=[
            pltpu.VMEM((rows, len(shards) * out_cols), jnp.bfloat16),
            pltpu.SemaphoreType.DMA((len(shards),)),
        ],
        out_shape=pltpu.HBM((rows, width), jnp.bfloat16),
        input_output_aliases={} if result is None else {len(operands): 0},
        compiler_params=params(),
        cost_estimate=estimate(micros),
        name="columns_of",
    )(index, *operands)


def on_device(hidden_in, segment_ids, w_query, w_key, w_value, w_out):
    count = lax.axis_size("ctx")
    me = lax.axis_index("ctx")
    plane = lax.axis_index("dp")
    core, chip = me % 2, me // 2
    rows, width = hidden_in.shape
    block = rows // 2
    head_dim = w_key.shape[1]
    q_rows, out_cols = w_out.shape

    reach = REACH * block // rows
    pair = jnp.where(core == 0, chip, count - 1 - chip)
    pair_pos = pair * rows + jnp.arange(rows, dtype=jnp.int32)
    cosine, sine = rotary_tables(pair_pos, head_dim)
    seg_blocks = segment_ids.reshape(2 * count, block)
    seq_block = pair * 2 - 2 * reach + jnp.arange(2 * reach + 2, dtype=jnp.int32)
    clipped = jnp.maximum(seq_block, 0)
    stored = jnp.where(clipped < count, 2 * clipped, 2 * (2 * count - 1 - clipped) + 1)
    seg_rows = seg_blocks[stored]
    key_seg = jnp.where(seq_block[:, None] >= 0, seg_rows, -1).reshape(1, -1)
    tables = (cosine, sine, cosine, sine, key_seg)
    index = [core, plane, pair % 2]

    def row_windows(joined):
        sends = [(device, device ^ 2) for device in range(count)]
        own_row = join_row(index, joined, lax.ppermute(joined, "ctx", sends))
        windows = []
        for back in range(1, reach // 2 + 1):
            sends = [
                (row_device(row, column, count), row_device(row + back, column, count))
                for row in range(count // 2 - back)
                for column in range(2)
            ]
            windows.append(lax.ppermute(own_row, "ctx", sends))
        return own_row, windows

    ringed = count <= RING_LIMIT
    if ringed:
        plane_index = plane.reshape(1).astype(jnp.int32)
        pairs = ring_pairs(count // 2)
        half = count // 4
        owners = shard_owners(me, count)
        index += [*owners, *shard_owners(me ^ 1, count)]
        index = jnp.stack(index).astype(jnp.int32)

        def ring(value):
            return lax.ppermute(value, "ctx", pairs)

        def add_projections(total, steps, begin, end, last=False):
            base = 0 if begin == 0 else 2 * begin - 1
            return project(index, base, (hidden_in, other), steps[begin:end], total, last)

        own_near, own_far, own_common = lay_out(plane_index, w_query, w_key, w_value)
        done = {"w_out": w_out}
        common_steps = [(1, (own_common,))]
        query_steps = [(1, (own_near, own_far))]

        def run(name, *ties):
            nonlocal index, cosine, sine, query_cosine, query_sine, key_seg

            def tied(value):
                return after(value, *(done[tie] for tie in ties)) if ties else value

            kind, step = name[:-1], int(name[-1])
            micros = MICROS.get(kind, 2)
            if name == "T0":
                first, index, cosine, sine, query_cosine, query_sine, key_seg = (
                    lax.optimization_barrier(
                        (done["C0"], index, cosine, sine, query_cosine, query_sine, key_seg)
                    )
                )
                done["C0"] = value = first
            elif name == "C0":
                value = both_of(own_common, core_swap(tied(own_common), count))
            elif name == "N0":
                value = both_of(own_near, core_swap(tied(own_near), count))
            elif name == "S0":
                value = core_swap(tied(done["H0"]), count)
            elif name == "H0":
                value = bring(tied(hidden_in), micros)
            elif name == "B0":
                done["W0"] = (core_swap(tied(w_out), count),)
                value = done["W0"][0]
                if HALVED:
                    value = rows_near_of(plane_index, value)
            elif name == "A0":
                value = w_out
            elif kind in ("C", "N"):
                value = done[f"{kind}{step - 1}"]
                value = ring(tied(first_of(value) if step == half else value))
                if kind == "C":
                    common_steps.append((value.shape[0], (value,)))
            elif kind == "F":
                near = done[f"N{step}"]
                value = plane_swap(tied(near))
                query_steps.append((near.shape[0], (near, value)))
            elif kind in ("A", "B"):
                value = ring(tied(done[f"{kind}{step - 1}"]))
            elif kind == "X":
                value = plane_swap(tied(done[f"B{step}"]))
            elif kind in ("K", "Q"):
                begin, end, last = PROJECTIONS[name]
                steps = list(common_steps if kind == "K" else query_steps)
                if ties:
                    used, parts = steps[begin]
                    steps[begin] = (used, (tied(parts[0]), *parts[1:]))
                value = project(
                    index,
                    0 if begin == 0 else 2 * begin - 1,
                    (done["H0"], done["S0"]),
                    steps[begin:end],
                    done.get(f"{kind}{step - 1}"),
                    last,
                    micros,
                )
                if last:
                    kept, sent = value
                    came = core_swap(sent, count)
                    if kind == "K":
                        value = rotate_sums(1, kept, came, cosine, sine)
                    else:
                        value = rotate_sums(
                            q_rows // head_dim, kept, came, query_cosine, query_sine
                        )
            elif name == "R0":
                sends = [(device, device ^ 2) for device in range(count)]
                joined = done["K3"]
                value = join_row(index, joined, lax.ppermute(tied(joined), "ctx", sends))
            elif kind == "R":
                sends = [
                    (row_device(row, column, count), row_device(row + step, column, count))
                    for row in range(count // 2 - step)
                    for column in range(2)
                ]
                value = lax.ppermute(tied(done["R0"]), "ctx", sends)
            elif name == "M0":
                windows = [done["R2"], done["R1"], done["R0"]]
                value = attend(index, tied(done["Q4"]), windows, key_seg, head_dim, micros)
            elif name == "M1":
                value = core_swap(tied(done["M0"]), count)
            elif kind == "W":
                value = [core_swap(tied(done[f"A{step}"]), count)]
                if step < half:
                    value.append(core_swap(done[f"B{step}"], count))
                    value.append(core_swap(done[f"X{step}"], count))
            elif kind == "O":
                shards = []
                for turn in COLUMNS[step]:
                    for base, held in (
                        (3, [done[key] for key in step_shards(turn, half)]),
                        (3 + 2 * half, done[f"W{turn}"]),
                    ):
                        place = base + (2 * turn - 1 if turn else 0)
                        shards.append((place, held[:1]))
                        if len(held) > 1:
                            shards.append((place + 1, held[1:]))
                value = columns_of(
                    index,
                    done["M0"],
                    tied(done["M1"]),
                    shards,
                    done.get("O0"),
                    width,
                    micros,
                )
            done[name] = value

        cosine, sine, query_cosine, query_sine, key_seg = tables
        for entry in PLAN:
            run(*entry.split())
        return done["O1"]
    else:
        index = jnp.stack(index).astype(jnp.int32)
        cosine, sine, query_cosine, query_sine, key_seg = tables
        gathered = lax.all_gather(
            jnp.concatenate([w_key, w_value, w_query], axis=1), "ctx", axis=0, tiled=True
        )
        ordered = jnp.where(core == 0, hidden_in, jnp.roll(hidden_in, block, axis=0))
        pair_tokens = jnp.concatenate([ordered[:block], core_swap(ordered[block:], count)], axis=0)
        sums = jnp.dot(pair_tokens, gathered, preferred_element_type=jnp.float32)
        kv_sums, query_sums = sums[:, : 2 * head_dim], sums[:, 2 * head_dim :]
        joined = rotate_sums(1, kv_sums, jnp.zeros_like(kv_sums), cosine, sine)
        queries = rotate_sums(
            q_rows // head_dim, query_sums, jnp.zeros_like(query_sums), query_cosine, query_sine
        )
        own_row, windows = row_windows(joined)

    mixed = attend(index, queries, [*windows[::-1], own_row], key_seg, head_dim, 4)
    returned = core_swap(mixed, count)
    kinds = (mixed[:block], returned[block:])
    own_rows = jnp.where(
        core == 0, jnp.concatenate(kinds, axis=0), jnp.concatenate(kinds[::-1], axis=0)
    )
    gathered = lax.all_gather(w_out, "ctx", axis=1, tiled=True)
    return jnp.dot(own_rows, gathered, preferred_element_type=jnp.float32).astype(jnp.bfloat16)


def solution(mesh):
    in_specs = (
        P(("dp", "ctx"), None),
        P("dp"),
        P("ctx", None),
        P("ctx", None),
        P("ctx", None),
        P(None, "ctx"),
    )
    out_specs = P(("dp", "ctx"), None)
    return jax.shard_map(
        on_device, mesh=mesh, in_specs=in_specs, out_specs=out_specs, check_vma=False
    )
```

```python
import functools
import math

import jax
import jax.numpy as jnp
from jax import lax
from jax.experimental import pallas as pl
from jax.experimental.pallas import tpu as pltpu
from jax.sharding import PartitionSpec as P

REACH = 8
ROPE_BASE = 500000.0
RING_LIMIT = 16
VMEM_LIMIT = 16 * 1024 * 1024
HALVED = True
PLAN = (
    "A0",
    "N0",
    "N1",
    "C0 N0",
    "T0",
    "B0 N1",
    "H0 C0",
    "S0 N1",
    "N2",
    "C1 N1",
    "F1",
    "A1",
    "N3 S0",
    "C2 N2 F1 N1",
    "F2",
    "B1 N3",
    "X1",
    "N4",
    "Q1",
    "C3 N3 F2 Q1",
    "F3",
    "A2 N4",
    "K1 F2",
    "F4",
    "Q2 B1",
    "C4 N4 Q2 F3",
    "K2 A2 Q2",
    "B2 N4",
    "X2 F4",
    "A3 C4 K2",
    "B3",
    "K3 X1",
    "Q3 K3",
    "Q4 A3",
    "R0 X2 Q3",
    "R1",
    "R2",
    "X3",
    "A4 R0",
    "M0 X3 R2",
    "M1",
    "W1 M0",
    "W2",
    "W3",
    "W4",
    "O0",
)
MICROS = {}
PROJECTIONS = {
    "K1": (0, 2, False),
    "K2": (2, 4, False),
    "K3": (4, 5, True),
    "Q1": (0, 2, False),
    "Q2": (2, 3, False),
    "Q3": (3, 4, False),
    "Q4": (4, 5, True),
}
COLUMNS = ((0, 1, 2, 3, 4),)


def step_shards(turn, half):
    if turn == 0 or turn == half:
        return (f"A{turn}",)
    return (f"A{turn}", f"B{turn}", f"X{turn}")


def chip_at(place, chips):
    place = place % chips
    return jnp.where(place < chips // 2, 2 * place, 2 * (chips - 1 - place) + 1)


def static_chip_at(place, chips):
    place %= chips
    return 2 * place if place < chips // 2 else 2 * (chips - 1 - place) + 1


def ring_pairs(chips):
    pairs = []
    for place in range(chips):
        here = static_chip_at(place, chips)
        pairs.append((2 * here, 2 * static_chip_at(place + 1, chips)))
        pairs.append((2 * here + 1, 2 * static_chip_at(place - 1, chips) + 1))
    return pairs


def core_swap(value, count):
    return lax.ppermute(value, "ctx", [(i, i ^ 1) for i in range(count)])


def plane_swap(value):
    return lax.ppermute(value, "dp", [(0, 1), (1, 0)])


def row_device(row, column, count):
    pair = 2 * row + (column if row < count // 4 else 1 - column)
    return 2 * pair if pair < count // 2 else 2 * (count - 1 - pair) + 1


def after(value, *others):
    return lax.optimization_barrier((value, *others))[0]


def shard_owners(me, count):
    chips = count // 2
    half = chips // 2
    core, chip = me % 2, me // 2
    place = jnp.where(chip % 2 == 0, chip // 2, chips - 1 - chip // 2)
    way = jnp.where(core == 0, -1, 1)
    owners = [me]
    for step in range(1, half + 1):
        source = chip_at(place + way * step + chips, chips)
        owners.append(2 * source + core)
        if step < half:
            owners.append(2 * source + 1 - core)
    return owners


def params(**settings):
    return pltpu.CompilerParams(vmem_limit_bytes=VMEM_LIMIT, **settings)


def in_vmem(*arrays):
    return [pltpu.with_memory_space_constraint(array, pltpu.VMEM) for array in arrays]


def in_hbm(*arrays):
    return [pltpu.with_memory_space_constraint(array, pltpu.HBM) for array in arrays]


def estimate(micros):
    return pl.CostEstimate(flops=int(micros * 1.1535e9), bytes_accessed=0, transcendentals=0)


IN_VMEM = pl.BlockSpec(memory_space=pltpu.VMEM)
IN_HBM = pl.BlockSpec(memory_space=pl.ANY)
IN_SMEM = pl.BlockSpec(memory_space=pltpu.SMEM)


def rotate_kernel(head_dim, heads, kept_ref, came_ref, cos_ref, sin_ref, out_ref):
    cosine, sine = cos_ref[...], sin_ref[...]
    for column in range(0, kept_ref.shape[1], head_dim):
        span = pl.ds(column, head_dim)
        part = kept_ref[:, span] + came_ref[:, span]
        if column < heads * head_dim:
            part = part * cosine + pltpu.roll(part, head_dim // 2, 1) * sine
        out_ref[:, span] = part.astype(jnp.bfloat16)


def rotary_tables(positions, head_dim):
    frequency = ROPE_BASE ** (
        -(jnp.arange(head_dim // 2, dtype=jnp.float32) * 2.0) / head_dim
    )
    angles = positions.astype(jnp.float32)[:, None] * frequency[None, :]
    cosine, sine = jnp.cos(angles), jnp.sin(angles)
    return jnp.concatenate([cosine, cosine], axis=1), jnp.concatenate([-sine, sine], axis=1)


def rotate_sums(heads, kept, came, cosine, sine):
    return pl.pallas_call(
        functools.partial(rotate_kernel, cosine.shape[1], heads),
        out_shape=pltpu.VMEM(kept.shape, jnp.bfloat16),
        in_specs=[IN_VMEM] * 4,
        out_specs=IN_VMEM,
        compiler_params=params(),
        name="rotate_sums",
    )(*in_vmem(kept, came, cosine, sine))


def join_row_kernel(index_ref, own_ref, beside_ref, out_ref):
    odd = index_ref[2]
    out_ref[odd] = own_ref[...]
    out_ref[1 - odd] = beside_ref[...]


def join_row(index, own, beside):
    return pl.pallas_call(
        join_row_kernel,
        in_specs=[IN_SMEM, IN_VMEM, IN_VMEM],
        out_specs=IN_VMEM,
        out_shape=pltpu.VMEM((2, *own.shape), own.dtype),
        compiler_params=params(),
        name="join_row",
    )(index, *in_vmem(own, beside))


def attend_kernel(head_dim, reach, index_ref, query_ref, key_seg_ref, *refs):
    row_refs, (mixed_ref, window) = refs[:-2], refs[-2:]
    rows = query_ref.shape[0]
    for place, row_ref in enumerate(row_refs):
        window[2 * place : 2 * place + 2] = row_ref[...]
    odd = index_ref[2]
    own_seg = key_seg_ref[:, pl.ds(reach * rows, rows)]
    query_seg = jnp.transpose(jnp.broadcast_to(own_seg, (rows, rows)))
    base = lax.broadcasted_iota(jnp.int32, (rows, rows), 0)
    offset = lax.broadcasted_iota(jnp.int32, (rows, rows), 1)
    allowed = []
    for piece in range(reach + 1):
        same = query_seg == key_seg_ref[:, pl.ds(piece * rows, rows)]
        if piece == reach:
            same = same & (offset <= base)
        allowed.append(same)
    scale = math.log2(math.e) / math.sqrt(head_dim)
    for column in range(0, query_ref.shape[1], head_dim):
        span = pl.ds(column, head_dim)
        query = query_ref[:, span]
        scores = []
        for piece in range(reach + 1):
            score = lax.dot_general(
                query,
                window[odd + piece, :, :head_dim],
                (((1,), (1,)), ((), ())),
                preferred_element_type=jnp.float32,
            )
            scores.append(jnp.where(allowed[piece], score, -1e30))
        peak = scores[0]
        for score in scores[1:]:
            peak = jnp.maximum(peak, score)
        peak = jnp.max(peak, axis=1, keepdims=True)
        terms = [jnp.exp2((score - peak) * scale) for score in scores]
        total = terms[0]
        for term in terms[1:]:
            total = total + term
        mixed = jnp.zeros((rows, head_dim), jnp.float32)
        for piece in range(reach + 1):
            mixed += jnp.dot(
                terms[piece].astype(jnp.bfloat16),
                window[odd + piece, :, head_dim:],
                preferred_element_type=jnp.float32,
            )
        mixed = mixed / jnp.sum(total, axis=1, keepdims=True)
        mixed_ref[:, span] = mixed.astype(jnp.bfloat16)


def attend(index, queries, row_windows, key_seg, head_dim, micros):
    reach = 2 * len(row_windows) - 2
    rows = queries.shape[0]
    return pl.pallas_call(
        functools.partial(attend_kernel, head_dim, reach),
        out_shape=pltpu.VMEM(queries.shape, jnp.bfloat16),
        in_specs=[IN_SMEM] + [IN_VMEM] * (2 + len(row_windows)),
        out_specs=IN_VMEM,
        scratch_shapes=[pltpu.VMEM((reach + 2, rows, 2 * head_dim), jnp.bfloat16)],
        compiler_params=params(),
        cost_estimate=estimate(micros),
        name="attend",
    )(index, *in_vmem(queries, key_seg, *row_windows))


def lay_out_kernel(plane_ref, query_ref, key_ref, value_ref, near_out, far_out, common_out, sems):
    q_half, kv_half = near_out.shape[2], common_out.shape[2] // 2
    near = pl.ds(pl.multiple_of(plane_ref[0] * q_half, q_half), q_half)
    far = pl.ds(pl.multiple_of((1 - plane_ref[0]) * q_half, q_half), q_half)
    moves = (
        (key_ref, common_out.at[0, :, :kv_half]),
        (value_ref, common_out.at[0, :, kv_half:]),
        (query_ref.at[:, near], near_out.at[0]),
        (query_ref.at[:, far], far_out.at[0]),
    )
    copies = [
        pltpu.make_async_copy(source, target, sems.at[place])
        for place, (source, target) in enumerate(moves)
    ]
    for copy in copies:
        copy.start()
    for copy in copies:
        copy.wait()


def lay_out(plane, query, key, value):
    depth, q_half = query.shape[0], query.shape[1] // 2
    shapes = ((1, depth, q_half), (1, depth, q_half), (1, depth, 2 * key.shape[1]))
    return pl.pallas_call(
        lay_out_kernel,
        in_specs=[IN_SMEM] + [IN_HBM] * 3,
        out_specs=[IN_VMEM] * 3,
        scratch_shapes=[pltpu.SemaphoreType.DMA((4,))],
        out_shape=[pltpu.VMEM(shape, jnp.bfloat16) for shape in shapes],
        compiler_params=params(),
        name="lay_out",
    )(plane, *in_hbm(query, key, value))


def rows_near_kernel(plane_ref, weight_ref, out_ref):
    half = out_ref.shape[0]
    near = pl.ds(pl.multiple_of(plane_ref[0] * half, half), half)
    out_ref[...] = weight_ref[near, :]


def rows_near_of(plane, weight):
    rows, columns = weight.shape
    return pl.pallas_call(
        rows_near_kernel,
        in_specs=[IN_SMEM, IN_VMEM],
        out_specs=IN_VMEM,
        out_shape=pltpu.VMEM((rows // 2, columns), weight.dtype),
        compiler_params=params(),
        name="rows_near",
    )(plane, *in_vmem(weight))


def both_kernel(first_ref, second_ref, out_ref):
    out_ref[0] = first_ref[0]
    out_ref[1] = second_ref[0]


def both_of(first, second):
    return pl.pallas_call(
        both_kernel,
        in_specs=[IN_VMEM] * 2,
        out_specs=IN_VMEM,
        out_shape=pltpu.VMEM((2, *first.shape[1:]), first.dtype),
        compiler_params=params(),
        name="both_of",
    )(*in_vmem(first, second))


def first_kernel(pair_ref, out_ref):
    out_ref[...] = pair_ref[:1]


def first_of(pair):
    return pl.pallas_call(
        first_kernel,
        in_specs=[IN_VMEM],
        out_specs=IN_VMEM,
        out_shape=pltpu.VMEM((1, *pair.shape[1:]), pair.dtype),
        compiler_params=params(),
        name="first_of",
    )(*in_vmem(pair))


def bring_kernel(source_ref, out_ref, sem):
    copy = pltpu.make_async_copy(source_ref, out_ref, sem)
    copy.start()
    copy.wait()


def bring(tokens, micros):
    return pl.pallas_call(
        bring_kernel,
        in_specs=[IN_HBM],
        out_specs=IN_VMEM,
        scratch_shapes=[pltpu.SemaphoreType.DMA],
        out_shape=pltpu.VMEM(tokens.shape, tokens.dtype),
        compiler_params=params(),
        cost_estimate=estimate(micros),
        name="bring",
    )(*in_hbm(tokens))


def project_kernel(slots, base, groups, first, last, index_ref, own_ref, other_ref, *refs):
    held_weights = groups * (1 + slots[-1][0])
    weights, refs = refs[:held_weights], refs[held_weights:]
    total_ref, refs = (None, refs) if first else (refs[0], refs[1:])
    rows = own_ref.shape[0]
    depth, width = weights[0].shape[-2:]
    block = rows // 2
    spans = [
        pl.ds(pl.multiple_of(index_ref[3 + base + place] * depth, depth), depth)
        for place in range(len(slots))
    ]
    out_ref = refs[2] if last else refs[0]
    for side, source_ref in enumerate((own_ref, other_ref)):
        for group in range(groups):
            columns = pl.ds(group * width, width)
            total = None if first else total_ref[side, :, columns]
            for place, (step, slot) in enumerate(slots):
                product = jnp.dot(
                    source_ref[:, spans[place]],
                    weights[groups * step + group][slot],
                    preferred_element_type=jnp.float32,
                )
                total = product if total is None else total + product
            out_ref[side, :, columns] = total
    if last:
        kept_ref, sent_ref, held = refs
        mine = pl.ds(pl.multiple_of(index_ref[0] * block, block), block)
        others = pl.ds(pl.multiple_of((1 - index_ref[0]) * block, block), block)
        kept_ref[:block] = held[0, mine, :]
        kept_ref[block:] = held[1, mine, :]
        sent_ref[:block] = held[1, others, :]
        sent_ref[block:] = held[0, others, :]


def project(index, base, tokens, steps, total, last, micros):
    groups = len(steps[0][1])
    slots = [(i, slot) for i, (used, _) in enumerate(steps) for slot in range(used)]
    rows = tokens[0].shape[0]
    columns = sum(part.shape[2] for part in steps[0][1])
    operands = in_vmem(*tokens, *(part for _, parts in steps for part in parts))
    if total is not None:
        operands += in_vmem(total)
    shapes = ((rows, columns), (rows, columns)) if last else ((2, rows, columns),)
    out = pl.pallas_call(
        functools.partial(project_kernel, slots, base, groups, total is None, last),
        in_specs=[IN_SMEM] + [IN_VMEM] * len(operands),
        out_specs=[IN_VMEM] * len(shapes),
        scratch_shapes=[pltpu.VMEM((2, rows, columns), jnp.float32)] if last else [],
        out_shape=[pltpu.VMEM(shape, jnp.float32) for shape in shapes],
        compiler_params=params(),
        cost_estimate=estimate(micros),
        name="project",
    )(index, *operands)
    return out if last else out[0]


def columns_kernel(entries, index_ref, mixed_ref, returned_ref, *refs):
    weights = list(refs[: sum(parts for _, parts in entries)])
    out_ref, held, sems = refs[-3:]
    block = mixed_ref.shape[0] // 2
    half = mixed_ref.shape[1] // 2
    width = weights[0].shape[-1]
    mine = pl.ds(pl.multiple_of(index_ref[0] * block, block), block)
    others = pl.ds(pl.multiple_of((1 - index_ref[0]) * block, block), block)
    near = pl.ds(pl.multiple_of(index_ref[1] * half, half), half)
    far = pl.ds(pl.multiple_of((1 - index_ref[1]) * half, half), half)
    rows_in = jnp.concatenate([mixed_ref[:block], returned_ref[block:]], axis=0)
    near_in, far_in = rows_in[:, :half], rows_in[:, half:]
    copies = []
    for place, (owner, parts) in enumerate(entries):
        if parts == 1:
            whole = weights.pop(0)
            low, high = whole[near, :], whole[far, :]
        else:
            low, high = weights.pop(0)[...], weights.pop(0)[...]
        value = jnp.dot(near_in, low, preferred_element_type=jnp.float32)
        value += jnp.dot(far_in, high, preferred_element_type=jnp.float32)
        value = value.astype(jnp.bfloat16)
        columns = pl.ds(place * width, width)
        held[mine, columns] = value[:block]
        held[others, columns] = value[block:]
        column = pl.multiple_of(index_ref[owner] * width, width)
        copy = pltpu.make_async_copy(
            held.at[:, columns], out_ref.at[:, pl.ds(column, width)], sems.at[place]
        )
        copy.start()
        copies.append(copy)
    for copy in copies:
        copy.wait()


def columns_of(index, mixed, returned, shards, result, width, micros):
    rows = mixed.shape[0]
    out_cols = shards[0][1][0].shape[-1]
    entries = [(owner, len(parts)) for owner, parts in shards]
    operands = in_vmem(mixed, returned, *(part for _, parts in shards for part in parts))
    specs = [IN_SMEM] + [IN_VMEM] * len(operands)
    if result is not None:
        operands += in_hbm(result)
        specs.append(IN_HBM)
    return pl.pallas_call(
        functools.partial(columns_kernel, entries),
        in_specs=specs,
        out_specs=IN_HBM,
        scratch_shapes=[
            pltpu.VMEM((rows, len(shards) * out_cols), jnp.bfloat16),
            pltpu.SemaphoreType.DMA((len(shards),)),
        ],
        out_shape=pltpu.HBM((rows, width), jnp.bfloat16),
        input_output_aliases={} if result is None else {len(operands): 0},
        compiler_params=params(),
        cost_estimate=estimate(micros),
        name="columns_of",
    )(index, *operands)


def on_device(hidden_in, segment_ids, w_query, w_key, w_value, w_out):
    count = lax.axis_size("ctx")
    me = lax.axis_index("ctx")
    plane = lax.axis_index("dp")
    core, chip = me % 2, me // 2
    rows, width = hidden_in.shape
    block = rows // 2
    head_dim = w_key.shape[1]
    q_rows, out_cols = w_out.shape

    reach = REACH * block // rows
    pair = jnp.where(core == 0, chip, count - 1 - chip)
    pair_pos = pair * rows + jnp.arange(rows, dtype=jnp.int32)
    cosine, sine = rotary_tables(pair_pos, head_dim)
    seg_blocks = segment_ids.reshape(2 * count, block)
    seq_block = pair * 2 - 2 * reach + jnp.arange(2 * reach + 2, dtype=jnp.int32)
    clipped = jnp.maximum(seq_block, 0)
    stored = jnp.where(clipped < count, 2 * clipped, 2 * (2 * count - 1 - clipped) + 1)
    seg_rows = seg_blocks[stored]
    key_seg = jnp.where(seq_block[:, None] >= 0, seg_rows, -1).reshape(1, -1)
    tables = (cosine, sine, cosine, sine, key_seg)
    index = [core, plane, pair % 2]

    def row_windows(joined):
        sends = [(device, device ^ 2) for device in range(count)]
        own_row = join_row(index, joined, lax.ppermute(joined, "ctx", sends))
        windows = []
        for back in range(1, reach // 2 + 1):
            sends = [
                (row_device(row, column, count), row_device(row + back, column, count))
                for row in range(count // 2 - back)
                for column in range(2)
            ]
            windows.append(lax.ppermute(own_row, "ctx", sends))
        return own_row, windows

    ringed = count <= RING_LIMIT
    if ringed:
        plane_index = plane.reshape(1).astype(jnp.int32)
        pairs = ring_pairs(count // 2)
        half = count // 4
        owners = shard_owners(me, count)
        index += [*owners, *shard_owners(me ^ 1, count)]
        index = jnp.stack(index).astype(jnp.int32)

        def ring(value):
            return lax.ppermute(value, "ctx", pairs)

        def add_projections(total, steps, begin, end, last=False):
            base = 0 if begin == 0 else 2 * begin - 1
            return project(index, base, (hidden_in, other), steps[begin:end], total, last)

        own_near, own_far, own_common = lay_out(plane_index, w_query, w_key, w_value)
        done = {"w_out": w_out}
        common_steps = [(1, (own_common,))]
        query_steps = [(1, (own_near, own_far))]

        def run(name, *ties):
            nonlocal index, cosine, sine, query_cosine, query_sine, key_seg

            def tied(value):
                return after(value, *(done[tie] for tie in ties)) if ties else value

            kind, step = name[:-1], int(name[-1])
            micros = MICROS.get(kind, 2)
            if name == "T0":
                first, index, cosine, sine, query_cosine, query_sine, key_seg = (
                    lax.optimization_barrier(
                        (done["C0"], index, cosine, sine, query_cosine, query_sine, key_seg)
                    )
                )
                done["C0"] = value = first
            elif name == "C0":
                value = both_of(own_common, core_swap(tied(own_common), count))
            elif name == "N0":
                value = both_of(own_near, core_swap(tied(own_near), count))
            elif name == "S0":
                value = core_swap(tied(done["H0"]), count)
            elif name == "H0":
                value = bring(tied(hidden_in), micros)
            elif name == "B0":
                done["W0"] = (core_swap(tied(w_out), count),)
                value = done["W0"][0]
                if HALVED:
                    value = rows_near_of(plane_index, value)
            elif name == "A0":
                value = w_out
            elif kind in ("C", "N"):
                value = done[f"{kind}{step - 1}"]
                value = ring(tied(first_of(value) if step == half else value))
                if kind == "C":
                    common_steps.append((value.shape[0], (value,)))
            elif kind == "F":
                near = done[f"N{step}"]
                value = plane_swap(tied(near))
                query_steps.append((near.shape[0], (near, value)))
            elif kind in ("A", "B"):
                value = ring(tied(done[f"{kind}{step - 1}"]))
            elif kind == "X":
                value = plane_swap(tied(done[f"B{step}"]))
            elif kind in ("K", "Q"):
                begin, end, last = PROJECTIONS[name]
                steps = list(common_steps if kind == "K" else query_steps)
                if ties:
                    used, parts = steps[begin]
                    steps[begin] = (used, (tied(parts[0]), *parts[1:]))
                value = project(
                    index,
                    0 if begin == 0 else 2 * begin - 1,
                    (done["H0"], done["S0"]),
                    steps[begin:end],
                    done.get(f"{kind}{step - 1}"),
                    last,
                    micros,
                )
                if last:
                    kept, sent = value
                    came = core_swap(sent, count)
                    if kind == "K":
                        value = rotate_sums(1, kept, came, cosine, sine)
                    else:
                        value = rotate_sums(
                            q_rows // head_dim, kept, came, query_cosine, query_sine
                        )
            elif name == "R0":
                sends = [(device, device ^ 2) for device in range(count)]
                joined = done["K3"]
                value = join_row(index, joined, lax.ppermute(tied(joined), "ctx", sends))
            elif kind == "R":
                sends = [
                    (row_device(row, column, count), row_device(row + step, column, count))
                    for row in range(count // 2 - step)
                    for column in range(2)
                ]
                value = lax.ppermute(tied(done["R0"]), "ctx", sends)
            elif name == "M0":
                windows = [done["R2"], done["R1"], done["R0"]]
                value = attend(index, tied(done["Q4"]), windows, key_seg, head_dim, micros)
            elif name == "M1":
                value = core_swap(tied(done["M0"]), count)
            elif kind == "W":
                value = [core_swap(tied(done[f"A{step}"]), count)]
                if step < half:
                    value.append(core_swap(done[f"B{step}"], count))
                    value.append(core_swap(done[f"X{step}"], count))
            elif kind == "O":
                shards = []
                for turn in COLUMNS[step]:
                    for base, held in (
                        (3, [done[key] for key in step_shards(turn, half)]),
                        (3 + 2 * half, done[f"W{turn}"]),
                    ):
                        place = base + (2 * turn - 1 if turn else 0)
                        shards.append((place, held[:1]))
                        if len(held) > 1:
                            shards.append((place + 1, held[1:]))
                value = columns_of(
                    index,
                    done["M0"],
                    tied(done["M1"]),
                    shards,
                    done.get("O0"),
                    width,
                    micros,
                )
            done[name] = value

        cosine, sine, query_cosine, query_sine, key_seg = tables
        for entry in PLAN:
            run(*entry.split())
        return done["O0"]
    else:
        index = jnp.stack(index).astype(jnp.int32)
        cosine, sine, query_cosine, query_sine, key_seg = tables
        gathered = lax.all_gather(
            jnp.concatenate([w_key, w_value, w_query], axis=1), "ctx", axis=0, tiled=True
        )
        ordered = jnp.where(core == 0, hidden_in, jnp.roll(hidden_in, block, axis=0))
        pair_tokens = jnp.concatenate([ordered[:block], core_swap(ordered[block:], count)], axis=0)
        sums = jnp.dot(pair_tokens, gathered, preferred_element_type=jnp.float32)
        kv_sums, query_sums = sums[:, : 2 * head_dim], sums[:, 2 * head_dim :]
        joined = rotate_sums(1, kv_sums, jnp.zeros_like(kv_sums), cosine, sine)
        queries = rotate_sums(
            q_rows // head_dim, query_sums, jnp.zeros_like(query_sums), query_cosine, query_sine
        )
        own_row, windows = row_windows(joined)

    mixed = attend(index, queries, [*windows[::-1], own_row], key_seg, head_dim, 4)
    returned = core_swap(mixed, count)
    kinds = (mixed[:block], returned[block:])
    own_rows = jnp.where(
        core == 0, jnp.concatenate(kinds, axis=0), jnp.concatenate(kinds[::-1], axis=0)
    )
    gathered = lax.all_gather(w_out, "ctx", axis=1, tiled=True)
    return jnp.dot(own_rows, gathered, preferred_element_type=jnp.float32).astype(jnp.bfloat16)


def solution(mesh):
    in_specs = (
        P(("dp", "ctx"), None),
        P("dp"),
        P("ctx", None),
        P("ctx", None),
        P("ctx", None),
        P(None, "ctx"),
    )
    out_specs = P(("dp", "ctx"), None)
    return jax.shard_map(
        on_device, mesh=mesh, in_specs=in_specs, out_specs=out_specs, check_vma=False
    )
```
